512 devices in a mesh: grp: 4 (over z_lo), gx: 16 (over y, x), gy: 8 (over z_hi, core).
Axes of the slice: x: 4, y: 4, z: 16 (z_hi: 4, z_lo: 4; z = z_hi * 4 + z_lo), core: 2. Of those that a mesh axis runs over, the one named last changes fastest.
Arguments:
- fields: float32 [4, 6, 2, 256, 1024], P('grp', None, None, 'gx', 'gy'), may hold values from -6 to 6
- stored: bfloat16 [4, 2, 6, 2, 256, 1024], P('grp', None, None, None, 'gx', 'gy'), may hold values from -6 to 6
- material: int32 [2, 256, 1024], P(None, 'gx', 'gy'), may hold values from 0 to 3
- design: float32 [256, 1024], P('gx', 'gy'), may hold values from 0 to 2
- mat_eps: float32 [4], replicated, may hold values from 1 to 4
- mat_chi: float32 [4], replicated, may hold values from 0.05 to 0.4
- source_wave: float32 [2, 4], replicated, may hold values from -4 to 4
- source_cells: int32 [2048], replicated, may hold values from 0 to 524287
- monitor_cells: int32 [2048], replicated, may hold values from 0 to 524287
- owners: int32 [2048], replicated, may hold values from 0 to 2047, each once
Outputs:
- fields_next: float32 [4, 6, 2, 256, 1024], P('grp', None, None, 'gx', 'gy')
- stored_next: bfloat16 [4, 2, 6, 2, 256, 1024], P('grp', None, None, None, 'gx', 'gy')
- design_grad: float32 [2048, 128], P(('grp', 'gx', 'gy'))
The draws below stay inside these ranges and needn't reach their ends.
Inputs may be any that keep to these rules, and one draw needn't show every extreme that they name: owners names every row of design_grad exactly once.
All inputs are finite; a program needn't handle non-finite values.
Results may differ from the reference program's by a relative error of at most 0.00105.
Values may be sent and summed in bfloat16 or wider, within the bound.
A program may use at most 64 MiB of HBM per device.

```python
import math
import jax
import jax.numpy as jnp
from jax import lax

NZ = 2
CY = 128
STEPS = 4
NMAT = 4
NSRC = 2048
NMON = 2048
HALF = 2
NX = 256
NY = 1024
N_GY = 8


def plant(entries, own_key, low, largest):
    longest = entries.shape.index(max(entries.shape))
    spots = []
    for shift in (0, 1):
        where = [jax.random.randint(jax.random.fold_in(own_key, axis), (), 0, length) for axis, length in enumerate(entries.shape)]
        where[longest] = (where[longest] + shift) % entries.shape[longest]
        spots.append(tuple(where))
    return entries.at[spots[0]].set(low).at[spots[1]].set(largest)


def block_levels(key, extent, pieces, least, largest):
    gain = 1.0
    for dim, parts in pieces:
        steps = jax.random.uniform(jax.random.fold_in(jax.random.fold_in(key, 6), dim), (parts,), jnp.float32, least / len(pieces), largest / len(pieces))
        gain = gain * jnp.repeat(jnp.exp(steps), extent[dim] // parts).reshape((-1,) + (1,) * (len(extent) - 1 - dim))
    return gain


def centred(own_key, shape, scale, reach, shards=(), kind=jnp.bfloat16):
    result = scale * jax.random.normal(own_key, shape, jnp.float32)
    if shards:
        result = result * block_levels(own_key, shape, shards, -0.22, 0.18)
    return jnp.clip(result, -reach, reach).astype(kind)


def setup_inputs(seed: int = 0) -> dict:
    seeds = jax.random.split(jax.random.key(seed), 11)
    fields = centred(seeds[0], (4, 6, NZ, NX, NY), 1.0, 6.0, ((0, 4), (3, 16), (4, 8)), jnp.float32)
    stored = centred(seeds[1], (4, HALF, 6, NZ, NX, NY), 1.0, 6.0, ((0, 4), (4, 16), (5, 8)))
    material = plant(jax.random.randint(seeds[2], (NZ, NX, NY), 0, NMAT), jax.random.fold_in(seeds[2], 1), 0, NMAT - 1).astype(jnp.int32)
    design = jnp.clip(2.0 * jax.random.uniform(seeds[3], (NX, NY), jnp.float32) ** block_levels(seeds[3], (NX, NY), ((0, 16), (1, 8)), -0.2, 0.2), 0.0, 2.0)
    mat_eps = jnp.clip(jax.random.uniform(seeds[4], (NMAT,), jnp.float32, 1.0, 4.0), 1.0, 4.0)
    mat_chi = jnp.clip(jnp.exp(jax.random.uniform(seeds[5], (NMAT,), jnp.float32, math.log(0.05), math.log(0.4))), 0.05, 0.4)
    source_wave = centred(seeds[6], (2, STEPS), 1.0, 4.0, (), jnp.float32)
    source_cells = plant(jax.random.randint(seeds[7], (NSRC,), 0, NZ * NX * NY), jax.random.fold_in(seeds[7], 1), 0, (NZ * NX * NY) - 1).astype(jnp.int32)
    monitor_cells = plant(jax.random.randint(seeds[8], (NMON,), 0, NZ * NX * NY), jax.random.fold_in(seeds[8], 1), 0, (NZ * NX * NY) - 1).astype(jnp.int32)
    owners = jax.random.permutation(seeds[9], NX * N_GY).astype(jnp.int32)
    return dict(fields=fields, stored=stored, material=material, design=design, mat_eps=mat_eps, mat_chi=mat_chi, source_wave=source_wave, source_cells=source_cells, monitor_cells=monitor_cells, owners=owners)


time_step = 0.5


def shifted(values, axis, upward):
    length = values.shape[axis]
    border = jnp.zeros_like(lax.slice_in_dim(values, 0, 1, axis=axis))
    if upward:
        interior = lax.slice_in_dim(values, 1, length, axis=axis)
        return jnp.concatenate([interior, border], axis=axis) - values
    interior = lax.slice_in_dim(values, 0, length - 1, axis=axis)
    return values - jnp.concatenate([border, interior], axis=axis)


def curl_of(values, upward):
    x_part = shifted(values[2], 2, upward) - shifted(values[1], 0, upward)
    y_part = shifted(values[0], 0, upward) - shifted(values[2], 1, upward)
    z_part = shifted(values[1], 1, upward) - shifted(values[0], 2, upward)
    return jnp.stack([x_part, y_part, z_part])


def reference(fields, stored, material, design, mat_eps, mat_chi, source_wave, source_cells, monitor_cells, owners):
    permittivity = mat_eps[material] + design[None]
    kerr_chi = mat_chi[material]
    cell_count = NZ * NX * NY
    forward_states = []
    adjoint_states = []
    stored_first = []
    stored_second = []
    grad_cells = jnp.zeros((NZ, NX, NY), jnp.float32)
    for s in range(2):
        electric = fields[s, :3]
        magnetic = fields[s, 3:]
        records = []
        for n in range(STEPS):
            factor = time_step / (permittivity + kerr_chi * jnp.sum(electric * electric, axis=0))
            magnetic = magnetic - time_step * curl_of(electric, True)
            rotated = curl_of(magnetic, False)
            records.append(jnp.concatenate([electric, rotated]).astype(jnp.bfloat16))
            electric = electric + factor * rotated
            flat_field = electric.reshape(3, cell_count).at[0, source_cells].add(source_wave[s, n])
            electric = flat_field.reshape(3, NZ, NX, NY)
        forward_states.append(jnp.concatenate([electric, magnetic]))
        stored_first.append(jnp.stack(records[:HALF]))
        stored_second.append(jnp.stack(records[HALF:]))
        snapshots = jnp.concatenate([stored[s], stored[s + 2]], axis=0)
        adj_electric = fields[s + 2, :3]
        adj_magnetic = fields[s + 2, 3:]
        for n in range(STEPS - 1, -1, -1):
            past_field = snapshots[n, :3].astype(jnp.float32)
            curled = snapshots[n, 3:].astype(jnp.float32)
            factor = time_step / (permittivity + kerr_chi * jnp.sum(past_field * past_field, axis=0))
            contracted = jnp.sum(curled * adj_electric, axis=0)
            adj_magnetic = adj_magnetic + curl_of(factor * adj_electric, True)
            grad_cells = grad_cells - (factor * factor / time_step) * contracted
            kerr_term = (-2.0 / time_step) * kerr_chi * factor * factor * contracted * past_field
            adj_electric = adj_electric + kerr_term - time_step * curl_of(adj_magnetic, False)
            flat_past = past_field.reshape(3, cell_count)
            flat_adj = adj_electric.reshape(3, cell_count).at[:, monitor_cells].add(flat_past[:, monitor_cells])
            adj_electric = flat_adj.reshape(3, NZ, NX, NY)
        adjoint_states.append(jnp.concatenate([adj_electric, adj_magnetic]))
    fields_next = jnp.stack(forward_states + adjoint_states)
    stored_next = jnp.stack(stored_first + stored_second)
    grad_plane = jnp.sum(grad_cells, axis=0)
    grad_tiles = grad_plane.reshape(NX * N_GY, CY)
    design_grad = jnp.zeros((NX * N_GY, CY), jnp.float32).at[owners].set(grad_tiles)
    return fields_next, stored_next, design_grad
```

```python
import functools

import jax
import jax.numpy as jnp
from jax import lax
from jax.experimental import pallas as pl
from jax.experimental.pallas import tpu as pltpu
from jax.sharding import PartitionSpec as P

MESH = pl.DeviceIdType.MESH
F32 = jnp.float32
BF16 = jnp.bfloat16

NZ = 2
TX = 16
TY = 128
RIM = 4
EX = TX + 2 * RIM
EY = 2 * TY
STEPS = 4
HALF = 2
DT = 0.5
SHARE = 4

AROUND = ((-1, 0), (1, 0), (0, -1), (0, 1), (-1, -1), (-1, 1), (1, -1), (1, 1))


def iota(shape, axis):
    return lax.broadcasted_iota(jnp.int32, shape, axis)


def pack_columns(planes):
    column = iota((TX, TY), 1)
    window = ((column + RIM) // 8) % 16
    packed = planes[0]
    for p in range(1, len(planes)):
        packed = jnp.where(window == p, pltpu.roll(planes[p], 8 * p, 1), packed)
    return packed


def pack_rows(one, two):
    low = iota((8, TY), 0) < RIM
    first = jnp.where(low, one[:8], one[8:])
    second = pltpu.roll(jnp.where(low, two[:8], two[8:]), RIM, 0)
    return jnp.where(low, first, second), jnp.where(low, second, first)


def unpack_rows(after, before):
    low = iota((8, TY), 0) < RIM
    return jnp.where(low, after, before), pltpu.roll(jnp.where(low, before, after), RIM, 0)


def merge_columns(right, left, corners):
    side = iota((TX, TY), 1) % 8 < RIM
    beside = jnp.where(side, right, left)
    side = side[:8]
    from_after_right, from_after_left, from_before_right, from_before_left = corners
    low = iota((8, TY), 0) < RIM
    after = jnp.where(side, from_after_right, from_after_left)
    before = jnp.where(side, from_before_right, from_before_left)
    return jnp.concatenate([beside, jnp.where(low, after, before)], axis=0)


def extended(tile, rows, columns, p):
    body = jnp.concatenate([tile, rows], axis=0)
    beside = columns if p == 0 else pltpu.roll(columns, TY - 8 * p, 1)
    return jnp.concatenate([body, beside], axis=1)


def next_x(v):
    return pltpu.roll(v, EX - 1, 0) - v


def next_y(v):
    return pltpu.roll(v, EY - 1, 1) - v


def next_z(v):
    return [v[1] - v[0], -v[1]]


def last_x(v):
    return v - pltpu.roll(v, 1, 0)


def last_y(v):
    return v - pltpu.roll(v, 1, 1)


def last_z(v):
    return [v[0], v[1] - v[0]]


def curl(v, along_x, along_y, along_z):
    z_of_y, z_of_x = along_z(v[1]), along_z(v[0])
    return (
        [along_y(v[2][z]) - z_of_y[z] for z in range(NZ)],
        [z_of_x[z] - along_x(v[2][z]) for z in range(NZ)],
        [along_x(v[1][z]) - along_y(v[0][z]) for z in range(NZ)],
    )


def curl_up(v):
    return curl(v, next_x, next_y, next_z)


def curl_down(v):
    return curl(v, last_x, last_y, last_z)


def kernel(
    n_gx,
    n_gy,
    fields,
    stored,
    material,
    design,
    mat_eps,
    mat_chi,
    source_wave,
    source_cells,
    monitor_cells,
    owners,
    fields_next,
    stored_next,
    design_grad,
    col_out,
    colh_out,
    row_out,
    rowh_out,
    col_in,
    corner_in,
    row_in,
    colh_in,
    rowh_in,
    half_in,
    records,
    state,
    counts_ref,
    chosen,
    tiles,
    shares,
    gathered,
    own_sem,
    ownh_sem,
    half_send,
    in_sem,
    inh_sem,
    half_sem,
    record_send,
    record_sem,
    tile_send,
    tile_sem,
    share_send,
    share_sem,
    local_sem,
):
    grp, gx, gy = lax.axis_index("grp"), lax.axis_index("gx"), lax.axis_index("gy")
    forward = grp < 2
    ahead = jnp.where(forward, 1, 0)
    half_lane = grp + 2 * ahead
    twin = jnp.where(forward, grp + 2, grp - 2)

    def device(lane, dx, dy):
        return {
            "grp": lane,
            "gx": lax.rem(gx + dx + n_gx, n_gx),
            "gy": lax.rem(gy + dy + n_gy, n_gy),
        }

    barrier = pltpu.get_barrier_semaphore()

    def greet(target):
        pl.semaphore_signal(barrier, inc=1, device_id=target, device_id_type=MESH)

    for dx, dy in AROUND:
        greet(device(grp, dx, dy))
        greet(device(twin, dx, dy))
    greet(device(twin, 0, 0))

    @pl.when(forward)
    def _():
        def column(i, carry):
            greet({"grp": 2 + i // n_gy, "gx": gx, "gy": lax.rem(i, n_gy)})
            return carry

        lax.fori_loop(0, 2 * n_gy, column, 0)

    @pl.when(jnp.logical_not(forward))
    def _():
        def line(j, carry):
            greet(device(grp, j, 0))
            return carry

        lax.fori_loop(1, n_gx, line, 0)

        def column(i, carry):
            greet(device(lax.rem(grp + i // n_gy, 4), 0, lax.rem(i, n_gy)))
            return carry

        lax.fori_loop(1, 4 * n_gy, column, 0)

    def lookup(index, entries):
        value = jnp.zeros(index.shape, F32)
        for k in range(4):
            value = jnp.where(index == k, entries[k], value)
        return value

    kinds = [material[z] for z in range(NZ)]
    eps = [lookup(kinds[z], mat_eps) + design[...] for z in range(NZ)]
    chi = [lookup(kinds[z], mat_chi) for z in range(NZ)]
    own = [fields[c, z] for c in range(6) for z in range(NZ)] + eps + chi
    col_out[...] = pack_columns(own)
    for i in range(8):
        row_out[0, i], row_out[1, i] = pack_rows(own[2 * i], own[2 * i + 1])

    pl.semaphore_wait(barrier, jnp.where(forward, 17 + 2 * n_gy, 17 + n_gx - 1 + 4 * n_gy - 1))

    def row_copy(i):
        return pltpu.make_async_remote_copy(
            src_ref=row_out.at[i],
            dst_ref=row_in.at[i],
            send_sem=own_sem.at[i],
            recv_sem=in_sem.at[i],
            device_id=device(grp, *AROUND[i]),
            device_id_type=MESH,
        )

    def col_copy(i):
        return pltpu.make_async_remote_copy(
            src_ref=col_out,
            dst_ref=col_in.at[i - 2],
            send_sem=own_sem.at[i],
            recv_sem=in_sem.at[i],
            device_id=device(grp, *AROUND[i]),
            device_id_type=MESH,
        )

    def corner_copy(i):
        start = 0 if AROUND[i][0] < 0 else 8
        return pltpu.make_async_remote_copy(
            src_ref=col_out.at[pl.ds(start, 8)],
            dst_ref=corner_in.at[i - 4],
            send_sem=own_sem.at[i],
            recv_sem=in_sem.at[i],
            device_id=device(grp, *AROUND[i]),
            device_id_type=MESH,
        )

    def rim_copies():
        return [row_copy(0), row_copy(1), col_copy(2), col_copy(3)] + [corner_copy(i) for i in range(4, 8)]

    for copy in rim_copies():
        copy.start()

    for k in range(HALF):
        planes = [stored[k, c, z].astype(F32) for c in range(6) for z in range(NZ)]
        colh_out[k] = pack_columns(planes).astype(BF16)
        for i in range(3):
            one = pack_rows(planes[4 * i], planes[4 * i + 1])
            two = pack_rows(planes[4 * i + 2], planes[4 * i + 3])
            for side in range(2):
                rowh_out[side, 3 * k + i] = jnp.concatenate([one[side], two[side]], axis=0).astype(BF16)

    def half_copy(which, i):
        if i < 2:
            src, dst = rowh_out.at[i], rowh_in.at[which, i]
        else:
            src, dst = colh_out, colh_in.at[which, i - 2]
        return pltpu.make_async_remote_copy(
            src_ref=src,
            dst_ref=dst,
            send_sem=ownh_sem.at[i],
            recv_sem=inh_sem.at[which, i],
            device_id=device(half_lane, *AROUND[i]),
            device_id_type=MESH,
        )

    for i in range(8):
        half_copy(ahead, i).start()

    def whole_half():
        return pltpu.make_async_remote_copy(
            src_ref=stored,
            dst_ref=half_in,
            send_sem=half_send,
            recv_sem=half_sem,
            device_id=device(half_lane, 0, 0),
            device_id_type=MESH,
        )

    @pl.when(forward)
    def _():
        whole_half().start()

    row = iota((NZ * EX, TY), 0)
    depth = jnp.where(row >= EX, 1, 0)
    row = row - depth * EX
    x = gx * TX + jnp.where(row < TX + RIM, row, row - EX)
    sought_x = jnp.where((x >= 0) & (x < n_gx * TX), depth * (n_gx * TX) + x, -1)
    column = iota((TY, TY), 0)
    sought_y = gy * TY + column
    sought_high = sought_y[:8] + TY
    sought_low = sought_y[TY - 8 :] - TY
    listed = jnp.where(forward, source_cells[...], monitor_cells[...])
    listed_x = listed // (n_gy * TY)
    listed_y = listed % (n_gy * TY)

    def hits(found):
        return jnp.where(found, 1.0, 0.0)

    def wide(m, i, rows):
        return jnp.broadcast_to(m[i : i + 1], (rows, TY))

    entries = listed.shape[0]
    rows_hit = jnp.concatenate(
        [hits(wide(listed_x, i, NZ * EX) == sought_x) for i in range(entries)], axis=1
    ).astype(BF16)
    columns_hit = jnp.concatenate(
        [hits(wide(listed_y, i, TY) == sought_y) for i in range(entries)], axis=1
    ).astype(BF16)
    high_hit = jnp.concatenate([hits(wide(listed_y, i, 8) == sought_high) for i in range(entries)], axis=1)
    low_hit = jnp.concatenate([hits(wide(listed_y, i, 8) == sought_low) for i in range(entries)], axis=1)
    rim_hit = jnp.concatenate(
        [high_hit, jnp.zeros((TY - 16, entries * TY), F32), low_hit], axis=0
    ).astype(BF16)

    def tally(a, b):
        return lax.dot_general(a, b, (((1,), (1,)), ((), ())), preferred_element_type=F32)

    counts_ref[...] = jnp.concatenate([tally(rows_hit, columns_hit), tally(rows_hit, rim_hit)], axis=1)

    @pl.when(jnp.logical_not(forward))
    def _():
        lanes = owners.shape[1]
        pick = iota((TX, lanes), 1) == iota((TX, lanes), 0) * n_gy + gy
        coarse, fine = [], []
        for j in range(n_gx):
            line = jnp.broadcast_to(owners[pl.ds(lax.rem(gx - j + n_gx, n_gx), 1)], (TX, lanes))
            line = jnp.where(pick, line, 0)
            part = line // 64 * 64
            coarse.append(part.astype(F32))
            fine.append((line - part).astype(F32))
        rows = 4 * n_gy * SHARE
        ones = jnp.ones((rows, lanes), BF16)
        owner = tally(ones, jnp.concatenate(coarse, axis=0).astype(BF16))
        owner = owner + tally(ones, jnp.concatenate(fine, axis=0).astype(BF16))
        place = iota((rows, n_gx * TX), 0)
        share = place // SHARE
        lane = (grp + share // n_gy) % 4
        spot = (gy + share % n_gy) % n_gy
        wanted = ((lane * n_gx + gx) * n_gy + spot) * SHARE + place % SHARE
        chosen[...] = jnp.where(owner == wanted.astype(F32), 1.0, 0.0).astype(BF16)

    row = iota((EX, EY), 0)
    column = iota((EX, EY), 1)
    x = gx * TX + jnp.where(row < TX + RIM, row, row - EX)
    y = gy * TY + jnp.where(column < TY + TY // 2, column, column - EY)
    inside = (x >= 0) & (x < n_gx * TX) & (y >= 0) & (y < n_gy * TY)
    unit = jnp.where(inside, 1.0, 0.0)
    step = jnp.where(inside, DT, 0.0)
    counts = [counts_ref[z * EX : (z + 1) * EX] for z in range(NZ)]

    for copy in rim_copies():
        copy.wait_recv()
    columns = merge_columns(col_in[0], col_in[1], [corner_in[i] for i in range(4)])
    whole = []
    for i in range(8):
        for k, rows in enumerate(unpack_rows(row_in[0, i], row_in[1, i])):
            whole.append(extended(own[2 * i + k], rows, columns, 2 * i + k))
    eps = whole[12:14]
    chi = whole[14:16]
    whole = [jnp.where(inside, v, 0.0) for v in whole[:12]]
    first = [whole[2 * c : 2 * c + 2] for c in range(3)]
    second = [whole[2 * c : 2 * c + 2] for c in range(3, 6)]

    def state_copy():
        return pltpu.make_async_copy(state, fields_next, local_sem.at[0])

    def finish(electric, magnetic):
        for c in range(3):
            for z in range(NZ):
                state[c, z] = electric[c][z][:TX, :TY]
                state[3 + c, z] = magnetic[c][z][:TX, :TY]
        state_copy().start()

    def record_copy(n):
        return pltpu.make_async_remote_copy(
            src_ref=records.at[n],
            dst_ref=stored_next.at[n - HALF],
            send_sem=record_send.at[n - HALF],
            recv_sem=record_sem.at[n - HALF],
            device_id=device(half_lane, 0, 0),
            device_id_type=MESH,
        )

    def kept_copy(n):
        return pltpu.make_async_copy(records.at[n], stored_next.at[n], local_sem.at[1 + n])

    def square(v, z):
        return v[0][z] * v[0][z] + v[1][z] * v[1][z] + v[2][z] * v[2][z]

    @pl.when(forward)
    def _():
        electric, magnetic = first, second
        for n in range(STEPS):
            factor = [step / (eps[z] + chi[z] * square(electric, z)) for z in range(NZ)]
            turn = curl_up(electric)
            magnetic = [[magnetic[c][z] - step * turn[c][z] for z in range(NZ)] for c in range(3)]
            turn = curl_down(magnetic)
            for c in range(3):
                for z in range(NZ):
                    records[n, c, z] = electric[c][z][:TX, :TY].astype(BF16)
                    records[n, 3 + c, z] = turn[c][z][:TX, :TY].astype(BF16)
            (kept_copy if n < HALF else record_copy)(n).start()
            wave = source_wave[lax.rem(grp, 2), n]
            electric = [[electric[c][z] + factor[z] * turn[c][z] for z in range(NZ)] for c in range(3)]
            electric[0] = [electric[0][z] + wave * counts[z] for z in range(NZ)]
        finish(electric, magnetic)

    def rims_of_half(which, k):
        rows = []
        for i in range(3):
            after = rowh_in[which, 0, 3 * k + i].astype(F32)
            before = rowh_in[which, 1, 3 * k + i].astype(F32)
            rows.extend(unpack_rows(after[:8], before[:8]))
            rows.extend(unpack_rows(after[8:], before[8:]))
        packed = [colh_in[which, i, k].astype(F32) for i in range(6)]
        corners = [packed[2][:8], packed[3][:8], packed[4][8:], packed[5][8:]]
        return rows, merge_columns(packed[0], packed[1], corners)

    def snapshot(which, k):
        tile = stored if which == 0 else half_in
        rows, columns = rims_of_half(which, k)
        planes = [
            extended(tile[k, c, z].astype(F32), rows[2 * c + z], columns, 2 * c + z)
            for c in range(6)
            for z in range(NZ)
        ]
        past = [planes[2 * c : 2 * c + 2] for c in range(3)]
        curled = [planes[2 * c : 2 * c + 2] for c in range(3, 6)]
        return past, curled

    @pl.when(jnp.logical_not(forward))
    def _():
        electric, magnetic = first, second
        gradient = jnp.zeros((TX, TY), F32)
        for n in range(STEPS - 1, -1, -1):
            which, k = (0, n - HALF) if n >= HALF else (1, n)
            if k == HALF - 1:
                for i in range(8):
                    half_copy(which, i).wait_recv()
                if which == 1:
                    whole_half().wait_recv()
            past, curled = snapshot(which, k)
            factor = [DT / (eps[z] + chi[z] * square(past, z)) for z in range(NZ)]
            inner = [
                curled[0][z] * electric[0][z] + curled[1][z] * electric[1][z] + curled[2][z] * electric[2][z]
                for z in range(NZ)
            ]
            turn = curl_up([[factor[z] * electric[c][z] for z in range(NZ)] for c in range(3)])
            magnetic = [[magnetic[c][z] + unit * turn[c][z] for z in range(NZ)] for c in range(3)]
            turn = curl_down(magnetic)
            slope = [factor[z] * factor[z] * inner[z] for z in range(NZ)]
            gradient = gradient - (1.0 / DT) * (slope[0] + slope[1])[:TX, :TY]
            weight = [counts[z] - (2.0 / DT) * chi[z] * slope[z] for z in range(NZ)]
            electric = [
                [electric[c][z] + weight[z] * past[c][z] - step * turn[c][z] for z in range(NZ)] for c in range(3)
            ]
        tiles[0] = gradient
        finish(electric, magnetic)

    def tile_copy(j):
        return pltpu.make_async_remote_copy(
            src_ref=tiles.at[0],
            dst_ref=tiles.at[j],
            send_sem=tile_send.at[j],
            recv_sem=tile_sem.at[j],
            device_id=device(grp, j, 0),
            device_id_type=MESH,
        )

    def share_copy(i):
        return pltpu.make_async_remote_copy(
            src_ref=shares.at[i],
            dst_ref=gathered.at[i],
            send_sem=share_send.at[i],
            recv_sem=share_sem.at[i],
            device_id=device(lax.rem(grp + i // n_gy, 4), 0, lax.rem(i, n_gy)),
            device_id_type=MESH,
        )

    def each(low, high, act):
        def body(i, carry):
            act(i)
            return carry

        lax.fori_loop(low, high, body, 0)

    @pl.when(jnp.logical_not(forward))
    def _():
        each(1, n_gx, lambda j: tile_copy(j).start())
        each(1, n_gx, lambda j: tile_copy(j).wait_recv())
        rest = jnp.concatenate([tiles[j] for j in range(n_gx)], axis=0)
        total = jnp.zeros((4 * n_gy * SHARE, TY), F32)
        for _ in range(3):
            part = rest.astype(BF16)
            total = total + jnp.dot(chosen[...], part, preferred_element_type=F32)
            rest = rest - part.astype(F32)
        for i in range(4 * n_gy):
            shares[i] = total[SHARE * i : SHARE * (i + 1)]
        gathered[0] = total[:SHARE]
        each(1, 4 * n_gy, lambda i: share_copy(i).start())

    sum_of = jnp.zeros((SHARE, TY), F32)
    for lane in (2, 3):
        start = lax.rem(grp + 4 - lane, 4) * n_gy
        each(start + jnp.where(start == 0, 1, 0), start + n_gy, lambda i: share_copy(i).wait_recv())
        for j in range(n_gy):
            sum_of = sum_of + gathered[start + j]
    design_grad[...] = sum_of

    for copy in rim_copies():
        copy.wait_send()
    for i in range(8):
        half_copy(ahead, i).wait_send()
    state_copy().wait()

    @pl.when(forward)
    def _():
        whole_half().wait_send()
        for n in range(STEPS):
            if n < HALF:
                kept_copy(n).wait()
            else:
                record_copy(n).wait_send()

    @pl.when(jnp.logical_not(forward))
    def _():
        for n in range(HALF, STEPS):
            record_copy(n).wait_recv()
        each(1, n_gx, lambda j: tile_copy(j).wait_send())
        each(1, 4 * n_gy, lambda i: share_copy(i).wait_send())


def local(fields, stored, material, design, mat_eps, mat_chi, source_wave, source_cells, monitor_cells, owners):
    n_gx, n_gy = lax.axis_size("gx"), lax.axis_size("gy")
    vmem = pl.BlockSpec(memory_space=pltpu.VMEM)
    smem = pl.BlockSpec(memory_space=pltpu.SMEM)
    anywhere = pl.BlockSpec(memory_space=pl.ANY)
    dma = pltpu.SemaphoreType.DMA
    cells = source_cells.shape[0]
    fields_next, stored_next, design_grad = pl.pallas_call(
        functools.partial(kernel, n_gx, n_gy),
        out_shape=(
            jax.ShapeDtypeStruct((6, NZ, TX, TY), F32),
            jax.ShapeDtypeStruct((HALF, 6, NZ, TX, TY), BF16),
            jax.ShapeDtypeStruct((SHARE, TY), F32),
        ),
        in_specs=[vmem, vmem, vmem, vmem, smem, smem, smem, vmem, vmem, vmem],
        out_specs=(anywhere, anywhere, vmem),
        scratch_shapes=[
            pltpu.VMEM((TX, TY), F32),
            pltpu.VMEM((HALF, TX, TY), BF16),
            pltpu.VMEM((2, 8, 8, TY), F32),
            pltpu.VMEM((2, 6, TX, TY), BF16),
            pltpu.VMEM((2, TX, TY), F32),
            pltpu.VMEM((4, 8, TY), F32),
            pltpu.VMEM((2, 8, 8, TY), F32),
            pltpu.VMEM((2, 6, HALF, TX, TY), BF16),
            pltpu.VMEM((2, 2, 6, TX, TY), BF16),
            pltpu.VMEM((HALF, 6, NZ, TX, TY), BF16),
            pltpu.VMEM((STEPS, 6, NZ, TX, TY), BF16),
            pltpu.VMEM((6, NZ, TX, TY), F32),
            pltpu.VMEM((NZ * EX, EY), F32),
            pltpu.VMEM((4 * n_gy * SHARE, n_gx * TX), BF16),
            pltpu.VMEM((n_gx, TX, TY), F32),
            pltpu.VMEM((4 * n_gy, SHARE, TY), F32),
            pltpu.VMEM((4 * n_gy, SHARE, TY), F32),
            dma((8,)),
            dma((8,)),
            dma,
            dma((8,)),
            dma((2, 8)),
            dma,
            dma((HALF,)),
            dma((HALF,)),
            dma((n_gx,)),
            dma((n_gx,)),
            dma((4 * n_gy,)),
            dma((4 * n_gy,)),
            dma((3,)),
        ],
        compiler_params=pltpu.CompilerParams(
            collective_id=0, has_side_effects=True, vmem_limit_bytes=32 * 1024 * 1024
        ),
        name="interval",
    )(
        fields[0],
        stored[0],
        material,
        design,
        mat_eps,
        mat_chi,
        source_wave,
        source_cells.reshape(cells // TY, TY),
        monitor_cells.reshape(cells // TY, TY),
        owners.reshape(n_gx, TX * n_gy),
    )
    return fields_next[None], stored_next[None], design_grad


def solution(mesh):
    in_specs = (
        P("grp", None, None, "gx", "gy"),
        P("grp", None, None, None, "gx", "gy"),
        P(None, "gx", "gy"),
        P("gx", "gy"),
        P(),
        P(),
        P(),
        P(),
        P(),
        P(),
    )
    out_specs = (
        P("grp", None, None, "gx", "gy"),
        P("grp", None, None, None, "gx", "gy"),
        P(("grp", "gx", "gy"), None),
    )
    return jax.shard_map(local, mesh=mesh, in_specs=in_specs, out_specs=out_specs, check_vma=False)
```

```python
import functools

import jax
import jax.numpy as jnp
from jax import lax
from jax.experimental import pallas as pl
from jax.experimental.pallas import tpu as pltpu
from jax.sharding import PartitionSpec as P

MESH = pl.DeviceIdType.MESH
F32 = jnp.float32
BF16 = jnp.bfloat16

NZ = 2
TX = 16
TY = 128
RIM = 4
EX = TX + 2 * RIM
EY = 2 * TY
STEPS = 4
HALF = 2
DT = 0.5
SHARE = 4

AROUND = ((-1, 0), (1, 0), (0, -1), (0, 1), (-1, -1), (-1, 1), (1, -1), (1, 1))


def far_first(length):
    return sorted(range(length), key=lambda j: -min(j, length - j))


def iota(shape, axis):
    return lax.broadcasted_iota(jnp.int32, shape, axis)


def pack_columns(planes, slot=8):
    column = iota((TX, TY), 1)
    window = ((column + slot // 2) // slot) % (TY // slot)
    packed = planes[0]
    for p in range(1, len(planes)):
        packed = jnp.where(window == p, pltpu.roll(planes[p], slot * p, 1), packed)
    return packed


def pack_rows(one, two):
    low = iota((8, TY), 0) < RIM
    first = jnp.where(low, one[:8], one[8:])
    second = pltpu.roll(jnp.where(low, two[:8], two[8:]), RIM, 0)
    return jnp.where(low, first, second), jnp.where(low, second, first)


def unpack_rows(after, before):
    low = iota((8, TY), 0) < RIM
    return jnp.where(low, after, before), pltpu.roll(jnp.where(low, before, after), RIM, 0)


def pack_thin_rows(planes):
    row = iota((8, TY), 0)
    both = [jnp.where(row < RIM, p[:8], p[8:]) for p in planes]
    before = after = both[0]
    for q in range(1, len(planes)):
        turned = pltpu.roll(both[q], 2 * q, 0)
        before = jnp.where(row // 2 == q, turned, before)
        after = jnp.where((row // 2 + 1) % 4 == q, turned, after)
    return before, after


def unpack_thin_rows(after, before, q):
    rows = jnp.where(iota((8, TY), 0) // 2 == q, after, before)
    return rows if q == 0 else pltpu.roll(rows, 8 - 2 * q, 0)


def merge_columns(right, left, corners, slot=8):
    side = iota((TX, TY), 1) % slot < slot // 2
    beside = jnp.where(side, right, left)
    side = side[:8]
    from_after_right, from_after_left, from_before_right, from_before_left = corners
    low = iota((8, TY), 0) < RIM
    after = jnp.where(side, from_after_right, from_after_left)
    before = jnp.where(side, from_before_right, from_before_left)
    return jnp.concatenate([beside, jnp.where(low, after, before)], axis=0)


def extended(tile, rows, columns, shift):
    body = jnp.concatenate([tile, rows], axis=0)
    beside = columns if shift == 0 else pltpu.roll(columns, TY - shift, 1)
    return jnp.concatenate([body, beside], axis=1)


def next_x(v):
    return pltpu.roll(v, EX - 1, 0) - v


def next_y(v):
    return pltpu.roll(v, EY - 1, 1) - v


def next_z(v):
    return [v[1] - v[0], -v[1]]


def last_x(v):
    return v - pltpu.roll(v, 1, 0)


def last_y(v):
    return v - pltpu.roll(v, 1, 1)


def last_z(v):
    return [v[0], v[1] - v[0]]


def curl(v, along_x, along_y, along_z):
    z_of_y, z_of_x = along_z(v[1]), along_z(v[0])
    return (
        [along_y(v[2][z]) - z_of_y[z] for z in range(NZ)],
        [z_of_x[z] - along_x(v[2][z]) for z in range(NZ)],
        [along_x(v[1][z]) - along_y(v[0][z]) for z in range(NZ)],
    )


def curl_up(v):
    return curl(v, next_x, next_y, next_z)


def curl_down(v):
    return curl(v, last_x, last_y, last_z)


def kernel(
    n_gx,
    n_gy,
    fields_in,
    stored_in,
    material_in,
    design_in,
    mat_eps_in,
    mat_chi_in,
    source_wave_in,
    source_cells_in,
    monitor_cells_in,
    owners_in,
    fields_next,
    stored_next,
    design_grad,
    fields,
    stored,
    material,
    design,
    mat_eps,
    mat_chi,
    source_wave,
    source_cells,
    monitor_cells,
    owners,
    col_out,
    colh_out,
    row_out,
    rowh_out,
    col_in,
    corner_in,
    row_in,
    colh_in,
    rowh_in,
    half_in,
    rowc_out,
    rowc_in,
    colc_out,
    colc_in,
    records,
    state,
    counts_ref,
    chosen,
    tiles,
    shares,
    gathered,
    own_sem,
    ownh_sem,
    half_send,
    in_sem,
    inh_sem,
    half_sem,
    thin_send,
    thin_sem,
    record_send,
    record_sem,
    tile_send,
    tile_sem,
    share_send,
    share_sem,
    local_sem,
    load_sem,
):
    grp, gx, gy = lax.axis_index("grp"), lax.axis_index("gx"), lax.axis_index("gy")
    forward = grp < 2
    twin = jnp.where(forward, grp + 2, grp - 2)

    def device(lane, dx, dy):
        return {
            "grp": lane,
            "gx": lax.rem(gx + dx + n_gx, n_gx),
            "gy": lax.rem(gy + dy + n_gy, n_gy),
        }

    barrier = pltpu.get_barrier_semaphore()

    def greet(target):
        pl.semaphore_signal(barrier, inc=1, device_id=target, device_id_type=MESH)

    def on_grid(dx, dy):
        x, y = gx + dx, gy + dy
        return (x >= 0) & (x < n_gx) & (y >= 0) & (y < n_gy)

    neighbours = 0
    for dx, dy in AROUND[::-1]:
        neighbours = neighbours + jnp.where(on_grid(dx, dy), 1, 0)

        @pl.when(on_grid(dx, dy))
        def _():
            greet(device(twin, dx, dy))
            greet(device(grp, dx, dy))

    greet(device(twin, 0, 0))

    held = (fields, stored, material, design, mat_eps, mat_chi, source_wave, source_cells, monitor_cells, owners)
    given = (
        fields_in,
        stored_in,
        material_in,
        design_in,
        mat_eps_in,
        mat_chi_in,
        source_wave_in,
        source_cells_in,
        monitor_cells_in,
        owners_in,
    )
    loads = [pltpu.make_async_copy(a, b, load_sem.at[i]) for i, (a, b) in enumerate(zip(given, held))]
    for load in loads:
        load.start()

    @pl.when(forward)
    def _():
        for j in range(n_gy):
            for lane in (2, 3):
                greet({"grp": lane, "gx": gx, "gy": lax.rem(gy + far_first(n_gy)[j], n_gy)})

    @pl.when(jnp.logical_not(forward))
    def _():
        for j in far_first(n_gy):
            for lane in range(4):
                if j + lane:
                    greet(device(lax.rem(grp + lane, 4), 0, j))
        for j in far_first(n_gx)[:-1]:
            greet(device(grp, j, 0))

    for i, (dx, dy) in enumerate(AROUND):
        x, y = gx - dx, gy - dy

        @pl.when((x < 0) | (x >= n_gx) | (y < 0) | (y >= n_gy))
        def _():
            if i < 2:
                row_in[i] = jnp.zeros(row_in.shape[1:], F32)
                rowh_in[i] = jnp.zeros(rowh_in.shape[1:], BF16)
                rowc_in[i] = jnp.zeros(rowc_in.shape[1:], BF16)
                return
            if i < 4:
                col_in[i - 2] = jnp.zeros(col_in.shape[1:], F32)
            else:
                corner_in[i - 4] = jnp.zeros(corner_in.shape[1:], F32)
            colh_in[i - 2] = jnp.zeros(colh_in.shape[1:], BF16)
            colc_in[i - 2] = jnp.zeros(colc_in.shape[1:], BF16)

    def lookup(index, entries):
        value = jnp.zeros(index.shape, F32)
        for k in range(4):
            value = jnp.where(index == k, entries[k], value)
        return value

    def own_planes():
        kinds = [material[z] for z in range(NZ)]
        eps = [lookup(kinds[z], mat_eps) + design[...] for z in range(NZ)]
        chi = [lookup(kinds[z], mat_chi) for z in range(NZ)]
        return [fields[c, z] for c in range(6) for z in range(NZ)] + eps + chi

    def half_planes(k, components):
        return [stored[k, c, z].astype(F32) for c in range(components) for z in range(NZ)]

    def row_copy(i):
        return pltpu.make_async_remote_copy(
            src_ref=row_out.at[i],
            dst_ref=row_in.at[i],
            send_sem=own_sem.at[i],
            recv_sem=in_sem.at[i],
            device_id=device(grp, *AROUND[i]),
            device_id_type=MESH,
        )

    def col_copy(i):
        return pltpu.make_async_remote_copy(
            src_ref=col_out,
            dst_ref=col_in.at[i - 2],
            send_sem=own_sem.at[i],
            recv_sem=in_sem.at[i],
            device_id=device(grp, *AROUND[i]),
            device_id_type=MESH,
        )

    def corner_copy(i):
        start = 0 if AROUND[i][0] < 0 else 8
        return pltpu.make_async_remote_copy(
            src_ref=col_out.at[pl.ds(start, 8)],
            dst_ref=corner_in.at[i - 4],
            send_sem=own_sem.at[i],
            recv_sem=in_sem.at[i],
            device_id=device(grp, *AROUND[i]),
            device_id_type=MESH,
        )

    def rim_copies():
        return [row_copy(0), row_copy(1), col_copy(2), col_copy(3)] + [corner_copy(i) for i in range(4, 8)]

    def half_copy(k, i):
        if i < 2:
            src, dst = rowh_out.at[i, k], rowh_in.at[i, k]
        else:
            src, dst = colh_out.at[k], colh_in.at[i - 2, k]
        return pltpu.make_async_remote_copy(
            src_ref=src,
            dst_ref=dst,
            send_sem=ownh_sem.at[k, i],
            recv_sem=inh_sem.at[k, i],
            device_id=device(grp, *AROUND[i]),
            device_id_type=MESH,
        )

    def thin_copy(i):
        if i < 2:
            src, dst = rowc_out.at[i], rowc_in.at[i]
        else:
            src, dst = colc_out, colc_in.at[i - 2]
        return pltpu.make_async_remote_copy(
            src_ref=src,
            dst_ref=dst,
            send_sem=thin_send.at[i],
            recv_sem=thin_sem.at[i],
            device_id=device(twin, *AROUND[i]),
            device_id_type=MESH,
        )

    def whole_half(k):
        return pltpu.make_async_remote_copy(
            src_ref=stored.at[k],
            dst_ref=half_in.at[k],
            send_sem=half_send.at[k],
            recv_sem=half_sem.at[k],
            device_id=device(twin, 0, 0),
            device_id_type=MESH,
        )

    def sent(i, act):
        pl.when(on_grid(*AROUND[i]))(act)

    def received(i, act):
        dx, dy = AROUND[i]
        pl.when(on_grid(-dx, -dy))(act)

    def send_rims():
        for i, copy in enumerate(rim_copies()):
            sent(i, copy.start)

    def pack_rims():
        planes = own_planes()
        col_out[...] = pack_columns(planes)
        for i in range(8):
            row_out[0, i], row_out[1, i] = pack_rows(planes[2 * i], planes[2 * i + 1])

    def all_in():
        pl.semaphore_wait(barrier, 2 * neighbours + 1 + jnp.where(forward, 2 * n_gy, n_gx - 1 + 4 * n_gy - 1))

    stored_load = loads.pop(1)

    @pl.when(forward)
    def _():
        stored_load.wait()
        planes = half_planes(1, 6) + half_planes(0, 3)
        colc_out[...] = pack_columns(planes, RIM).astype(BF16)
        parts = [pack_thin_rows(planes[i : i + 4]) for i in range(0, len(planes), 4)]
        parts.append(parts[-1])
        for i in range(3):
            for side in range(2):
                rowc_out[side, i] = jnp.concatenate(
                    [parts[2 * i][side], parts[2 * i + 1][side]], axis=0
                ).astype(BF16)
        all_in()
        for i in range(8):
            sent(i, thin_copy(i).start)
        for k in range(HALF - 1, -1, -1):
            whole_half(k).start()
        for load in loads:
            load.wait()
        pack_rims()
        send_rims()

    @pl.when(jnp.logical_not(forward))
    def _():
        for load in loads:
            load.wait()
        pack_rims()
        all_in()
        send_rims()
        stored_load.wait()
        for k in range(HALF - 1, -1, -1):
            planes = half_planes(k, 6)
            colh_out[k] = pack_columns(planes).astype(BF16)
            for i in range(3):
                one = pack_rows(planes[4 * i], planes[4 * i + 1])
                two = pack_rows(planes[4 * i + 2], planes[4 * i + 3])
                for side in range(2):
                    rowh_out[side, k, i] = jnp.concatenate([one[side], two[side]], axis=0).astype(BF16)
            for i in range(8):
                sent(i, half_copy(k, i).start)

    row = iota((NZ * EX, TY), 0)
    depth = jnp.where(row >= EX, 1, 0)
    row = row - depth * EX
    x = gx * TX + jnp.where(row < TX + RIM, row, row - EX)
    sought_x = jnp.where((x >= 0) & (x < n_gx * TX), depth * (n_gx * TX) + x, -1)
    column = iota((TY, TY), 0)
    sought_y = gy * TY + column
    sought_high = sought_y[:8] + TY
    sought_low = sought_y[TY - 8 :] - TY
    listed = jnp.where(forward, source_cells[...], monitor_cells[...])
    listed_x = listed // (n_gy * TY)
    listed_y = listed % (n_gy * TY)

    def hits(found):
        return jnp.where(found, 1.0, 0.0)

    def wide(m, i, rows):
        return jnp.broadcast_to(m[i : i + 1], (rows, TY))

    entries = listed.shape[0]
    rows_hit = jnp.concatenate(
        [hits(wide(listed_x, i, NZ * EX) == sought_x) for i in range(entries)], axis=1
    ).astype(BF16)
    columns_hit = jnp.concatenate(
        [hits(wide(listed_y, i, TY) == sought_y) for i in range(entries)], axis=1
    ).astype(BF16)
    high_hit = jnp.concatenate([hits(wide(listed_y, i, 8) == sought_high) for i in range(entries)], axis=1)
    low_hit = jnp.concatenate([hits(wide(listed_y, i, 8) == sought_low) for i in range(entries)], axis=1)
    rim_hit = jnp.concatenate(
        [high_hit, jnp.zeros((TY - 16, entries * TY), F32), low_hit], axis=0
    ).astype(BF16)

    def tally(a, b):
        return lax.dot_general(a, b, (((1,), (1,)), ((), ())), preferred_element_type=F32)

    counts_ref[...] = jnp.concatenate([tally(rows_hit, columns_hit), tally(rows_hit, rim_hit)], axis=1)

    @pl.when(jnp.logical_not(forward))
    def _():
        lanes = owners.shape[1]
        pick = iota((TX, lanes), 1) == iota((TX, lanes), 0) * n_gy + gy
        coarse, fine = [], []
        for j in range(n_gx):
            line = jnp.broadcast_to(owners[pl.ds(lax.rem(gx - j + n_gx, n_gx), 1)], (TX, lanes))
            line = jnp.where(pick, line, 0)
            part = line // 64 * 64
            coarse.append(part.astype(F32))
            fine.append((line - part).astype(F32))
        rows = 4 * n_gy * SHARE
        ones = jnp.ones((rows, lanes), BF16)
        owner = tally(ones, jnp.concatenate(coarse, axis=0).astype(BF16))
        owner = owner + tally(ones, jnp.concatenate(fine, axis=0).astype(BF16))
        place = iota((rows, n_gx * TX), 0)
        share = place // SHARE
        lane = (grp + share // n_gy) % 4
        spot = (gy + share % n_gy) % n_gy
        wanted = ((lane * n_gx + gx) * n_gy + spot) * SHARE + place % SHARE
        chosen[...] = jnp.where(owner == wanted.astype(F32), 1.0, 0.0).astype(BF16)

    row = iota((EX, EY), 0)
    column = iota((EX, EY), 1)
    x = gx * TX + jnp.where(row < TX + RIM, row, row - EX)
    y = gy * TY + jnp.where(column < TY + TY // 2, column, column - EY)
    inside = (x >= 0) & (x < n_gx * TX) & (y >= 0) & (y < n_gy * TY)
    unit = jnp.where(inside, 1.0, 0.0)
    step = jnp.where(inside, DT, 0.0)
    counts = [counts_ref[z * EX : (z + 1) * EX] for z in range(NZ)]

    for i, copy in enumerate(rim_copies()):
        received(i, copy.wait_recv)
    own = own_planes()
    columns = merge_columns(col_in[0], col_in[1], [corner_in[i] for i in range(4)])
    whole = []
    for i in range(8):
        for k, rows in enumerate(unpack_rows(row_in[0, i], row_in[1, i])):
            whole.append(extended(own[2 * i + k], rows, columns, 8 * (2 * i + k)))
    eps = [jnp.where(inside, v, 1.0) for v in whole[12:14]]
    chi = whole[14:16]
    whole = [jnp.where(inside, v, 0.0) for v in whole[:12]]
    first = [whole[2 * c : 2 * c + 2] for c in range(3)]
    second = [whole[2 * c : 2 * c + 2] for c in range(3, 6)]

    def state_copy():
        return pltpu.make_async_copy(state, fields_next, local_sem.at[0])

    def finish(electric, magnetic):
        for c in range(3):
            for z in range(NZ):
                state[c, z] = electric[c][z][:TX, :TY]
                state[3 + c, z] = magnetic[c][z][:TX, :TY]
        state_copy().start()

    def record_copy(n):
        return pltpu.make_async_remote_copy(
            src_ref=records.at[n],
            dst_ref=stored_next.at[n - HALF],
            send_sem=record_send.at[n - HALF],
            recv_sem=record_sem.at[n - HALF],
            device_id=device(twin, 0, 0),
            device_id_type=MESH,
        )

    def kept_copy(n):
        return pltpu.make_async_copy(records.at[n], stored_next.at[n], local_sem.at[1 + n])

    def square(v, z):
        return v[0][z] * v[0][z] + v[1][z] * v[1][z] + v[2][z] * v[2][z]

    @pl.when(forward)
    def _():
        electric, magnetic = first, second
        for n in range(STEPS):
            factor = [step / (eps[z] + chi[z] * square(electric, z)) for z in range(NZ)]
            turn = curl_up(electric)
            magnetic = [[magnetic[c][z] - step * turn[c][z] for z in range(NZ)] for c in range(3)]
            turn = curl_down(magnetic)
            for c in range(3):
                for z in range(NZ):
                    records[n, c, z] = electric[c][z][:TX, :TY].astype(BF16)
                    records[n, 3 + c, z] = turn[c][z][:TX, :TY].astype(BF16)
            (kept_copy if n < HALF else record_copy)(n).start()
            wave = source_wave[lax.rem(grp, 2), n]
            electric = [[electric[c][z] + factor[z] * turn[c][z] for z in range(NZ)] for c in range(3)]
            electric[0] = [electric[0][z] + wave * counts[z] for z in range(NZ)]
        finish(electric, magnetic)

    def corners_of(packed):
        return [packed[2][:8], packed[3][:8], packed[4][8:], packed[5][8:]]

    def vectors(planes):
        return [planes[2 * c : 2 * c + 2] for c in range(len(planes) // 2)]

    def late_snapshot(k):
        rows = []
        for i in range(3):
            after, before = rowh_in[0, k, i].astype(F32), rowh_in[1, k, i].astype(F32)
            rows.extend(unpack_rows(after[:8], before[:8]))
            rows.extend(unpack_rows(after[8:], before[8:]))
        packed = [colh_in[i, k].astype(F32) for i in range(6)]
        columns = merge_columns(packed[0], packed[1], corners_of(packed))
        return vectors([extended(v, rows[p], columns, 8 * p) for p, v in enumerate(half_planes(k, 6))])

    def early_snapshot(k, columns):
        planes = []
        for p in range(12):
            tile = half_in[k, p // NZ, p % NZ].astype(F32)
            place = p if k else 12 + p
            if place >= 18:
                planes.append(extended(tile, jnp.zeros((8, TY), F32), jnp.zeros((EX, TY), F32), 0))
                continue
            slot = slice(8 * (place // 4 % 2), 8 * (place // 4 % 2) + 8)
            after, before = [rowc_in[side, place // 8].astype(F32)[slot] for side in range(2)]
            planes.append(extended(tile, unpack_thin_rows(after, before, place % 4), columns, RIM * place))
        return vectors(planes)

    def tile_copy(j):
        return pltpu.make_async_remote_copy(
            src_ref=tiles.at[0],
            dst_ref=tiles.at[j],
            send_sem=tile_send.at[j],
            recv_sem=tile_sem.at[j],
            device_id=device(grp, j, 0),
            device_id_type=MESH,
        )

    def share_copy(i):
        return pltpu.make_async_remote_copy(
            src_ref=shares.at[i],
            dst_ref=gathered.at[i],
            send_sem=share_send.at[i],
            recv_sem=share_sem.at[i],
            device_id=device(lax.rem(grp + i // n_gy, 4), 0, lax.rem(i, n_gy)),
            device_id_type=MESH,
        )

    @pl.when(jnp.logical_not(forward))
    def _():
        electric, magnetic = first, second
        gradient = jnp.zeros((TX, TY), F32)
        for n in range(STEPS - 1, -1, -1):
            if n >= HALF:
                for i in range(8):
                    received(i, half_copy(n - HALF, i).wait_recv)
                snapshot = late_snapshot(n - HALF)
            else:
                whole_half(n).wait_recv()
                if n == HALF - 1:
                    for i in range(8):
                        received(i, thin_copy(i).wait_recv)
                    packed = [colc_in[i].astype(F32) for i in range(6)]
                    columns = merge_columns(packed[0], packed[1], corners_of(packed), RIM)
                snapshot = early_snapshot(n, columns)
            past, curled = snapshot[:3], snapshot[3:]
            factor = [DT / (eps[z] + chi[z] * square(past, z)) for z in range(NZ)]
            inner = [
                curled[0][z] * electric[0][z] + curled[1][z] * electric[1][z] + curled[2][z] * electric[2][z]
                for z in range(NZ)
            ]
            slope = [factor[z] * factor[z] * inner[z] for z in range(NZ)]
            gradient = gradient - (1.0 / DT) * (slope[0] + slope[1])[:TX, :TY]
            if n == 0:
                tiles[0] = gradient
                for j in far_first(n_gx)[:-1]:
                    tile_copy(j).start()
            turn = curl_up([[factor[z] * electric[c][z] for z in range(NZ)] for c in range(3)])
            magnetic = [[magnetic[c][z] + unit * turn[c][z] for z in range(NZ)] for c in range(3)]
            turn = curl_down(magnetic)
            weight = [counts[z] - (2.0 / DT) * chi[z] * slope[z] for z in range(NZ)]
            electric = [
                [electric[c][z] + weight[z] * past[c][z] - step * turn[c][z] for z in range(NZ)] for c in range(3)
            ]
        finish(electric, magnetic)

    def each(low, high, act):
        def body(i, carry):
            act(i)
            return carry

        lax.fori_loop(low, high, body, 0)

    @pl.when(jnp.logical_not(forward))
    def _():
        for j in range(1, n_gx):
            tile_copy(j).wait_recv()
        rest = jnp.concatenate([tiles[j] for j in range(n_gx)], axis=0)
        total = jnp.zeros((4 * n_gy * SHARE, TY), F32)
        for _ in range(3):
            part = rest.astype(BF16)
            total = total + jnp.dot(chosen[...], part, preferred_element_type=F32)
            rest = rest - part.astype(F32)
        for i in range(4 * n_gy):
            shares[i] = total[SHARE * i : SHARE * (i + 1)]
        gathered[0] = total[:SHARE]
        for j in far_first(n_gy):
            for lane in (2, 1, 3, 0):
                if lane + j:
                    share_copy(lane * n_gy + j).start()

    sum_of = jnp.zeros((SHARE, TY), F32)
    for lane in (2, 3):
        start = lax.rem(grp + 4 - lane, 4) * n_gy
        each(start + jnp.where(start == 0, 1, 0), start + n_gy, lambda i: share_copy(i).wait_recv())
        for j in range(n_gy):
            sum_of = sum_of + gathered[start + j]
    design_grad[...] = sum_of

    for i, copy in enumerate(rim_copies()):
        sent(i, copy.wait_send)
    state_copy().wait()

    @pl.when(forward)
    def _():
        for k in range(HALF):
            whole_half(k).wait_send()
        for i in range(8):
            sent(i, thin_copy(i).wait_send)
        for n in range(STEPS):
            if n < HALF:
                kept_copy(n).wait()
            else:
                record_copy(n).wait_send()

    @pl.when(jnp.logical_not(forward))
    def _():
        for k in range(HALF):
            for i in range(8):
                sent(i, half_copy(k, i).wait_send)
        for n in range(HALF, STEPS):
            record_copy(n).wait_recv()
        for j in range(1, n_gx):
            tile_copy(j).wait_send()
        for i in range(1, 4 * n_gy):
            share_copy(i).wait_send()


def store(fields, stored, design_grad, fields_next, stored_next, design_grad_next):
    fields_next[...] = fields[...]
    stored_next[...] = stored[...]
    design_grad_next[...] = design_grad[...]


def local(fields, stored, material, design, mat_eps, mat_chi, source_wave, source_cells, monitor_cells, owners):
    n_gx, n_gy = lax.axis_size("gx"), lax.axis_size("gy")
    vmem = pl.BlockSpec(memory_space=pltpu.VMEM)
    hbm = pl.BlockSpec(memory_space=pltpu.HBM)
    dma = pltpu.SemaphoreType.DMA
    cells = source_cells.shape[0]
    outs = pl.pallas_call(
        functools.partial(kernel, n_gx, n_gy),
        out_shape=(
            jax.ShapeDtypeStruct((6, NZ, TX, TY), F32),
            jax.ShapeDtypeStruct((HALF, 6, NZ, TX, TY), BF16),
            jax.ShapeDtypeStruct((SHARE, TY), F32),
        ),
        in_specs=[hbm] * 10,
        out_specs=(hbm, hbm, vmem),
        scratch_shapes=[
            pltpu.VMEM((6, NZ, TX, TY), F32),
            pltpu.VMEM((HALF, 6, NZ, TX, TY), BF16),
            pltpu.VMEM((NZ, TX, TY), jnp.int32),
            pltpu.VMEM((TX, TY), F32),
            pltpu.SMEM((4,), F32),
            pltpu.SMEM((4,), F32),
            pltpu.SMEM((2, STEPS), F32),
            pltpu.VMEM((cells // TY, TY), jnp.int32),
            pltpu.VMEM((cells // TY, TY), jnp.int32),
            pltpu.VMEM((n_gx, TX * n_gy), jnp.int32),
            pltpu.VMEM((TX, TY), F32),
            pltpu.VMEM((HALF, TX, TY), BF16),
            pltpu.VMEM((2, 8, 8, TY), F32),
            pltpu.VMEM((2, HALF, 3, TX, TY), BF16),
            pltpu.VMEM((2, TX, TY), F32),
            pltpu.VMEM((4, 8, TY), F32),
            pltpu.VMEM((2, 8, 8, TY), F32),
            pltpu.VMEM((6, HALF, TX, TY), BF16),
            pltpu.VMEM((2, HALF, 3, TX, TY), BF16),
            pltpu.VMEM((HALF, 6, NZ, TX, TY), BF16),
            pltpu.VMEM((2, 3, TX, TY), BF16),
            pltpu.VMEM((2, 3, TX, TY), BF16),
            pltpu.VMEM((TX, TY), BF16),
            pltpu.VMEM((6, TX, TY), BF16),
            pltpu.VMEM((STEPS, 6, NZ, TX, TY), BF16),
            pltpu.VMEM((6, NZ, TX, TY), F32),
            pltpu.VMEM((NZ * EX, EY), F32),
            pltpu.VMEM((4 * n_gy * SHARE, n_gx * TX), BF16),
            pltpu.VMEM((n_gx, TX, TY), F32),
            pltpu.VMEM((4 * n_gy, SHARE, TY), F32),
            pltpu.VMEM((4 * n_gy, SHARE, TY), F32),
            dma((8,)),
            dma((HALF, 8)),
            dma((HALF,)),
            dma((8,)),
            dma((HALF, 8)),
            dma((HALF,)),
            dma((8,)),
            dma((8,)),
            dma((HALF,)),
            dma((HALF,)),
            dma((n_gx,)),
            dma((n_gx,)),
            dma((4 * n_gy,)),
            dma((4 * n_gy,)),
            dma((3,)),
            dma((10,)),
        ],
        compiler_params=pltpu.CompilerParams(
            collective_id=0, has_side_effects=True, vmem_limit_bytes=56 * 1024 * 1024
        ),
        name="interval",
    )(
        fields[0],
        stored[0],
        material,
        design,
        mat_eps,
        mat_chi,
        source_wave,
        source_cells.reshape(cells // TY, TY),
        monitor_cells.reshape(cells // TY, TY),
        owners.reshape(n_gx, TX * n_gy),
    )
    fields_next, stored_next, design_grad = pl.pallas_call(
        store,
        out_shape=tuple(jax.ShapeDtypeStruct(a.shape, a.dtype) for a in outs),
        in_specs=[vmem] * 3,
        out_specs=(vmem,) * 3,
        compiler_params=pltpu.CompilerParams(vmem_limit_bytes=56 * 1024 * 1024),
        name="store",
    )(*outs)
    return fields_next[None], stored_next[None], design_grad


def solution(mesh):
    in_specs = (
        P("grp", None, None, "gx", "gy"),
        P("grp", None, None, None, "gx", "gy"),
        P(None, "gx", "gy"),
        P("gx", "gy"),
        P(),
        P(),
        P(),
        P(),
        P(),
        P(),
    )
    out_specs = (
        P("grp", None, None, "gx", "gy"),
        P("grp", None, None, None, "gx", "gy"),
        P(("grp", "gx", "gy"), None),
    )
    return jax.shard_map(local, mesh=mesh, in_specs=in_specs, out_specs=out_specs, check_vma=False)
```

```python
import functools
import math

import jax
import jax.numpy as jnp
from jax import lax
from jax.experimental import pallas as pl
from jax.experimental.pallas import tpu as pltpu
from jax.sharding import PartitionSpec as P

MESH = pl.DeviceIdType.MESH
F32 = jnp.float32
BF16 = jnp.bfloat16

NZ = 2
TX = 16
TY = 128
RIM = 4
EX = TX + 2 * RIM
EY = 2 * TY
STEPS = 4
HALF = 2
DT = 0.5
SHARE = 4

AROUND = ((-1, 0), (1, 0), (0, -1), (0, 1), (-1, -1), (-1, 1), (1, -1), (1, 1))


def far_first(length):
    return sorted(range(length), key=lambda j: -min(j, length - j))


def iota(shape, axis):
    return lax.broadcasted_iota(jnp.int32, shape, axis)


def pack_columns(planes, slot=8):
    column = iota((TX, TY), 1)
    window = ((column + slot // 2) // slot) % (TY // slot)
    packed = planes[0]
    for p in range(1, len(planes)):
        packed = jnp.where(window == p, pltpu.roll(planes[p], slot * p, 1), packed)
    return packed


def pack_rows(one, two):
    low = iota((8, TY), 0) < RIM
    first = jnp.where(low, one[:8], one[8:])
    second = pltpu.roll(jnp.where(low, two[:8], two[8:]), RIM, 0)
    return jnp.where(low, first, second), jnp.where(low, second, first)


def unpack_rows(after, before):
    low = iota((8, TY), 0) < RIM
    return jnp.where(low, after, before), pltpu.roll(jnp.where(low, before, after), RIM, 0)


def pack_thin_rows(planes):
    row = iota((8, TY), 0)
    both = [jnp.where(row < RIM, p[:8], p[8:]) for p in planes]
    before = after = both[0]
    for q in range(1, len(planes)):
        turned = pltpu.roll(both[q], 2 * q, 0)
        before = jnp.where(row // 2 == q, turned, before)
        after = jnp.where((row // 2 + 1) % 4 == q, turned, after)
    return before, after


def unpack_thin_rows(after, before, q):
    rows = jnp.where(iota((8, TY), 0) // 2 == q, after, before)
    return rows if q == 0 else pltpu.roll(rows, 8 - 2 * q, 0)


def merge_columns(right, left, corners, slot=8):
    side = iota((TX, TY), 1) % slot < slot // 2
    beside = jnp.where(side, right, left)
    side = side[:8]
    from_after_right, from_after_left, from_before_right, from_before_left = corners
    low = iota((8, TY), 0) < RIM
    after = jnp.where(side, from_after_right, from_after_left)
    before = jnp.where(side, from_before_right, from_before_left)
    return jnp.concatenate([beside, jnp.where(low, after, before)], axis=0)


def extended(tile, rows, columns, shift):
    body = jnp.concatenate([tile, rows], axis=0)
    beside = columns if shift == 0 else pltpu.roll(columns, TY - shift, 1)
    return jnp.concatenate([body, beside], axis=1)


def next_x(v):
    return pltpu.roll(v, EX - 1, 0) - v


def next_y(v):
    return pltpu.roll(v, EY - 1, 1) - v


def next_z(v):
    return [v[1] - v[0], -v[1]]


def last_x(v):
    return v - pltpu.roll(v, 1, 0)


def last_y(v):
    return v - pltpu.roll(v, 1, 1)


def last_z(v):
    return [v[0], v[1] - v[0]]


def curl(v, along_x, along_y, along_z):
    z_of_y, z_of_x = along_z(v[1]), along_z(v[0])
    return (
        [along_y(v[2][z]) - z_of_y[z] for z in range(NZ)],
        [z_of_x[z] - along_x(v[2][z]) for z in range(NZ)],
        [along_x(v[1][z]) - along_y(v[0][z]) for z in range(NZ)],
    )


def curl_up(v):
    return curl(v, next_x, next_y, next_z)


def curl_down(v):
    return curl(v, last_x, last_y, last_z)


def kernel(
    n_gx,
    n_gy,
    fields_in,
    stored_in,
    material_in,
    design_in,
    mat_eps_in,
    mat_chi_in,
    source_wave_in,
    source_cells_in,
    monitor_cells_in,
    owners_in,
    fields_next,
    stored_next,
    gathered,
    fields,
    stored,
    material,
    design,
    mat_eps,
    mat_chi,
    source_wave,
    source_cells,
    monitor_cells,
    owners,
    col_out,
    colh_out,
    row_out,
    rowh_out,
    col_in,
    corner_in,
    row_in,
    colh_in,
    rowh_in,
    half_in,
    rowc_out,
    rowc_in,
    colc_out,
    colc_in,
    rowc_here,
    colc_here,
    records,
    state,
    counts_ref,
    chosen,
    tiles,
    shares,
    own_sem,
    ownh_sem,
    half_send,
    in_sem,
    inh_sem,
    half_sem,
    thin_send,
    thin_sem,
    hand_send,
    hand_sem,
    second_round,
    third_round,
    record_send,
    record_sem,
    tile_send,
    tile_sem,
    share_send,
    share_sem,
    local_sem,
    load_sem,
):
    grp, gx, gy = lax.axis_index("grp"), lax.axis_index("gx"), lax.axis_index("gy")
    forward = grp < 2
    twin = jnp.where(forward, grp + 2, grp - 2)

    def device(lane, dx, dy):
        return {
            "grp": lane,
            "gx": lax.rem(gx + dx + n_gx, n_gx),
            "gy": lax.rem(gy + dy + n_gy, n_gy),
        }

    barrier = pltpu.get_barrier_semaphore()
    side = math.isqrt(n_gx)

    def on_grid(dx, dy):
        x, y = gx + dx, gy + dy
        return (x >= 0) & (x < n_gx) & (y >= 0) & (y < n_gy)

    def greet(target):
        pl.semaphore_signal(barrier, inc=1, device_id=target, device_id_type=MESH)

    def in_row(d):
        return {"grp": grp, "gx": gx - gx % side + (gx + d) % side, "gy": gy}

    def in_pair(d, other):
        return {"grp": grp, "gx": gx, "gy": lax.rem(gy - gy % 2 + (gy + other) % 2 + 2 * d + n_gy, n_gy)}

    def in_lane(d):
        return device(lax.rem(grp + d, 4), 0, 0)

    neighbours = 0
    for dx, dy in AROUND[::-1]:
        if dx:
            neighbours = neighbours + jnp.where(on_grid(dx, dy), 1, 0)
            pl.when(on_grid(dx, dy))(functools.partial(greet, device(grp, dx, dy)))
    near = [in_pair(d, other) for d in (-1, 1) for other in (0, 1)] + [in_pair(0, 1)]
    near += [in_lane(d) for d in range(1, 4)]
    near += [in_row(d) for d in range(1, side)] + [device(grp, side * d, 0) for d in range(1, n_gx // side)]
    for target in near:
        greet(target)

    def all_in():
        pl.semaphore_wait(barrier, neighbours + len(near))
        for target in second:
            pl.semaphore_signal(second_round, inc=1, device_id=target, device_id_type=MESH)

    second = [in_pair(d, 0) for d in (-1, 1)] + [in_row(d) for d in range(1, side)]
    third = [in_lane(d) for d in range(1, 4)]

    def lane_in():
        pl.semaphore_wait(second_round, len(second))
        for target in third:
            pl.semaphore_signal(third_round, inc=1, device_id=target, device_id_type=MESH)

    held = (fields, stored, material, design, mat_eps, mat_chi, source_wave, source_cells, monitor_cells, owners)
    given = (
        fields_in,
        stored_in,
        material_in,
        design_in,
        mat_eps_in,
        mat_chi_in,
        source_wave_in,
        source_cells_in,
        monitor_cells_in,
        owners_in,
    )
    loads = [pltpu.make_async_copy(a, b, load_sem.at[i]) for i, (a, b) in enumerate(zip(given, held))]
    for load in loads:
        load.start()

    for i, (dx, dy) in enumerate(AROUND):
        x, y = gx - dx, gy - dy

        @pl.when((x < 0) | (x >= n_gx) | (y < 0) | (y >= n_gy))
        def _():
            if i < 2:
                row_in[i] = jnp.zeros(row_in.shape[1:], F32)
                rowh_in[i] = jnp.zeros(rowh_in.shape[1:], BF16)
                rowc_in[i] = jnp.zeros(rowc_in.shape[1:], BF16)
                return
            if i < 4:
                col_in[i - 2] = jnp.zeros(col_in.shape[1:], F32)
            else:
                corner_in[i - 4] = jnp.zeros(corner_in.shape[1:], F32)
            colh_in[i - 2] = jnp.zeros(colh_in.shape[1:], BF16)
            colc_in[i - 2] = jnp.zeros(colc_in.shape[1:], BF16)

    def lookup(index, entries):
        value = jnp.zeros(index.shape, F32)
        for k in range(4):
            value = jnp.where(index == k, entries[k], value)
        return value

    def own_planes():
        kinds = [material[z] for z in range(NZ)]
        eps = [lookup(kinds[z], mat_eps) + design[...] for z in range(NZ)]
        chi = [lookup(kinds[z], mat_chi) for z in range(NZ)]
        return [fields[c, z] for c in range(6) for z in range(NZ)] + eps + chi

    def half_planes(k, components):
        return [stored[k, c, z].astype(F32) for c in range(components) for z in range(NZ)]

    def row_copy(i):
        return pltpu.make_async_remote_copy(
            src_ref=row_out.at[i],
            dst_ref=row_in.at[i],
            send_sem=own_sem.at[i],
            recv_sem=in_sem.at[i],
            device_id=device(grp, *AROUND[i]),
            device_id_type=MESH,
        )

    def col_copy(i):
        return pltpu.make_async_remote_copy(
            src_ref=col_out,
            dst_ref=col_in.at[i - 2],
            send_sem=own_sem.at[i],
            recv_sem=in_sem.at[i],
            device_id=device(grp, *AROUND[i]),
            device_id_type=MESH,
        )

    def corner_copy(i):
        start = 0 if AROUND[i][0] < 0 else 8
        return pltpu.make_async_remote_copy(
            src_ref=col_out.at[pl.ds(start, 8)],
            dst_ref=corner_in.at[i - 4],
            send_sem=own_sem.at[i],
            recv_sem=in_sem.at[i],
            device_id=device(grp, *AROUND[i]),
            device_id_type=MESH,
        )

    def rim_copies():
        return [row_copy(0), row_copy(1), col_copy(2), col_copy(3)] + [corner_copy(i) for i in range(4, 8)]

    def half_copy(k, i):
        if i < 2:
            src, dst = rowh_out.at[i, k], rowh_in.at[i, k]
        else:
            src, dst = colh_out.at[k], colh_in.at[i - 2, k]
        return pltpu.make_async_remote_copy(
            src_ref=src,
            dst_ref=dst,
            send_sem=ownh_sem.at[k, i],
            recv_sem=inh_sem.at[k, i],
            device_id=device(grp, *AROUND[i]),
            device_id_type=MESH,
        )

    def thin_copies():
        pairs = ((rowc_out, rowc_here), (colc_out, colc_here))
        return [
            pltpu.make_async_remote_copy(
                src_ref=src,
                dst_ref=dst,
                send_sem=hand_send.at[i],
                recv_sem=hand_sem.at[i],
                device_id=device(twin, 0, 0),
                device_id_type=MESH,
            )
            for i, (src, dst) in enumerate(pairs)
        ]

    def thin_copy(i):
        if i < 2:
            src, dst = rowc_here.at[i], rowc_in.at[i]
        else:
            src, dst = colc_here, colc_in.at[i - 2]
        return pltpu.make_async_remote_copy(
            src_ref=src,
            dst_ref=dst,
            send_sem=thin_send.at[i],
            recv_sem=thin_sem.at[i],
            device_id=device(grp, *AROUND[i]),
            device_id_type=MESH,
        )

    def whole_half(k):
        return pltpu.make_async_remote_copy(
            src_ref=stored.at[k],
            dst_ref=half_in.at[k],
            send_sem=half_send.at[k],
            recv_sem=half_sem.at[k],
            device_id=device(twin, 0, 0),
            device_id_type=MESH,
        )

    def sent(i, act):
        pl.when(on_grid(*AROUND[i]))(act)

    def received(i, act):
        dx, dy = AROUND[i]
        pl.when(on_grid(-dx, -dy))(act)

    def send_rims():
        for i, copy in enumerate(rim_copies()):
            sent(i, copy.start)

    def pack_rims():
        planes = own_planes()
        col_out[...] = pack_columns(planes)
        for i in range(8):
            row_out[0, i], row_out[1, i] = pack_rows(planes[2 * i], planes[2 * i + 1])

    stored_load = loads.pop(1)

    @pl.when(forward)
    def _():
        stored_load.wait()
        planes = half_planes(1, 6) + half_planes(0, 3)
        colc_out[...] = pack_columns(planes, RIM).astype(BF16)
        parts = [pack_thin_rows(planes[i : i + 4]) for i in range(0, len(planes), 4)]
        parts.append(parts[-1])
        for i in range(3):
            for side in range(2):
                rowc_out[side, i] = jnp.concatenate(
                    [parts[2 * i][side], parts[2 * i + 1][side]], axis=0
                ).astype(BF16)
        all_in()
        for copy in thin_copies():
            copy.start()
        whole_half(1).start()
        for load in loads:
            load.wait()
        pack_rims()
        whole_half(1).wait_send()
        whole_half(0).start()
        whole_half(0).wait_send()
        send_rims()

    @pl.when(jnp.logical_not(forward))
    def _():
        for load in loads:
            load.wait()
        pack_rims()
        all_in()
        send_rims()
        stored_load.wait()
        for k in range(HALF - 1, -1, -1):
            planes = half_planes(k, 6)
            colh_out[k] = pack_columns(planes).astype(BF16)
            for i in range(3):
                one = pack_rows(planes[4 * i], planes[4 * i + 1])
                two = pack_rows(planes[4 * i + 2], planes[4 * i + 3])
                for side in range(2):
                    rowh_out[side, k, i] = jnp.concatenate([one[side], two[side]], axis=0).astype(BF16)
            for i in range(8):
                sent(i, half_copy(k, i).start)

    row = iota((NZ * EX, TY), 0)
    depth = jnp.where(row >= EX, 1, 0)
    row = row - depth * EX
    x = gx * TX + jnp.where(row < TX + RIM, row, row - EX)
    sought_x = jnp.where((x >= 0) & (x < n_gx * TX), depth * (n_gx * TX) + x, -1)
    column = iota((TY, TY), 0)
    sought_y = gy * TY + column
    sought_high = sought_y[:8] + TY
    sought_low = sought_y[TY - 8 :] - TY
    listed = jnp.where(forward, source_cells[...], monitor_cells[...])
    listed_x = listed // (n_gy * TY)
    listed_y = listed % (n_gy * TY)

    def hits(found):
        return jnp.where(found, 1.0, 0.0)

    def wide(m, i, rows):
        return jnp.broadcast_to(m[i : i + 1], (rows, TY))

    entries = listed.shape[0]
    rows_hit = jnp.concatenate(
        [hits(wide(listed_x, i, NZ * EX) == sought_x) for i in range(entries)], axis=1
    ).astype(BF16)
    columns_hit = jnp.concatenate(
        [hits(wide(listed_y, i, TY) == sought_y) for i in range(entries)], axis=1
    ).astype(BF16)
    high_hit = jnp.concatenate([hits(wide(listed_y, i, 8) == sought_high) for i in range(entries)], axis=1)
    low_hit = jnp.concatenate([hits(wide(listed_y, i, 8) == sought_low) for i in range(entries)], axis=1)
    rim_hit = jnp.concatenate(
        [high_hit, jnp.zeros((TY - 16, entries * TY), F32), low_hit], axis=0
    ).astype(BF16)

    def tally(a, b):
        return lax.dot_general(a, b, (((1,), (1,)), ((), ())), preferred_element_type=F32)

    counts_ref[...] = jnp.concatenate([tally(rows_hit, columns_hit), tally(rows_hit, rim_hit)], axis=1)

    @pl.when(jnp.logical_not(forward))
    def _():
        lanes = owners.shape[1]
        pick = iota((TX, lanes), 1) == iota((TX, lanes), 0) * n_gy + gy
        coarse, fine = [], []
        for j in range(n_gx):
            line = jnp.broadcast_to(owners[pl.ds(lax.rem(gx - j + n_gx, n_gx), 1)], (TX, lanes))
            line = jnp.where(pick, line, 0)
            part = line // 64 * 64
            coarse.append(part.astype(F32))
            fine.append((line - part).astype(F32))
        rows = 4 * n_gy * SHARE
        ones = jnp.ones((rows, lanes), BF16)
        owner = tally(ones, jnp.concatenate(coarse, axis=0).astype(BF16))
        owner = owner + tally(ones, jnp.concatenate(fine, axis=0).astype(BF16))
        place = iota((rows, n_gx * TX), 0)
        share = place // SHARE
        lane = (grp + share // n_gy) % 4
        spot = (gy + share % n_gy) % n_gy
        wanted = ((lane * n_gx + gx) * n_gy + spot) * SHARE + place % SHARE
        chosen[...] = jnp.where(owner == wanted.astype(F32), 1.0, 0.0).astype(BF16)

    row = iota((EX, EY), 0)
    column = iota((EX, EY), 1)
    x = gx * TX + jnp.where(row < TX + RIM, row, row - EX)
    y = gy * TY + jnp.where(column < TY + TY // 2, column, column - EY)
    inside = (x >= 0) & (x < n_gx * TX) & (y >= 0) & (y < n_gy * TY)
    unit = jnp.where(inside, 1.0, 0.0)
    step = jnp.where(inside, DT, 0.0)
    counts = [counts_ref[z * EX : (z + 1) * EX] for z in range(NZ)]

    @pl.when(jnp.logical_not(forward))
    def _():
        for copy in thin_copies():
            copy.wait_recv()
        for i in range(8):
            sent(i, thin_copy(i).start)

    lane_in()
    for i, copy in enumerate(rim_copies()):
        received(i, copy.wait_recv)
    own = own_planes()
    columns = merge_columns(col_in[0], col_in[1], [corner_in[i] for i in range(4)])
    whole = []
    for i in range(8):
        for k, rows in enumerate(unpack_rows(row_in[0, i], row_in[1, i])):
            whole.append(extended(own[2 * i + k], rows, columns, 8 * (2 * i + k)))
    eps = [jnp.where(inside, v, 1.0) for v in whole[12:14]]
    chi = whole[14:16]
    whole = [jnp.where(inside, v, 0.0) for v in whole[:12]]
    first = [whole[2 * c : 2 * c + 2] for c in range(3)]
    second = [whole[2 * c : 2 * c + 2] for c in range(3, 6)]

    def state_copy():
        return pltpu.make_async_copy(state, fields_next, local_sem.at[0])

    def finish(electric, magnetic):
        for c in range(3):
            for z in range(NZ):
                state[c, z] = electric[c][z][:TX, :TY]
                state[3 + c, z] = magnetic[c][z][:TX, :TY]
        state_copy().start()

    def record_copy(n):
        return pltpu.make_async_remote_copy(
            src_ref=records.at[n],
            dst_ref=stored_next.at[n - HALF],
            send_sem=record_send.at[n - HALF],
            recv_sem=record_sem.at[n - HALF],
            device_id=device(twin, 0, 0),
            device_id_type=MESH,
        )

    def kept_copy(n):
        return pltpu.make_async_copy(records.at[n], stored_next.at[n], local_sem.at[1 + n])

    def square(v, z):
        return v[0][z] * v[0][z] + v[1][z] * v[1][z] + v[2][z] * v[2][z]

    @pl.when(forward)
    def _():
        electric, magnetic = first, second
        for n in range(STEPS):
            factor = [step / (eps[z] + chi[z] * square(electric, z)) for z in range(NZ)]
            turn = curl_up(electric)
            magnetic = [[magnetic[c][z] - step * turn[c][z] for z in range(NZ)] for c in range(3)]
            turn = curl_down(magnetic)
            for c in range(3):
                for z in range(NZ):
                    records[n, c, z] = electric[c][z][:TX, :TY].astype(BF16)
                    records[n, 3 + c, z] = turn[c][z][:TX, :TY].astype(BF16)
            (kept_copy if n < HALF else record_copy)(n).start()
            wave = source_wave[lax.rem(grp, 2), n]
            electric = [[electric[c][z] + factor[z] * turn[c][z] for z in range(NZ)] for c in range(3)]
            electric[0] = [electric[0][z] + wave * counts[z] for z in range(NZ)]
        finish(electric, magnetic)

    def corners_of(packed):
        return [packed[2][:8], packed[3][:8], packed[4][8:], packed[5][8:]]

    def vectors(planes):
        return [planes[2 * c : 2 * c + 2] for c in range(len(planes) // 2)]

    def late_snapshot(k):
        rows = []
        for i in range(3):
            after, before = rowh_in[0, k, i].astype(F32), rowh_in[1, k, i].astype(F32)
            rows.extend(unpack_rows(after[:8], before[:8]))
            rows.extend(unpack_rows(after[8:], before[8:]))
        packed = [colh_in[i, k].astype(F32) for i in range(6)]
        columns = merge_columns(packed[0], packed[1], corners_of(packed))
        return vectors([extended(v, rows[p], columns, 8 * p) for p, v in enumerate(half_planes(k, 6))])

    def early_snapshot(k, columns):
        planes = []
        for p in range(12):
            tile = half_in[k, p // NZ, p % NZ].astype(F32)
            place = p if k else 12 + p
            if place >= 18:
                planes.append(extended(tile, jnp.zeros((8, TY), F32), jnp.zeros((EX, TY), F32), 0))
                continue
            slot = slice(8 * (place // 4 % 2), 8 * (place // 4 % 2) + 8)
            after, before = [rowc_in[side, place // 8].astype(F32)[slot] for side in range(2)]
            planes.append(extended(tile, unpack_thin_rows(after, before, place % 4), columns, RIM * place))
        return vectors(planes)

    def tile_copy(j):
        return pltpu.make_async_remote_copy(
            src_ref=tiles.at[0],
            dst_ref=tiles.at[j],
            send_sem=tile_send.at[j],
            recv_sem=tile_sem.at[j],
            device_id=device(grp, j, 0),
            device_id_type=MESH,
        )

    def own_share():
        return pltpu.make_async_copy(shares.at[0], gathered.at[0], local_sem.at[3])

    def share_copy(i):
        return pltpu.make_async_remote_copy(
            src_ref=shares.at[i],
            dst_ref=gathered.at[i],
            send_sem=share_send.at[i],
            recv_sem=share_sem.at[i],
            device_id=device(lax.rem(grp + i // n_gy, 4), 0, lax.rem(i, n_gy)),
            device_id_type=MESH,
        )

    @pl.when(jnp.logical_not(forward))
    def _():
        electric, magnetic = first, second
        gradient = jnp.zeros((TX, TY), F32)
        for n in range(STEPS - 1, -1, -1):
            if n >= HALF:
                for i in range(8):
                    received(i, half_copy(n - HALF, i).wait_recv)
                snapshot = late_snapshot(n - HALF)
            else:
                whole_half(n).wait_recv()
                if n == HALF - 1:
                    for i in range(8):
                        received(i, thin_copy(i).wait_recv)
                    packed = [colc_in[i].astype(F32) for i in range(6)]
                    columns = merge_columns(packed[0], packed[1], corners_of(packed), RIM)
                snapshot = early_snapshot(n, columns)
            past, curled = snapshot[:3], snapshot[3:]
            factor = [DT / (eps[z] + chi[z] * square(past, z)) for z in range(NZ)]
            inner = [
                curled[0][z] * electric[0][z] + curled[1][z] * electric[1][z] + curled[2][z] * electric[2][z]
                for z in range(NZ)
            ]
            slope = [factor[z] * factor[z] * inner[z] for z in range(NZ)]
            gradient = gradient - (1.0 / DT) * (slope[0] + slope[1])[:TX, :TY]
            if n == 0:
                tiles[0] = gradient
                for j in far_first(n_gx)[:-1]:
                    tile_copy(j).start()
            turn = curl_up([[factor[z] * electric[c][z] for z in range(NZ)] for c in range(3)])
            magnetic = [[magnetic[c][z] + unit * turn[c][z] for z in range(NZ)] for c in range(3)]
            turn = curl_down(magnetic)
            weight = [counts[z] - (2.0 / DT) * chi[z] * slope[z] for z in range(NZ)]
            electric = [
                [electric[c][z] + weight[z] * past[c][z] - step * turn[c][z] for z in range(NZ)] for c in range(3)
            ]
        finish(electric, magnetic)

    def each(low, high, act):
        def body(i, carry):
            act(i)
            return carry

        lax.fori_loop(low, high, body, 0)

    @pl.when(jnp.logical_not(forward))
    def _():
        for j in range(1, n_gx):
            tile_copy(j).wait_recv()
        rest = jnp.concatenate([tiles[j] for j in range(n_gx)], axis=0)
        total = jnp.zeros((4 * n_gy * SHARE, TY), F32)
        for _ in range(3):
            part = rest.astype(BF16)
            total = total + jnp.dot(chosen[...], part, preferred_element_type=F32)
            rest = rest - part.astype(F32)
        for i in range(4 * n_gy):
            shares[i] = total[SHARE * i : SHARE * (i + 1)]
        own_share().start()
        pl.semaphore_wait(third_round, len(third))
        for j in far_first(n_gy):
            for lane in (2, 1, 3, 0):
                if lane + j:
                    share_copy(lane * n_gy + j).start()

    @pl.when(forward)
    def _():
        pl.semaphore_wait(third_round, len(third))

    for lane in (2, 3):
        start = lax.rem(grp + 4 - lane, 4) * n_gy
        each(start + jnp.where(start == 0, 1, 0), start + n_gy, lambda i: share_copy(i).wait_recv())

    for i, copy in enumerate(rim_copies()):
        sent(i, copy.wait_send)
    state_copy().wait()

    @pl.when(forward)
    def _():
        for copy in thin_copies():
            copy.wait_send()
        for n in range(STEPS):
            if n < HALF:
                kept_copy(n).wait()
            else:
                record_copy(n).wait_send()

    @pl.when(jnp.logical_not(forward))
    def _():
        for k in range(HALF):
            for i in range(8):
                sent(i, half_copy(k, i).wait_send)
        for i in range(8):
            sent(i, thin_copy(i).wait_send)
        for n in range(HALF, STEPS):
            record_copy(n).wait_recv()
        for j in range(1, n_gx):
            tile_copy(j).wait_send()
        for i in range(1, 4 * n_gy):
            share_copy(i).wait_send()
        own_share().wait()


def store(n_gy, fields, stored, gathered, fields_next, stored_next, design_grad):
    fields_next[...] = fields[...]
    stored_next[...] = stored[...]
    total = jnp.zeros((SHARE, TY), F32)
    for lane in (2, 3):
        start = lax.rem(lax.axis_index("grp") + 4 - lane, 4) * n_gy
        for j in range(n_gy):
            total = total + gathered[start + j]
    design_grad[...] = total


def local(fields, stored, material, design, mat_eps, mat_chi, source_wave, source_cells, monitor_cells, owners):
    n_gx, n_gy = lax.axis_size("gx"), lax.axis_size("gy")
    vmem = pl.BlockSpec(memory_space=pltpu.VMEM)
    hbm = pl.BlockSpec(memory_space=pltpu.HBM)
    dma = pltpu.SemaphoreType.DMA
    cells = source_cells.shape[0]
    outs = pl.pallas_call(
        functools.partial(kernel, n_gx, n_gy),
        out_shape=(
            jax.ShapeDtypeStruct((6, NZ, TX, TY), F32),
            jax.ShapeDtypeStruct((HALF, 6, NZ, TX, TY), BF16),
            jax.ShapeDtypeStruct((4 * n_gy, SHARE, TY), F32),
        ),
        in_specs=[hbm] * 10,
        out_specs=(hbm, hbm, hbm),
        scratch_shapes=[
            pltpu.VMEM((6, NZ, TX, TY), F32),
            pltpu.VMEM((HALF, 6, NZ, TX, TY), BF16),
            pltpu.VMEM((NZ, TX, TY), jnp.int32),
            pltpu.VMEM((TX, TY), F32),
            pltpu.SMEM((4,), F32),
            pltpu.SMEM((4,), F32),
            pltpu.SMEM((2, STEPS), F32),
            pltpu.VMEM((cells // TY, TY), jnp.int32),
            pltpu.VMEM((cells // TY, TY), jnp.int32),
            pltpu.VMEM((n_gx, TX * n_gy), jnp.int32),
            pltpu.VMEM((TX, TY), F32),
            pltpu.VMEM((HALF, TX, TY), BF16),
            pltpu.VMEM((2, 8, 8, TY), F32),
            pltpu.VMEM((2, HALF, 3, TX, TY), BF16),
            pltpu.VMEM((2, TX, TY), F32),
            pltpu.VMEM((4, 8, TY), F32),
            pltpu.VMEM((2, 8, 8, TY), F32),
            pltpu.VMEM((6, HALF, TX, TY), BF16),
            pltpu.VMEM((2, HALF, 3, TX, TY), BF16),
            pltpu.VMEM((HALF, 6, NZ, TX, TY), BF16),
            pltpu.VMEM((2, 3, TX, TY), BF16),
            pltpu.VMEM((2, 3, TX, TY), BF16),
            pltpu.VMEM((TX, TY), BF16),
            pltpu.VMEM((6, TX, TY), BF16),
            pltpu.VMEM((2, 3, TX, TY), BF16),
            pltpu.VMEM((TX, TY), BF16),
            pltpu.VMEM((STEPS, 6, NZ, TX, TY), BF16),
            pltpu.VMEM((6, NZ, TX, TY), F32),
            pltpu.VMEM((NZ * EX, EY), F32),
            pltpu.VMEM((4 * n_gy * SHARE, n_gx * TX), BF16),
            pltpu.VMEM((n_gx, TX, TY), F32),
            pltpu.VMEM((4 * n_gy, SHARE, TY), F32),
            dma((8,)),
            dma((HALF, 8)),
            dma((HALF,)),
            dma((8,)),
            dma((HALF, 8)),
            dma((HALF,)),
            dma((8,)),
            dma((8,)),
            dma((2,)),
            dma((2,)),
            pltpu.SemaphoreType.REGULAR,
            pltpu.SemaphoreType.REGULAR,
            dma((HALF,)),
            dma((HALF,)),
            dma((n_gx,)),
            dma((n_gx,)),
            dma((4 * n_gy,)),
            dma((4 * n_gy,)),
            dma((4,)),
            dma((10,)),
        ],
        compiler_params=pltpu.CompilerParams(
            collective_id=0, has_side_effects=True, vmem_limit_bytes=56 * 1024 * 1024
        ),
        name="interval",
    )(
        fields[0],
        stored[0],
        material,
        design,
        mat_eps,
        mat_chi,
        source_wave,
        source_cells.reshape(cells // TY, TY),
        monitor_cells.reshape(cells // TY, TY),
        owners.reshape(n_gx, TX * n_gy),
    )
    fields_next, stored_next, design_grad = pl.pallas_call(
        functools.partial(store, n_gy),
        out_shape=(
            jax.ShapeDtypeStruct(outs[0].shape, F32),
            jax.ShapeDtypeStruct(outs[1].shape, BF16),
            jax.ShapeDtypeStruct((SHARE, TY), F32),
        ),
        in_specs=[vmem] * 3,
        out_specs=(vmem,) * 3,
        compiler_params=pltpu.CompilerParams(vmem_limit_bytes=56 * 1024 * 1024),
        name="store",
    )(*outs)
    return fields_next[None], stored_next[None], design_grad


def solution(mesh):
    in_specs = (
        P("grp", None, None, "gx", "gy"),
        P("grp", None, None, None, "gx", "gy"),
        P(None, "gx", "gy"),
        P("gx", "gy"),
        P(),
        P(),
        P(),
        P(),
        P(),
        P(),
    )
    out_specs = (
        P("grp", None, None, "gx", "gy"),
        P("grp", None, None, None, "gx", "gy"),
        P(("grp", "gx", "gy"), None),
    )
    return jax.shard_map(local, mesh=mesh, in_specs=in_specs, out_specs=out_specs, check_vma=False)
```

```python
import functools
import math

import jax
import jax.numpy as jnp
from jax import lax
from jax.experimental import pallas as pl
from jax.experimental.pallas import tpu as pltpu
from jax.sharding import PartitionSpec as P

MESH = pl.DeviceIdType.MESH
F32 = jnp.float32
BF16 = jnp.bfloat16

NZ = 2
TX = 16
TY = 128
RIM = 4
EX = TX + 2 * RIM
EY = 2 * TY
STEPS = 4
HALF = 2
DT = 0.5
SHARE = 4

AROUND = ((-1, 0), (1, 0), (0, -1), (0, 1), (-1, -1), (-1, 1), (1, -1), (1, 1))


def far_first(length):
    return sorted(range(length), key=lambda j: -min(j, length - j))


def iota(shape, axis):
    return lax.broadcasted_iota(jnp.int32, shape, axis)


def pack_columns(planes, slot=8):
    column = iota((TX, TY), 1)
    window = ((column + slot // 2) // slot) % (TY // slot)
    packed = planes[0]
    for p in range(1, len(planes)):
        packed = jnp.where(window == p, pltpu.roll(planes[p], slot * p, 1), packed)
    return packed


def pack_rows(one, two):
    low = iota((8, TY), 0) < RIM
    first = jnp.where(low, one[:8], one[8:])
    second = pltpu.roll(jnp.where(low, two[:8], two[8:]), RIM, 0)
    return jnp.where(low, first, second), jnp.where(low, second, first)


def unpack_rows(after, before):
    low = iota((8, TY), 0) < RIM
    return jnp.where(low, after, before), pltpu.roll(jnp.where(low, before, after), RIM, 0)


def pack_thin_rows(planes):
    row = iota((8, TY), 0)
    both = [jnp.where(row < RIM, p[:8], p[8:]) for p in planes]
    before = after = both[0]
    for q in range(1, len(planes)):
        turned = pltpu.roll(both[q], 2 * q, 0)
        before = jnp.where(row // 2 == q, turned, before)
        after = jnp.where((row // 2 + 1) % 4 == q, turned, after)
    return before, after


def unpack_thin_rows(after, before, q):
    rows = jnp.where(iota((8, TY), 0) // 2 == q, after, before)
    return rows if q == 0 else pltpu.roll(rows, 8 - 2 * q, 0)


def merge_columns(right, left, corners, slot=8):
    side = iota((TX, TY), 1) % slot < slot // 2
    beside = jnp.where(side, right, left)
    side = side[:8]
    from_after_right, from_after_left, from_before_right, from_before_left = corners
    low = iota((8, TY), 0) < RIM
    after = jnp.where(side, from_after_right, from_after_left)
    before = jnp.where(side, from_before_right, from_before_left)
    return jnp.concatenate([beside, jnp.where(low, after, before)], axis=0)


def extended(tile, rows, columns, shift):
    body = jnp.concatenate([tile, rows], axis=0)
    beside = columns if shift == 0 else pltpu.roll(columns, TY - shift, 1)
    return jnp.concatenate([body, beside], axis=1)


def next_x(v):
    return pltpu.roll(v, EX - 1, 0) - v


def next_y(v):
    return pltpu.roll(v, EY - 1, 1) - v


def next_z(v):
    return [v[1] - v[0], -v[1]]


def last_x(v):
    return v - pltpu.roll(v, 1, 0)


def last_y(v):
    return v - pltpu.roll(v, 1, 1)


def last_z(v):
    return [v[0], v[1] - v[0]]


def curl(v, along_x, along_y, along_z):
    z_of_y, z_of_x = along_z(v[1]), along_z(v[0])
    return (
        [along_y(v[2][z]) - z_of_y[z] for z in range(NZ)],
        [z_of_x[z] - along_x(v[2][z]) for z in range(NZ)],
        [along_x(v[1][z]) - along_y(v[0][z]) for z in range(NZ)],
    )


def curl_up(v):
    return curl(v, next_x, next_y, next_z)


def curl_down(v):
    return curl(v, last_x, last_y, last_z)


def kernel(
    n_gx,
    n_gy,
    fields_in,
    stored_in,
    material_in,
    design_in,
    mat_eps_in,
    mat_chi_in,
    source_wave_in,
    source_cells_in,
    monitor_cells_in,
    owners_in,
    fields_next,
    stored_next,
    gathered,
    fields,
    stored,
    material,
    design,
    mat_eps,
    mat_chi,
    source_wave,
    source_cells,
    monitor_cells,
    owners,
    col_out,
    colh_out,
    row_out,
    rowh_out,
    col_in,
    corner_in,
    row_in,
    colh_in,
    rowh_in,
    half_in,
    rowc_out,
    rowc_in,
    colc_out,
    colc_in,
    rowc_here,
    colc_here,
    records,
    state,
    counts_ref,
    chosen,
    tiles,
    shares,
    own_sem,
    ownh_sem,
    half_send,
    in_sem,
    inh_sem,
    half_sem,
    thin_send,
    thin_sem,
    hand_send,
    hand_sem,
    second_round,
    third_round,
    fourth_round,
    go,
    record_send,
    record_sem,
    tile_send,
    tile_sem,
    share_send,
    share_sem,
    local_sem,
    load_sem,
):
    grp, gx, gy = lax.axis_index("grp"), lax.axis_index("gx"), lax.axis_index("gy")
    forward = grp < 2
    twin = jnp.where(forward, grp + 2, grp - 2)

    def device(lane, dx, dy):
        return {
            "grp": lane,
            "gx": lax.rem(gx + dx + n_gx, n_gx),
            "gy": lax.rem(gy + dy + n_gy, n_gy),
        }

    barrier = pltpu.get_barrier_semaphore()
    adjoint = jnp.logical_not(forward)
    side = math.isqrt(n_gx)

    def on_grid(dx, dy):
        x, y = gx + dx, gy + dy
        return (x >= 0) & (x < n_gx) & (y >= 0) & (y < n_gy)

    def signal(semaphore, target):
        pl.semaphore_signal(semaphore, inc=1, device_id=target, device_id_type=MESH)

    def in_row(d):
        return {"grp": grp, "gx": gx - gx % side + (gx + d) % side, "gy": gy}

    def in_pair(d, other):
        return {"grp": grp, "gx": gx, "gy": lax.rem(gy - gy % 2 + (gy + other) % 2 + 2 * d + n_gy, n_gy)}

    beside = [(dx, dy) for dx, dy in AROUND[::-1] if dx]
    neighbours = sum(jnp.where(on_grid(dx, dy), 1, 0) for dx, dy in beside)
    pairs = [in_pair(d, other) for d in (-1, 1) for other in (0, 1)] + [in_pair(0, 1)]
    rows = [in_row(d) for d in range(1, side)]
    lines = [device(grp, side * d, 0) for d in range(1, n_gx // side)]
    other_lane = device(5 - grp, 0, 0)

    def signal_all(semaphore, targets):
        for dx, dy in beside:
            pl.when(on_grid(dx, dy))(functools.partial(signal, semaphore, device(grp, dx, dy)))
        for target in targets:
            signal(semaphore, target)

    signal(barrier, device(twin, 0, 0))

    @pl.when(adjoint)
    def _():
        signal_all(barrier, pairs + rows + lines + [other_lane])

    def all_in():
        first_round = neighbours + len(pairs) + len(rows) + len(lines) + 2
        pl.semaphore_wait(barrier, jnp.where(forward, 1, first_round))

    def begin_second():
        signal_all(second_round, pairs + rows)

    def end_second():
        pl.semaphore_wait(second_round, neighbours + len(pairs) + len(rows))
        signal(go, device(twin, 0, 0))
        for d in (-1, 1):
            signal(third_round, in_pair(d, 0))

    def end_third():
        pl.semaphore_wait(third_round, 2)
        signal(fourth_round, other_lane)

    held = (fields, stored, material, design, mat_eps, mat_chi, source_wave, source_cells, monitor_cells, owners)
    given = (
        fields_in,
        stored_in,
        material_in,
        design_in,
        mat_eps_in,
        mat_chi_in,
        source_wave_in,
        source_cells_in,
        monitor_cells_in,
        owners_in,
    )
    loads = [pltpu.make_async_copy(a, b, load_sem.at[i]) for i, (a, b) in enumerate(zip(given, held))]
    for load in loads:
        load.start()

    for i, (dx, dy) in enumerate(AROUND):
        x, y = gx - dx, gy - dy

        @pl.when((x < 0) | (x >= n_gx) | (y < 0) | (y >= n_gy))
        def _():
            if i < 2:
                row_in[i] = jnp.zeros(row_in.shape[1:], F32)
                rowh_in[i] = jnp.zeros(rowh_in.shape[1:], BF16)
                rowc_in[i] = jnp.zeros(rowc_in.shape[1:], BF16)
                return
            if i < 4:
                col_in[i - 2] = jnp.zeros(col_in.shape[1:], F32)
            else:
                corner_in[i - 4] = jnp.zeros(corner_in.shape[1:], F32)
            colh_in[i - 2] = jnp.zeros(colh_in.shape[1:], BF16)
            colc_in[i - 2] = jnp.zeros(colc_in.shape[1:], BF16)

    def lookup(index, entries):
        value = jnp.zeros(index.shape, F32)
        for k in range(4):
            value = jnp.where(index == k, entries[k], value)
        return value

    def own_planes():
        kinds = [material[z] for z in range(NZ)]
        eps = [lookup(kinds[z], mat_eps) + design[...] for z in range(NZ)]
        chi = [lookup(kinds[z], mat_chi) for z in range(NZ)]
        return [fields[c, z] for c in range(6) for z in range(NZ)] + eps + chi

    def half_planes(k, components):
        return [stored[k, c, z].astype(F32) for c in range(components) for z in range(NZ)]

    def row_copy(i):
        return pltpu.make_async_remote_copy(
            src_ref=row_out.at[i],
            dst_ref=row_in.at[i],
            send_sem=own_sem.at[i],
            recv_sem=in_sem.at[i],
            device_id=device(grp, *AROUND[i]),
            device_id_type=MESH,
        )

    def col_copy(i):
        return pltpu.make_async_remote_copy(
            src_ref=col_out,
            dst_ref=col_in.at[i - 2],
            send_sem=own_sem.at[i],
            recv_sem=in_sem.at[i],
            device_id=device(grp, *AROUND[i]),
            device_id_type=MESH,
        )

    def corner_copy(i):
        start = 0 if AROUND[i][0] < 0 else 8
        return pltpu.make_async_remote_copy(
            src_ref=col_out.at[pl.ds(start, 8)],
            dst_ref=corner_in.at[i - 4],
            send_sem=own_sem.at[i],
            recv_sem=in_sem.at[i],
            device_id=device(grp, *AROUND[i]),
            device_id_type=MESH,
        )

    def rim_copies():
        return [row_copy(0), row_copy(1), col_copy(2), col_copy(3)] + [corner_copy(i) for i in range(4, 8)]

    def half_copy(k, i):
        if i < 2:
            src, dst = rowh_out.at[i, k], rowh_in.at[i, k]
        else:
            src, dst = colh_out.at[k], colh_in.at[i - 2, k]
        return pltpu.make_async_remote_copy(
            src_ref=src,
            dst_ref=dst,
            send_sem=ownh_sem.at[k, i],
            recv_sem=inh_sem.at[k, i],
            device_id=device(grp, *AROUND[i]),
            device_id_type=MESH,
        )

    def thin_copies():
        pairs = ((rowc_out, rowc_here), (colc_out, colc_here))
        return [
            pltpu.make_async_remote_copy(
                src_ref=src,
                dst_ref=dst,
                send_sem=hand_send.at[i],
                recv_sem=hand_sem.at[i],
                device_id=device(twin, 0, 0),
                device_id_type=MESH,
            )
            for i, (src, dst) in enumerate(pairs)
        ]

    def thin_copy(i):
        if i < 2:
            src, dst = rowc_here.at[i], rowc_in.at[i]
        else:
            src, dst = colc_here, colc_in.at[i - 2]
        return pltpu.make_async_remote_copy(
            src_ref=src,
            dst_ref=dst,
            send_sem=thin_send.at[i],
            recv_sem=thin_sem.at[i],
            device_id=device(grp, *AROUND[i]),
            device_id_type=MESH,
        )

    def whole_half(k):
        return pltpu.make_async_remote_copy(
            src_ref=stored.at[k],
            dst_ref=half_in.at[k],
            send_sem=half_send.at[k],
            recv_sem=half_sem.at[k],
            device_id=device(twin, 0, 0),
            device_id_type=MESH,
        )

    def sent(i, act):
        pl.when(on_grid(*AROUND[i]))(act)

    def received(i, act):
        dx, dy = AROUND[i]
        pl.when(on_grid(-dx, -dy))(act)

    def send_rims():
        for i, copy in enumerate(rim_copies()):
            sent(i, copy.start)

    def pack_rims():
        planes = own_planes()
        col_out[...] = pack_columns(planes)
        for i in range(8):
            row_out[0, i], row_out[1, i] = pack_rows(planes[2 * i], planes[2 * i + 1])

    stored_load = loads.pop(1)

    @pl.when(forward)
    def _():
        stored_load.wait()
        planes = half_planes(1, 6) + half_planes(0, 3)
        colc_out[...] = pack_columns(planes, RIM).astype(BF16)
        parts = [pack_thin_rows(planes[i : i + 4]) for i in range(0, len(planes), 4)]
        parts.append(parts[-1])
        for i in range(3):
            for side in range(2):
                rowc_out[side, i] = jnp.concatenate(
                    [parts[2 * i][side], parts[2 * i + 1][side]], axis=0
                ).astype(BF16)
        all_in()
        for copy in thin_copies():
            copy.start()
        whole_half(1).start()
        for load in loads:
            load.wait()
        pack_rims()
        whole_half(1).wait_send()
        whole_half(0).start()

    @pl.when(adjoint)
    def _():
        for load in loads:
            load.wait()
        pack_rims()
        all_in()
        send_rims()
        begin_second()
        stored_load.wait()
        for k in range(HALF - 1, -1, -1):
            planes = half_planes(k, 6)
            colh_out[k] = pack_columns(planes).astype(BF16)
            for i in range(3):
                one = pack_rows(planes[4 * i], planes[4 * i + 1])
                two = pack_rows(planes[4 * i + 2], planes[4 * i + 3])
                for side in range(2):
                    rowh_out[side, k, i] = jnp.concatenate([one[side], two[side]], axis=0).astype(BF16)
            for i in range(8):
                sent(i, half_copy(k, i).start)

    row = iota((NZ * EX, TY), 0)
    depth = jnp.where(row >= EX, 1, 0)
    row = row - depth * EX
    x = gx * TX + jnp.where(row < TX + RIM, row, row - EX)
    sought_x = jnp.where((x >= 0) & (x < n_gx * TX), depth * (n_gx * TX) + x, -1)
    column = iota((TY, TY), 0)
    sought_y = gy * TY + column
    sought_high = sought_y[:8] + TY
    sought_low = sought_y[TY - 8 :] - TY
    listed = jnp.where(forward, source_cells[...], monitor_cells[...])
    listed_x = listed // (n_gy * TY)
    listed_y = listed % (n_gy * TY)

    def hits(found):
        return jnp.where(found, 1.0, 0.0)

    def wide(m, i, rows):
        return jnp.broadcast_to(m[i : i + 1], (rows, TY))

    entries = listed.shape[0]
    rows_hit = jnp.concatenate(
        [hits(wide(listed_x, i, NZ * EX) == sought_x) for i in range(entries)], axis=1
    ).astype(BF16)
    columns_hit = jnp.concatenate(
        [hits(wide(listed_y, i, TY) == sought_y) for i in range(entries)], axis=1
    ).astype(BF16)
    high_hit = jnp.concatenate([hits(wide(listed_y, i, 8) == sought_high) for i in range(entries)], axis=1)
    low_hit = jnp.concatenate([hits(wide(listed_y, i, 8) == sought_low) for i in range(entries)], axis=1)
    rim_hit = jnp.concatenate(
        [high_hit, jnp.zeros((TY - 16, entries * TY), F32), low_hit], axis=0
    ).astype(BF16)

    def tally(a, b):
        return lax.dot_general(a, b, (((1,), (1,)), ((), ())), preferred_element_type=F32)

    counts_ref[...] = jnp.concatenate([tally(rows_hit, columns_hit), tally(rows_hit, rim_hit)], axis=1)

    @pl.when(adjoint)
    def _():
        lanes = owners.shape[1]
        pick = iota((TX, lanes), 1) == iota((TX, lanes), 0) * n_gy + gy
        coarse, fine = [], []
        for j in range(n_gx):
            line = jnp.broadcast_to(owners[pl.ds(lax.rem(gx - j + n_gx, n_gx), 1)], (TX, lanes))
            line = jnp.where(pick, line, 0)
            part = line // 64 * 64
            coarse.append(part.astype(F32))
            fine.append((line - part).astype(F32))
        rows = 4 * n_gy * SHARE
        ones = jnp.ones((rows, lanes), BF16)
        owner = tally(ones, jnp.concatenate(coarse, axis=0).astype(BF16))
        owner = owner + tally(ones, jnp.concatenate(fine, axis=0).astype(BF16))
        place = iota((rows, n_gx * TX), 0)
        share = place // SHARE
        lane = (grp + share // n_gy) % 4
        spot = (gy + share % n_gy) % n_gy
        wanted = ((lane * n_gx + gx) * n_gy + spot) * SHARE + place % SHARE
        chosen[...] = jnp.where(owner == wanted.astype(F32), 1.0, 0.0).astype(BF16)

    row = iota((EX, EY), 0)
    column = iota((EX, EY), 1)
    x = gx * TX + jnp.where(row < TX + RIM, row, row - EX)
    y = gy * TY + jnp.where(column < TY + TY // 2, column, column - EY)
    inside = (x >= 0) & (x < n_gx * TX) & (y >= 0) & (y < n_gy * TY)
    unit = jnp.where(inside, 1.0, 0.0)
    step = jnp.where(inside, DT, 0.0)
    counts = [counts_ref[z * EX : (z + 1) * EX] for z in range(NZ)]

    @pl.when(adjoint)
    def _():
        for copy in thin_copies():
            copy.wait_recv()
        for i in range(8):
            sent(i, thin_copy(i).start)
        end_second()

    @pl.when(forward)
    def _():
        pl.semaphore_wait(go, 1)
        send_rims()

    for i, copy in enumerate(rim_copies()):
        received(i, copy.wait_recv)
    own = own_planes()
    columns = merge_columns(col_in[0], col_in[1], [corner_in[i] for i in range(4)])
    whole = []
    for i in range(8):
        for k, rows in enumerate(unpack_rows(row_in[0, i], row_in[1, i])):
            whole.append(extended(own[2 * i + k], rows, columns, 8 * (2 * i + k)))
    eps = [jnp.where(inside, v, 1.0) for v in whole[12:14]]
    chi = whole[14:16]
    whole = [jnp.where(inside, v, 0.0) for v in whole[:12]]
    first = [whole[2 * c : 2 * c + 2] for c in range(3)]
    second = [whole[2 * c : 2 * c + 2] for c in range(3, 6)]

    def state_copy():
        return pltpu.make_async_copy(state, fields_next, local_sem.at[0])

    def finish(electric, magnetic):
        for c in range(3):
            for z in range(NZ):
                state[c, z] = electric[c][z][:TX, :TY]
                state[3 + c, z] = magnetic[c][z][:TX, :TY]
        state_copy().start()

    def record_copy(n):
        return pltpu.make_async_remote_copy(
            src_ref=records.at[n],
            dst_ref=stored_next.at[n - HALF],
            send_sem=record_send.at[n - HALF],
            recv_sem=record_sem.at[n - HALF],
            device_id=device(twin, 0, 0),
            device_id_type=MESH,
        )

    def kept_copy(n):
        return pltpu.make_async_copy(records.at[n], stored_next.at[n], local_sem.at[1 + n])

    def square(v, z):
        return v[0][z] * v[0][z] + v[1][z] * v[1][z] + v[2][z] * v[2][z]

    @pl.when(forward)
    def _():
        electric, magnetic = first, second
        for n in range(STEPS):
            factor = [step / (eps[z] + chi[z] * square(electric, z)) for z in range(NZ)]
            turn = curl_up(electric)
            magnetic = [[magnetic[c][z] - step * turn[c][z] for z in range(NZ)] for c in range(3)]
            turn = curl_down(magnetic)
            for c in range(3):
                for z in range(NZ):
                    records[n, c, z] = electric[c][z][:TX, :TY].astype(BF16)
                    records[n, 3 + c, z] = turn[c][z][:TX, :TY].astype(BF16)
            (kept_copy if n < HALF else record_copy)(n).start()
            wave = source_wave[lax.rem(grp, 2), n]
            electric = [[electric[c][z] + factor[z] * turn[c][z] for z in range(NZ)] for c in range(3)]
            electric[0] = [electric[0][z] + wave * counts[z] for z in range(NZ)]
        finish(electric, magnetic)

    def corners_of(packed):
        return [packed[2][:8], packed[3][:8], packed[4][8:], packed[5][8:]]

    def vectors(planes):
        return [planes[2 * c : 2 * c + 2] for c in range(len(planes) // 2)]

    def late_snapshot(k):
        rows = []
        for i in range(3):
            after, before = rowh_in[0, k, i].astype(F32), rowh_in[1, k, i].astype(F32)
            rows.extend(unpack_rows(after[:8], before[:8]))
            rows.extend(unpack_rows(after[8:], before[8:]))
        packed = [colh_in[i, k].astype(F32) for i in range(6)]
        columns = merge_columns(packed[0], packed[1], corners_of(packed))
        return vectors([extended(v, rows[p], columns, 8 * p) for p, v in enumerate(half_planes(k, 6))])

    def early_snapshot(k, columns):
        planes = []
        for p in range(12):
            tile = half_in[k, p // NZ, p % NZ].astype(F32)
            place = p if k else 12 + p
            if place >= 18:
                planes.append(extended(tile, jnp.zeros((8, TY), F32), jnp.zeros((EX, TY), F32), 0))
                continue
            slot = slice(8 * (place // 4 % 2), 8 * (place // 4 % 2) + 8)
            after, before = [rowc_in[side, place // 8].astype(F32)[slot] for side in range(2)]
            planes.append(extended(tile, unpack_thin_rows(after, before, place % 4), columns, RIM * place))
        return vectors(planes)

    def tile_copy(j):
        return pltpu.make_async_remote_copy(
            src_ref=tiles.at[0],
            dst_ref=tiles.at[j],
            send_sem=tile_send.at[j],
            recv_sem=tile_sem.at[j],
            device_id=device(grp, j, 0),
            device_id_type=MESH,
        )

    def own_share():
        return pltpu.make_async_copy(shares.at[0], gathered.at[0], local_sem.at[3])

    def share_copy(i):
        return pltpu.make_async_remote_copy(
            src_ref=shares.at[i],
            dst_ref=gathered.at[i],
            send_sem=share_send.at[i],
            recv_sem=share_sem.at[i],
            device_id=device(lax.rem(grp + i // n_gy, 4), 0, lax.rem(i, n_gy)),
            device_id_type=MESH,
        )

    @pl.when(adjoint)
    def _():
        electric, magnetic = first, second
        gradient = jnp.zeros((TX, TY), F32)
        for n in range(STEPS - 1, -1, -1):
            if n >= HALF:
                for i in range(8):
                    received(i, half_copy(n - HALF, i).wait_recv)
                snapshot = late_snapshot(n - HALF)
            else:
                whole_half(n).wait_recv()
                if n == HALF - 1:
                    for i in range(8):
                        received(i, thin_copy(i).wait_recv)
                    packed = [colc_in[i].astype(F32) for i in range(6)]
                    columns = merge_columns(packed[0], packed[1], corners_of(packed), RIM)
                snapshot = early_snapshot(n, columns)
            past, curled = snapshot[:3], snapshot[3:]
            factor = [DT / (eps[z] + chi[z] * square(past, z)) for z in range(NZ)]
            inner = [
                curled[0][z] * electric[0][z] + curled[1][z] * electric[1][z] + curled[2][z] * electric[2][z]
                for z in range(NZ)
            ]
            slope = [factor[z] * factor[z] * inner[z] for z in range(NZ)]
            gradient = gradient - (1.0 / DT) * (slope[0] + slope[1])[:TX, :TY]
            if n == 0:
                tiles[0] = gradient
                for j in far_first(n_gx)[:-1]:
                    tile_copy(j).start()
            turn = curl_up([[factor[z] * electric[c][z] for z in range(NZ)] for c in range(3)])
            magnetic = [[magnetic[c][z] + unit * turn[c][z] for z in range(NZ)] for c in range(3)]
            turn = curl_down(magnetic)
            weight = [counts[z] - (2.0 / DT) * chi[z] * slope[z] for z in range(NZ)]
            electric = [
                [electric[c][z] + weight[z] * past[c][z] - step * turn[c][z] for z in range(NZ)] for c in range(3)
            ]
        finish(electric, magnetic)

    def each(low, high, act):
        def body(i, carry):
            act(i)
            return carry

        lax.fori_loop(low, high, body, 0)

    @pl.when(adjoint)
    def _():
        end_third()
        for j in range(1, n_gx):
            tile_copy(j).wait_recv()
        rest = jnp.concatenate([tiles[j] for j in range(n_gx)], axis=0)
        total = jnp.zeros((4 * n_gy * SHARE, TY), F32)
        for _ in range(3):
            part = rest.astype(BF16)
            total = total + jnp.dot(chosen[...], part, preferred_element_type=F32)
            rest = rest - part.astype(F32)
        for i in range(4 * n_gy):
            shares[i] = total[SHARE * i : SHARE * (i + 1)]
        own_share().start()
        pl.semaphore_wait(fourth_round, 1)
        for j in far_first(n_gy):
            for lane in (2, 1, 3, 0):
                if lane + j:
                    share_copy(lane * n_gy + j).start()

    for lane in (2, 3):
        start = lax.rem(grp + 4 - lane, 4) * n_gy
        each(start + jnp.where(start == 0, 1, 0), start + n_gy, lambda i: share_copy(i).wait_recv())

    for i, copy in enumerate(rim_copies()):
        sent(i, copy.wait_send)
    state_copy().wait()

    @pl.when(forward)
    def _():
        for copy in thin_copies():
            copy.wait_send()
        for k in range(HALF - 1):
            whole_half(k).wait_send()
        for n in range(STEPS):
            if n < HALF:
                kept_copy(n).wait()
            else:
                record_copy(n).wait_send()

    @pl.when(adjoint)
    def _():
        for k in range(HALF):
            for i in range(8):
                sent(i, half_copy(k, i).wait_send)
        for i in range(8):
            sent(i, thin_copy(i).wait_send)
        for n in range(HALF, STEPS):
            record_copy(n).wait_recv()
        for j in range(1, n_gx):
            tile_copy(j).wait_send()
        for i in range(1, 4 * n_gy):
            share_copy(i).wait_send()
        own_share().wait()


def store(n_gy, fields, stored, gathered, fields_next, stored_next, design_grad):
    fields_next[...] = fields[...]
    stored_next[...] = stored[...]
    total = jnp.zeros((SHARE, TY), F32)
    for lane in (2, 3):
        start = lax.rem(lax.axis_index("grp") + 4 - lane, 4) * n_gy
        for j in range(n_gy):
            total = total + gathered[start + j]
    design_grad[...] = total


def local(fields, stored, material, design, mat_eps, mat_chi, source_wave, source_cells, monitor_cells, owners):
    n_gx, n_gy = lax.axis_size("gx"), lax.axis_size("gy")
    vmem = pl.BlockSpec(memory_space=pltpu.VMEM)
    hbm = pl.BlockSpec(memory_space=pltpu.HBM)
    dma = pltpu.SemaphoreType.DMA
    cells = source_cells.shape[0]
    outs = pl.pallas_call(
        functools.partial(kernel, n_gx, n_gy),
        out_shape=(
            jax.ShapeDtypeStruct((6, NZ, TX, TY), F32),
            jax.ShapeDtypeStruct((HALF, 6, NZ, TX, TY), BF16),
            jax.ShapeDtypeStruct((4 * n_gy, SHARE, TY), F32),
        ),
        in_specs=[hbm] * 10,
        out_specs=(hbm, hbm, hbm),
        scratch_shapes=[
            pltpu.VMEM((6, NZ, TX, TY), F32),
            pltpu.VMEM((HALF, 6, NZ, TX, TY), BF16),
            pltpu.VMEM((NZ, TX, TY), jnp.int32),
            pltpu.VMEM((TX, TY), F32),
            pltpu.SMEM((4,), F32),
            pltpu.SMEM((4,), F32),
            pltpu.SMEM((2, STEPS), F32),
            pltpu.VMEM((cells // TY, TY), jnp.int32),
            pltpu.VMEM((cells // TY, TY), jnp.int32),
            pltpu.VMEM((n_gx, TX * n_gy), jnp.int32),
            pltpu.VMEM((TX, TY), F32),
            pltpu.VMEM((HALF, TX, TY), BF16),
            pltpu.VMEM((2, 8, 8, TY), F32),
            pltpu.VMEM((2, HALF, 3, TX, TY), BF16),
            pltpu.VMEM((2, TX, TY), F32),
            pltpu.VMEM((4, 8, TY), F32),
            pltpu.VMEM((2, 8, 8, TY), F32),
            pltpu.VMEM((6, HALF, TX, TY), BF16),
            pltpu.VMEM((2, HALF, 3, TX, TY), BF16),
            pltpu.VMEM((HALF, 6, NZ, TX, TY), BF16),
            pltpu.VMEM((2, 3, TX, TY), BF16),
            pltpu.VMEM((2, 3, TX, TY), BF16),
            pltpu.VMEM((TX, TY), BF16),
            pltpu.VMEM((6, TX, TY), BF16),
            pltpu.VMEM((2, 3, TX, TY), BF16),
            pltpu.VMEM((TX, TY), BF16),
            pltpu.VMEM((STEPS, 6, NZ, TX, TY), BF16),
            pltpu.VMEM((6, NZ, TX, TY), F32),
            pltpu.VMEM((NZ * EX, EY), F32),
            pltpu.VMEM((4 * n_gy * SHARE, n_gx * TX), BF16),
            pltpu.VMEM((n_gx, TX, TY), F32),
            pltpu.VMEM((4 * n_gy, SHARE, TY), F32),
            dma((8,)),
            dma((HALF, 8)),
            dma((HALF,)),
            dma((8,)),
            dma((HALF, 8)),
            dma((HALF,)),
            dma((8,)),
            dma((8,)),
            dma((2,)),
            dma((2,)),
            pltpu.SemaphoreType.REGULAR,
            pltpu.SemaphoreType.REGULAR,
            pltpu.SemaphoreType.REGULAR,
            pltpu.SemaphoreType.REGULAR,
            dma((HALF,)),
            dma((HALF,)),
            dma((n_gx,)),
            dma((n_gx,)),
            dma((4 * n_gy,)),
            dma((4 * n_gy,)),
            dma((4,)),
            dma((10,)),
        ],
        compiler_params=pltpu.CompilerParams(
            collective_id=0, has_side_effects=True, vmem_limit_bytes=56 * 1024 * 1024
        ),
        name="interval",
    )(
        fields[0],
        stored[0],
        material,
        design,
        mat_eps,
        mat_chi,
        source_wave,
        source_cells.reshape(cells // TY, TY),
        monitor_cells.reshape(cells // TY, TY),
        owners.reshape(n_gx, TX * n_gy),
    )
    fields_next, stored_next, design_grad = pl.pallas_call(
        functools.partial(store, n_gy),
        out_shape=(
            jax.ShapeDtypeStruct(outs[0].shape, F32),
            jax.ShapeDtypeStruct(outs[1].shape, BF16),
            jax.ShapeDtypeStruct((SHARE, TY), F32),
        ),
        in_specs=[vmem] * 3,
        out_specs=(vmem,) * 3,
        compiler_params=pltpu.CompilerParams(vmem_limit_bytes=56 * 1024 * 1024),
        name="store",
    )(*outs)
    return fields_next[None], stored_next[None], design_grad


def solution(mesh):
    in_specs = (
        P("grp", None, None, "gx", "gy"),
        P("grp", None, None, None, "gx", "gy"),
        P(None, "gx", "gy"),
        P("gx", "gy"),
        P(),
        P(),
        P(),
        P(),
        P(),
        P(),
    )
    out_specs = (
        P("grp", None, None, "gx", "gy"),
        P("grp", None, None, None, "gx", "gy"),
        P(("grp", "gx", "gy"), None),
    )
    return jax.shard_map(local, mesh=mesh, in_specs=in_specs, out_specs=out_specs, check_vma=False)
```

```python
import functools
import math

import jax
import jax.numpy as jnp
from jax import lax
from jax.experimental import pallas as pl
from jax.experimental.pallas import tpu as pltpu
from jax.sharding import PartitionSpec as P

MESH = pl.DeviceIdType.MESH
F32 = jnp.float32
BF16 = jnp.bfloat16

NZ = 2
TX = 16
TY = 128
RIM = 4
EX = TX + 2 * RIM
EY = 2 * TY
STEPS = 4
HALF = 2
DT = 0.5
SHARE = 4

AROUND = ((-1, 0), (1, 0), (0, -1), (0, 1), (-1, -1), (-1, 1), (1, -1), (1, 1))


def far_first(length):
    return sorted(range(length), key=lambda j: -min(j, length - j))


def iota(shape, axis):
    return lax.broadcasted_iota(jnp.int32, shape, axis)


def pack_columns(planes, slot=8):
    column = iota((TX, TY), 1)
    window = ((column + slot // 2) // slot) % (TY // slot)
    packed = planes[0]
    for p in range(1, len(planes)):
        packed = jnp.where(window == p, pltpu.roll(planes[p], slot * p, 1), packed)
    return packed


def pack_rows(one, two):
    low = iota((8, TY), 0) < RIM
    first = jnp.where(low, one[:8], one[8:])
    second = pltpu.roll(jnp.where(low, two[:8], two[8:]), RIM, 0)
    return jnp.where(low, first, second), jnp.where(low, second, first)


def unpack_rows(after, before):
    low = iota((8, TY), 0) < RIM
    return jnp.where(low, after, before), pltpu.roll(jnp.where(low, before, after), RIM, 0)


def pack_thin_rows(planes):
    row = iota((8, TY), 0)
    both = [jnp.where(row < RIM, p[:8], p[8:]) for p in planes]
    before = after = both[0]
    for q in range(1, len(planes)):
        turned = pltpu.roll(both[q], 2 * q, 0)
        before = jnp.where(row // 2 == q, turned, before)
        after = jnp.where((row // 2 + 1) % 4 == q, turned, after)
    return before, after


def unpack_thin_rows(after, before, q):
    rows = jnp.where(iota((8, TY), 0) // 2 == q, after, before)
    return rows if q == 0 else pltpu.roll(rows, 8 - 2 * q, 0)


def merge_columns(right, left, corners, slot=8):
    side = iota((TX, TY), 1) % slot < slot // 2
    beside = jnp.where(side, right, left)
    side = side[:8]
    from_after_right, from_after_left, from_before_right, from_before_left = corners
    low = iota((8, TY), 0) < RIM
    after = jnp.where(side, from_after_right, from_after_left)
    before = jnp.where(side, from_before_right, from_before_left)
    return jnp.concatenate([beside, jnp.where(low, after, before)], axis=0)


def extended(tile, rows, columns, shift):
    body = jnp.concatenate([tile, rows], axis=0)
    beside = columns if shift == 0 else pltpu.roll(columns, TY - shift, 1)
    return jnp.concatenate([body, beside], axis=1)


def next_x(v):
    return pltpu.roll(v, EX - 1, 0) - v


def next_y(v):
    return pltpu.roll(v, EY - 1, 1) - v


def next_z(v):
    return [v[1] - v[0], -v[1]]


def last_x(v):
    return v - pltpu.roll(v, 1, 0)


def last_y(v):
    return v - pltpu.roll(v, 1, 1)


def last_z(v):
    return [v[0], v[1] - v[0]]


def curl(v, along_x, along_y, along_z):
    z_of_y, z_of_x = along_z(v[1]), along_z(v[0])
    return (
        [along_y(v[2][z]) - z_of_y[z] for z in range(NZ)],
        [z_of_x[z] - along_x(v[2][z]) for z in range(NZ)],
        [along_x(v[1][z]) - along_y(v[0][z]) for z in range(NZ)],
    )


def curl_up(v):
    return curl(v, next_x, next_y, next_z)


def curl_down(v):
    return curl(v, last_x, last_y, last_z)


def kernel(
    n_gx,
    n_gy,
    fields_in,
    stored_in,
    material_in,
    design_in,
    mat_eps_in,
    mat_chi_in,
    source_wave_in,
    source_cells_in,
    monitor_cells_in,
    owners_in,
    fields_next,
    stored_next,
    gathered,
    fields,
    stored,
    material,
    design,
    mat_eps,
    mat_chi,
    source_wave,
    source_cells,
    monitor_cells,
    owners,
    col_out,
    colh_out,
    row_out,
    rowh_out,
    col_in,
    corner_in,
    row_in,
    colh_in,
    rowh_in,
    half_in,
    rowc_out,
    rowc_in,
    colc_out,
    colc_in,
    rowc_here,
    colc_here,
    records,
    counts_ref,
    chosen,
    tiles,
    shares,
    own_sem,
    ownh_sem,
    half_send,
    in_sem,
    inh_sem,
    half_sem,
    thin_send,
    thin_sem,
    hand_send,
    hand_sem,
    second_round,
    third_round,
    fourth_round,
    go,
    record_send,
    record_sem,
    tile_send,
    tile_sem,
    share_send,
    share_sem,
    load_sem,
):
    grp, gx, gy = lax.axis_index("grp"), lax.axis_index("gx"), lax.axis_index("gy")
    forward = grp < 2
    twin = jnp.where(forward, grp + 2, grp - 2)

    def device(lane, dx, dy):
        return {
            "grp": lane,
            "gx": lax.rem(gx + dx + n_gx, n_gx),
            "gy": lax.rem(gy + dy + n_gy, n_gy),
        }

    barrier = pltpu.get_barrier_semaphore()
    adjoint = jnp.logical_not(forward)
    side = math.isqrt(n_gx)

    def on_grid(dx, dy):
        x, y = gx + dx, gy + dy
        return (x >= 0) & (x < n_gx) & (y >= 0) & (y < n_gy)

    def signal(semaphore, target):
        pl.semaphore_signal(semaphore, inc=1, device_id=target, device_id_type=MESH)

    def in_row(d):
        return {"grp": grp, "gx": gx - gx % side + (gx + d) % side, "gy": gy}

    def line_far_first():
        def across(place, c):
            return (place, place + 1 - 2 * (place % 2), (place + 2) % 4, 3 - place)[c]

        codes = [(a, b) for a in range(n_gx // side) for b in range(side)]
        for a, b in sorted(codes, key=lambda code: -sum(code))[:-1]:
            yield lax.rem(across(gx // side, a) * side + across(gx % side, b) - gx + n_gx, n_gx)

    def in_pair(d, other):
        return {"grp": grp, "gx": gx, "gy": lax.rem(gy - gy % 2 + (gy + other) % 2 + 2 * d + n_gy, n_gy)}

    beside = [(dx, dy) for dx, dy in AROUND[::-1] if dx]
    neighbours = sum(jnp.where(on_grid(dx, dy), 1, 0) for dx, dy in beside)
    pairs = [in_pair(d, other) for d in (-1, 1) for other in (0, 1)] + [in_pair(0, 1)]
    rows = [in_row(d) for d in range(1, side)]
    lines = [device(grp, side * d, 0) for d in range(1, n_gx // side)]
    other_lane = device(5 - grp, 0, 0)

    def signal_all(semaphore, targets):
        for dx, dy in beside:
            pl.when(on_grid(dx, dy))(functools.partial(signal, semaphore, device(grp, dx, dy)))
        for target in targets:
            signal(semaphore, target)

    signal(barrier, device(twin, 0, 0))

    @pl.when(adjoint)
    def _():
        signal_all(barrier, pairs + rows + lines + [other_lane])

    def all_in():
        first_round = neighbours + len(pairs) + len(rows) + len(lines) + 2
        pl.semaphore_wait(barrier, jnp.where(forward, 1, first_round))

    def begin_second():
        signal_all(second_round, pairs + rows)

    def end_second():
        pl.semaphore_wait(second_round, neighbours + len(pairs) + len(rows))
        signal(go, device(twin, 0, 0))
        for d in (-1, 1):
            signal(third_round, in_pair(d, 0))

    def end_third():
        pl.semaphore_wait(third_round, 2)
        signal(fourth_round, other_lane)

    held = (fields, stored, material, design, mat_eps, mat_chi, source_wave, source_cells, monitor_cells, owners)
    given = (
        fields_in,
        stored_in,
        material_in,
        design_in,
        mat_eps_in,
        mat_chi_in,
        source_wave_in,
        source_cells_in,
        monitor_cells_in,
        owners_in,
    )
    loads = [pltpu.make_async_copy(a, b, load_sem.at[i]) for i, (a, b) in enumerate(zip(given, held))]
    for load in loads:
        load.start()

    for i, (dx, dy) in enumerate(AROUND):
        x, y = gx - dx, gy - dy

        @pl.when((x < 0) | (x >= n_gx) | (y < 0) | (y >= n_gy))
        def _():
            if i < 2:
                row_in[i] = jnp.zeros(row_in.shape[1:], F32)
                rowh_in[i] = jnp.zeros(rowh_in.shape[1:], BF16)
                rowc_in[i] = jnp.zeros(rowc_in.shape[1:], BF16)
                return
            if i < 4:
                col_in[i - 2] = jnp.zeros(col_in.shape[1:], F32)
            else:
                corner_in[i - 4] = jnp.zeros(corner_in.shape[1:], F32)
            colh_in[i - 2] = jnp.zeros(colh_in.shape[1:], BF16)
            colc_in[i - 2] = jnp.zeros(colc_in.shape[1:], BF16)

    def lookup(index, entries):
        value = jnp.zeros(index.shape, F32)
        for k in range(4):
            value = jnp.where(index == k, entries[k], value)
        return value

    def own_planes():
        kinds = [material[z] for z in range(NZ)]
        eps = [lookup(kinds[z], mat_eps) + design[...] for z in range(NZ)]
        chi = [lookup(kinds[z], mat_chi) for z in range(NZ)]
        return [fields[c, z] for c in range(6) for z in range(NZ)] + eps + chi

    def half_planes(k, components):
        return [stored[k, c, z].astype(F32) for c in range(components) for z in range(NZ)]

    def row_copy(i):
        return pltpu.make_async_remote_copy(
            src_ref=row_out.at[i],
            dst_ref=row_in.at[i],
            send_sem=own_sem.at[i],
            recv_sem=in_sem.at[i],
            device_id=device(grp, *AROUND[i]),
            device_id_type=MESH,
        )

    def col_copy(i):
        return pltpu.make_async_remote_copy(
            src_ref=col_out,
            dst_ref=col_in.at[i - 2],
            send_sem=own_sem.at[i],
            recv_sem=in_sem.at[i],
            device_id=device(grp, *AROUND[i]),
            device_id_type=MESH,
        )

    def corner_copy(i):
        start = 0 if AROUND[i][0] < 0 else 8
        return pltpu.make_async_remote_copy(
            src_ref=col_out.at[pl.ds(start, 8)],
            dst_ref=corner_in.at[i - 4],
            send_sem=own_sem.at[i],
            recv_sem=in_sem.at[i],
            device_id=device(grp, *AROUND[i]),
            device_id_type=MESH,
        )

    def rim_copies():
        return [row_copy(0), row_copy(1), col_copy(2), col_copy(3)] + [corner_copy(i) for i in range(4, 8)]

    def half_copy(k, i):
        if i < 2:
            src, dst = rowh_out.at[i, k], rowh_in.at[i, k]
        else:
            src, dst = colh_out.at[k], colh_in.at[i - 2, k]
        return pltpu.make_async_remote_copy(
            src_ref=src,
            dst_ref=dst,
            send_sem=ownh_sem.at[k, i],
            recv_sem=inh_sem.at[k, i],
            device_id=device(grp, *AROUND[i]),
            device_id_type=MESH,
        )

    def thin_copies():
        pairs = ((rowc_out, rowc_here), (colc_out, colc_here))
        return [
            pltpu.make_async_remote_copy(
                src_ref=src,
                dst_ref=dst,
                send_sem=hand_send.at[i],
                recv_sem=hand_sem.at[i],
                device_id=device(twin, 0, 0),
                device_id_type=MESH,
            )
            for i, (src, dst) in enumerate(pairs)
        ]

    def thin_copy(i):
        if i < 2:
            src, dst = rowc_here.at[i], rowc_in.at[i]
        else:
            src, dst = colc_here, colc_in.at[i - 2]
        return pltpu.make_async_remote_copy(
            src_ref=src,
            dst_ref=dst,
            send_sem=thin_send.at[i],
            recv_sem=thin_sem.at[i],
            device_id=device(grp, *AROUND[i]),
            device_id_type=MESH,
        )

    def whole_half(k):
        return pltpu.make_async_remote_copy(
            src_ref=stored.at[k],
            dst_ref=half_in.at[k],
            send_sem=half_send.at[k],
            recv_sem=half_sem.at[k],
            device_id=device(twin, 0, 0),
            device_id_type=MESH,
        )

    def sent(i, act):
        pl.when(on_grid(*AROUND[i]))(act)

    def received(i, act):
        dx, dy = AROUND[i]
        pl.when(on_grid(-dx, -dy))(act)

    def send_rims():
        for i, copy in list(enumerate(rim_copies()))[::-1]:
            sent(i, copy.start)

    def pack_rims():
        planes = own_planes()
        col_out[...] = pack_columns(planes)
        for i in range(8):
            row_out[0, i], row_out[1, i] = pack_rows(planes[2 * i], planes[2 * i + 1])

    stored_load = loads.pop(1)

    @pl.when(forward)
    def _():
        stored_load.wait()
        planes = half_planes(1, 6) + half_planes(0, 3)
        colc_out[...] = pack_columns(planes, RIM).astype(BF16)
        parts = [pack_thin_rows(planes[i : i + 4]) for i in range(0, len(planes), 4)]
        parts.append(parts[-1])
        for i in range(3):
            for side in range(2):
                rowc_out[side, i] = jnp.concatenate(
                    [parts[2 * i][side], parts[2 * i + 1][side]], axis=0
                ).astype(BF16)
        all_in()
        for copy in thin_copies():
            copy.start()
        whole_half(1).start()
        for load in loads:
            load.wait()
        pack_rims()
        whole_half(1).wait_send()
        whole_half(0).start()

    @pl.when(adjoint)
    def _():
        for load in loads:
            load.wait()
        pack_rims()
        all_in()
        send_rims()
        begin_second()
        stored_load.wait()
        for k in range(HALF - 1, -1, -1):
            planes = half_planes(k, 6)
            colh_out[k] = pack_columns(planes).astype(BF16)
            for i in range(3):
                one = pack_rows(planes[4 * i], planes[4 * i + 1])
                two = pack_rows(planes[4 * i + 2], planes[4 * i + 3])
                for side in range(2):
                    rowh_out[side, k, i] = jnp.concatenate([one[side], two[side]], axis=0).astype(BF16)
            for i in range(7, -1, -1):
                sent(i, half_copy(k, i).start)

    row = iota((NZ * EX, TY), 0)
    depth = jnp.where(row >= EX, 1, 0)
    row = row - depth * EX
    x = gx * TX + jnp.where(row < TX + RIM, row, row - EX)
    sought_x = jnp.where((x >= 0) & (x < n_gx * TX), depth * (n_gx * TX) + x, -1)
    column = iota((TY, TY), 0)
    sought_y = gy * TY + column
    sought_high = sought_y[:8] + TY
    sought_low = sought_y[TY - 8 :] - TY
    listed = jnp.where(forward, source_cells[...], monitor_cells[...])
    listed_x = listed // (n_gy * TY)
    listed_y = listed % (n_gy * TY)

    def hits(found):
        return jnp.where(found, 1.0, 0.0)

    def wide(m, i, rows):
        return jnp.broadcast_to(m[i : i + 1], (rows, TY))

    entries = listed.shape[0]
    rows_hit = jnp.concatenate(
        [hits(wide(listed_x, i, NZ * EX) == sought_x) for i in range(entries)], axis=1
    ).astype(BF16)
    columns_hit = jnp.concatenate(
        [hits(wide(listed_y, i, TY) == sought_y) for i in range(entries)], axis=1
    ).astype(BF16)
    high_hit = jnp.concatenate([hits(wide(listed_y, i, 8) == sought_high) for i in range(entries)], axis=1)
    low_hit = jnp.concatenate([hits(wide(listed_y, i, 8) == sought_low) for i in range(entries)], axis=1)
    rim_hit = jnp.concatenate(
        [high_hit, jnp.zeros((TY - 16, entries * TY), F32), low_hit], axis=0
    ).astype(BF16)

    def tally(a, b):
        return lax.dot_general(a, b, (((1,), (1,)), ((), ())), preferred_element_type=F32)

    counts_ref[...] = jnp.concatenate([tally(rows_hit, columns_hit), tally(rows_hit, rim_hit)], axis=1)

    @pl.when(adjoint)
    def _():
        lanes = owners.shape[1]
        pick = iota((TX, lanes), 1) == iota((TX, lanes), 0) * n_gy + gy
        coarse, fine = [], []
        for j in range(n_gx):
            line = jnp.broadcast_to(owners[pl.ds(lax.rem(gx - j + n_gx, n_gx), 1)], (TX, lanes))
            line = jnp.where(pick, line, 0)
            part = line // 64 * 64
            coarse.append(part.astype(F32))
            fine.append((line - part).astype(F32))
        rows = 4 * n_gy * SHARE
        ones = jnp.ones((rows, lanes), BF16)
        owner = tally(ones, jnp.concatenate(coarse, axis=0).astype(BF16))
        owner = owner + tally(ones, jnp.concatenate(fine, axis=0).astype(BF16))
        place = iota((rows, n_gx * TX), 0)
        share = place // SHARE
        lane = (grp + share // n_gy) % 4
        spot = (gy + share % n_gy) % n_gy
        wanted = ((lane * n_gx + gx) * n_gy + spot) * SHARE + place % SHARE
        chosen[...] = jnp.where(owner == wanted.astype(F32), 1.0, 0.0).astype(BF16)

    row = iota((EX, EY), 0)
    column = iota((EX, EY), 1)
    x = gx * TX + jnp.where(row < TX + RIM, row, row - EX)
    y = gy * TY + jnp.where(column < TY + TY // 2, column, column - EY)
    inside = (x >= 0) & (x < n_gx * TX) & (y >= 0) & (y < n_gy * TY)
    unit = jnp.where(inside, 1.0, 0.0)
    step = jnp.where(inside, DT, 0.0)
    counts = [counts_ref[z * EX : (z + 1) * EX] for z in range(NZ)]

    @pl.when(adjoint)
    def _():
        for copy in thin_copies():
            copy.wait_recv()
        for i in range(7, -1, -1):
            sent(i, thin_copy(i).start)
        end_second()

    @pl.when(forward)
    def _():
        pl.semaphore_wait(go, 1)
        send_rims()

    for i, copy in enumerate(rim_copies()):
        received(i, copy.wait_recv)
    own = own_planes()
    columns = merge_columns(col_in[0], col_in[1], [corner_in[i] for i in range(4)])
    whole = []
    for i in range(8):
        for k, rows in enumerate(unpack_rows(row_in[0, i], row_in[1, i])):
            whole.append(extended(own[2 * i + k], rows, columns, 8 * (2 * i + k)))
    eps = [jnp.where(inside, v, 1.0) for v in whole[12:14]]
    chi = whole[14:16]
    whole = [jnp.where(inside, v, 0.0) for v in whole[:12]]
    first = [whole[2 * c : 2 * c + 2] for c in range(3)]
    second = [whole[2 * c : 2 * c + 2] for c in range(3, 6)]

    def finish(electric, magnetic):
        for c in range(3):
            for z in range(NZ):
                fields_next[c, z] = electric[c][z][:TX, :TY]
                fields_next[3 + c, z] = magnetic[c][z][:TX, :TY]

    def record_copy(n):
        return pltpu.make_async_remote_copy(
            src_ref=records.at[n - HALF],
            dst_ref=stored_next.at[n - HALF],
            send_sem=record_send.at[n - HALF],
            recv_sem=record_sem.at[n - HALF],
            device_id=device(twin, 0, 0),
            device_id_type=MESH,
        )

    def square(v, z):
        return v[0][z] * v[0][z] + v[1][z] * v[1][z] + v[2][z] * v[2][z]

    @pl.when(forward)
    def _():
        electric, magnetic = first, second
        for n in range(STEPS):
            factor = [step / (eps[z] + chi[z] * square(electric, z)) for z in range(NZ)]
            turn = curl_up(electric)
            magnetic = [[magnetic[c][z] - step * turn[c][z] for z in range(NZ)] for c in range(3)]
            turn = curl_down(magnetic)
            for c in range(3):
                for z in range(NZ):
                    record = stored_next if n < HALF else records
                    record[n % HALF, c, z] = electric[c][z][:TX, :TY].astype(BF16)
                    record[n % HALF, 3 + c, z] = turn[c][z][:TX, :TY].astype(BF16)
            if n >= HALF:
                record_copy(n).start()
            wave = source_wave[lax.rem(grp, 2), n]
            electric = [[electric[c][z] + factor[z] * turn[c][z] for z in range(NZ)] for c in range(3)]
            electric[0] = [electric[0][z] + wave * counts[z] for z in range(NZ)]
        finish(electric, magnetic)

    def corners_of(packed):
        return [packed[2][:8], packed[3][:8], packed[4][8:], packed[5][8:]]

    def vectors(planes):
        return [planes[2 * c : 2 * c + 2] for c in range(len(planes) // 2)]

    def late_snapshot(k):
        rows = []
        for i in range(3):
            after, before = rowh_in[0, k, i].astype(F32), rowh_in[1, k, i].astype(F32)
            rows.extend(unpack_rows(after[:8], before[:8]))
            rows.extend(unpack_rows(after[8:], before[8:]))
        packed = [colh_in[i, k].astype(F32) for i in range(6)]
        columns = merge_columns(packed[0], packed[1], corners_of(packed))
        return vectors([extended(v, rows[p], columns, 8 * p) for p, v in enumerate(half_planes(k, 6))])

    def early_snapshot(k, columns):
        planes = []
        for p in range(12):
            tile = half_in[k, p // NZ, p % NZ].astype(F32)
            place = p if k else 12 + p
            if place >= 18:
                planes.append(extended(tile, jnp.zeros((8, TY), F32), jnp.zeros((EX, TY), F32), 0))
                continue
            slot = slice(8 * (place // 4 % 2), 8 * (place // 4 % 2) + 8)
            after, before = [rowc_in[side, place // 8].astype(F32)[slot] for side in range(2)]
            planes.append(extended(tile, unpack_thin_rows(after, before, place % 4), columns, RIM * place))
        return vectors(planes)

    def tile_copy(j):
        return pltpu.make_async_remote_copy(
            src_ref=tiles.at[0],
            dst_ref=tiles.at[j],
            send_sem=tile_send.at[j],
            recv_sem=tile_sem.at[j],
            device_id=device(grp, j, 0),
            device_id_type=MESH,
        )

    def share_copy(i):
        return pltpu.make_async_remote_copy(
            src_ref=shares.at[i],
            dst_ref=gathered.at[i],
            send_sem=share_send.at[i],
            recv_sem=share_sem.at[i],
            device_id=device(lax.rem(grp + i // n_gy, 4), 0, lax.rem(i, n_gy)),
            device_id_type=MESH,
        )

    @pl.when(adjoint)
    def _():
        electric, magnetic = first, second
        gradient = jnp.zeros((TX, TY), F32)
        for n in range(STEPS - 1, -1, -1):
            if n >= HALF:
                for i in range(8):
                    received(i, half_copy(n - HALF, i).wait_recv)
                snapshot = late_snapshot(n - HALF)
            else:
                whole_half(n).wait_recv()
                if n == HALF - 1:
                    for i in range(8):
                        received(i, thin_copy(i).wait_recv)
                    packed = [colc_in[i].astype(F32) for i in range(6)]
                    columns = merge_columns(packed[0], packed[1], corners_of(packed), RIM)
                snapshot = early_snapshot(n, columns)
            past, curled = snapshot[:3], snapshot[3:]
            factor = [DT / (eps[z] + chi[z] * square(past, z)) for z in range(NZ)]
            inner = [
                curled[0][z] * electric[0][z] + curled[1][z] * electric[1][z] + curled[2][z] * electric[2][z]
                for z in range(NZ)
            ]
            slope = [factor[z] * factor[z] * inner[z] for z in range(NZ)]
            gradient = gradient - (1.0 / DT) * (slope[0] + slope[1])[:TX, :TY]
            if n == 0:
                tiles[0] = gradient
                for j in line_far_first():
                    tile_copy(j).start()
            turn = curl_up([[factor[z] * electric[c][z] for z in range(NZ)] for c in range(3)])
            magnetic = [[magnetic[c][z] + unit * turn[c][z] for z in range(NZ)] for c in range(3)]
            turn = curl_down(magnetic)
            weight = [counts[z] - (2.0 / DT) * chi[z] * slope[z] for z in range(NZ)]
            electric = [
                [electric[c][z] + weight[z] * past[c][z] - step * turn[c][z] for z in range(NZ)] for c in range(3)
            ]
        finish(electric, magnetic)

    def each(low, high, act):
        def body(i, carry):
            act(i)
            return carry

        lax.fori_loop(low, high, body, 0)

    @pl.when(adjoint)
    def _():
        end_third()
        for j in range(1, n_gx):
            tile_copy(j).wait_recv()
        rest = jnp.concatenate([tiles[j] for j in range(n_gx)], axis=0)
        total = jnp.zeros((4 * n_gy * SHARE, TY), F32)
        for _ in range(3):
            part = rest.astype(BF16)
            total = total + jnp.dot(chosen[...], part, preferred_element_type=F32)
            rest = rest - part.astype(F32)
        for i in range(4 * n_gy):
            shares[i] = total[SHARE * i : SHARE * (i + 1)]
        gathered[0] = total[:SHARE]
        pl.semaphore_wait(fourth_round, 1)
        for d in far_first(n_gy // 2):
            for lane in (0, 1, 3, 2):
                for other in (0, 1):
                    if d or lane or other:
                        place = lax.rem(gy - gy % 2 + (gy + other) % 2 + 2 * d, n_gy)
                        share_copy(lane * n_gy + lax.rem(place - gy + n_gy, n_gy)).start()

    for i, copy in enumerate(rim_copies()):
        sent(i, copy.wait_send)

    @pl.when(forward)
    def _():
        for copy in thin_copies():
            copy.wait_send()
        for k in range(HALF - 1):
            whole_half(k).wait_send()
        for n in range(HALF, STEPS):
            record_copy(n).wait_send()

    @pl.when(adjoint)
    def _():
        for k in range(HALF):
            for i in range(8):
                sent(i, half_copy(k, i).wait_send)
        for i in range(8):
            sent(i, thin_copy(i).wait_send)
        for n in range(HALF, STEPS):
            record_copy(n).wait_recv()
        for j in range(1, n_gx):
            tile_copy(j).wait_send()
        for i in range(1, 4 * n_gy):
            share_copy(i).wait_send()

    for lane in (2, 3):
        start = lax.rem(grp + 4 - lane, 4) * n_gy
        each(start + jnp.where(start == 0, 1, 0), start + n_gy, lambda i: share_copy(i).wait_recv())


def store(n_gy, fields, stored, gathered, fields_next, stored_next, design_grad, total, sem):
    copies = [
        pltpu.make_async_copy(fields, fields_next, sem.at[0]),
        pltpu.make_async_copy(stored, stored_next, sem.at[1]),
        pltpu.make_async_copy(total, design_grad, sem.at[2]),
    ]
    copies[0].start()
    copies[1].start()
    value = jnp.zeros((SHARE, TY), F32)
    for lane in (2, 3):
        start = lax.rem(lax.axis_index("grp") + 4 - lane, 4) * n_gy
        for j in range(n_gy):
            value = value + gathered[start + j]
    total[...] = value
    copies[2].start()
    for copy in copies:
        copy.wait()


def local(fields, stored, material, design, mat_eps, mat_chi, source_wave, source_cells, monitor_cells, owners):
    n_gx, n_gy = lax.axis_size("gx"), lax.axis_size("gy")
    vmem = pl.BlockSpec(memory_space=pltpu.VMEM)
    hbm = pl.BlockSpec(memory_space=pltpu.HBM)
    dma = pltpu.SemaphoreType.DMA
    cells = source_cells.shape[0]
    outs = pl.pallas_call(
        functools.partial(kernel, n_gx, n_gy),
        out_shape=(
            pltpu.VMEM((6, NZ, TX, TY), F32),
            pltpu.VMEM((HALF, 6, NZ, TX, TY), BF16),
            pltpu.VMEM((4 * n_gy, SHARE, TY), F32),
        ),
        in_specs=[hbm] * 10,
        out_specs=(vmem, vmem, vmem),
        scratch_shapes=[
            pltpu.VMEM((6, NZ, TX, TY), F32),
            pltpu.VMEM((HALF, 6, NZ, TX, TY), BF16),
            pltpu.VMEM((NZ, TX, TY), jnp.int32),
            pltpu.VMEM((TX, TY), F32),
            pltpu.SMEM((4,), F32),
            pltpu.SMEM((4,), F32),
            pltpu.SMEM((2, STEPS), F32),
            pltpu.VMEM((cells // TY, TY), jnp.int32),
            pltpu.VMEM((cells // TY, TY), jnp.int32),
            pltpu.VMEM((n_gx, TX * n_gy), jnp.int32),
            pltpu.VMEM((TX, TY), F32),
            pltpu.VMEM((HALF, TX, TY), BF16),
            pltpu.VMEM((2, 8, 8, TY), F32),
            pltpu.VMEM((2, HALF, 3, TX, TY), BF16),
            pltpu.VMEM((2, TX, TY), F32),
            pltpu.VMEM((4, 8, TY), F32),
            pltpu.VMEM((2, 8, 8, TY), F32),
            pltpu.VMEM((6, HALF, TX, TY), BF16),
            pltpu.VMEM((2, HALF, 3, TX, TY), BF16),
            pltpu.VMEM((HALF, 6, NZ, TX, TY), BF16),
            pltpu.VMEM((2, 3, TX, TY), BF16),
            pltpu.VMEM((2, 3, TX, TY), BF16),
            pltpu.VMEM((TX, TY), BF16),
            pltpu.VMEM((6, TX, TY), BF16),
            pltpu.VMEM((2, 3, TX, TY), BF16),
            pltpu.VMEM((TX, TY), BF16),
            pltpu.VMEM((HALF, 6, NZ, TX, TY), BF16),
            pltpu.VMEM((NZ * EX, EY), F32),
            pltpu.VMEM((4 * n_gy * SHARE, n_gx * TX), BF16),
            pltpu.VMEM((n_gx, TX, TY), F32),
            pltpu.VMEM((4 * n_gy, SHARE, TY), F32),
            dma((8,)),
            dma((HALF, 8)),
            dma((HALF,)),
            dma((8,)),
            dma((HALF, 8)),
            dma((HALF,)),
            dma((8,)),
            dma((8,)),
            dma((2,)),
            dma((2,)),
            pltpu.SemaphoreType.REGULAR,
            pltpu.SemaphoreType.REGULAR,
            pltpu.SemaphoreType.REGULAR,
            pltpu.SemaphoreType.REGULAR,
            dma((HALF,)),
            dma((HALF,)),
            dma((n_gx,)),
            dma((n_gx,)),
            dma((4 * n_gy,)),
            dma((4 * n_gy,)),
            dma((10,)),
        ],
        compiler_params=pltpu.CompilerParams(
            collective_id=0, has_side_effects=True, vmem_limit_bytes=56 * 1024 * 1024
        ),
        name="interval",
    )(
        fields[0],
        stored[0],
        material,
        design,
        mat_eps,
        mat_chi,
        source_wave,
        source_cells.reshape(cells // TY, TY),
        monitor_cells.reshape(cells // TY, TY),
        owners.reshape(n_gx, TX * n_gy),
    )
    fields_next, stored_next, design_grad = pl.pallas_call(
        functools.partial(store, n_gy),
        out_shape=(
            jax.ShapeDtypeStruct(outs[0].shape, F32),
            jax.ShapeDtypeStruct(outs[1].shape, BF16),
            jax.ShapeDtypeStruct((SHARE, TY), F32),
        ),
        in_specs=[vmem] * 3,
        out_specs=(hbm,) * 3,
        scratch_shapes=[pltpu.VMEM((SHARE, TY), F32), dma((3,))],
        compiler_params=pltpu.CompilerParams(vmem_limit_bytes=8 * 1024 * 1024),
        name="store",
    )(*outs)
    return fields_next[None], stored_next[None], design_grad


def solution(mesh):
    in_specs = (
        P("grp", None, None, "gx", "gy"),
        P("grp", None, None, None, "gx", "gy"),
        P(None, "gx", "gy"),
        P("gx", "gy"),
        P(),
        P(),
        P(),
        P(),
        P(),
        P(),
    )
    out_specs = (
        P("grp", None, None, "gx", "gy"),
        P("grp", None, None, None, "gx", "gy"),
        P(("grp", "gx", "gy"), None),
    )
    return jax.shard_map(local, mesh=mesh, in_specs=in_specs, out_specs=out_specs, check_vma=False)
```

```python
import functools
import math

import jax
import jax.numpy as jnp
from jax import lax
from jax.experimental import pallas as pl
from jax.experimental.pallas import tpu as pltpu
from jax.sharding import PartitionSpec as P

MESH = pl.DeviceIdType.MESH
F32 = jnp.float32
BF16 = jnp.bfloat16

NZ = 2
TX = 16
TY = 128
RIM = 4
EX = TX + 2 * RIM
EY = 2 * TY
STEPS = 4
HALF = 2
DT = 0.5
SHARE = 4

AROUND = ((-1, 0), (1, 0), (0, -1), (0, 1), (-1, -1), (-1, 1), (1, -1), (1, 1))


def iota(shape, axis):
    return lax.broadcasted_iota(jnp.int32, shape, axis)


def pack_columns(planes, slot=8):
    column = iota((TX, TY), 1)
    window = ((column + slot // 2) // slot) % (TY // slot)
    packed = planes[0]
    for p in range(1, len(planes)):
        packed = jnp.where(window == p, pltpu.roll(planes[p], slot * p, 1), packed)
    return packed


def pack_rows(one, two):
    low = iota((8, TY), 0) < RIM
    first = jnp.where(low, one[:8], one[8:])
    second = pltpu.roll(jnp.where(low, two[:8], two[8:]), RIM, 0)
    return jnp.where(low, first, second), jnp.where(low, second, first)


def unpack_rows(after, before):
    low = iota((8, TY), 0) < RIM
    return jnp.where(low, after, before), pltpu.roll(jnp.where(low, before, after), RIM, 0)


def pack_thin_rows(planes):
    row = iota((8, TY), 0)
    both = [jnp.where(row < RIM, p[:8], p[8:]) for p in planes]
    before = after = both[0]
    for q in range(1, len(planes)):
        turned = pltpu.roll(both[q], 2 * q, 0)
        before = jnp.where(row // 2 == q, turned, before)
        after = jnp.where((row // 2 + 1) % 4 == q, turned, after)
    return before, after


def unpack_thin_rows(after, before, q):
    rows = jnp.where(iota((8, TY), 0) // 2 == q, after, before)
    return rows if q == 0 else pltpu.roll(rows, 8 - 2 * q, 0)


def merge_columns(right, left, corners, slot=8):
    side = iota((TX, TY), 1) % slot < slot // 2
    beside = jnp.where(side, right, left)
    side = side[:8]
    from_after_right, from_after_left, from_before_right, from_before_left = corners
    low = iota((8, TY), 0) < RIM
    after = jnp.where(side, from_after_right, from_after_left)
    before = jnp.where(side, from_before_right, from_before_left)
    return jnp.concatenate([beside, jnp.where(low, after, before)], axis=0)


def extended(tile, rows, columns, shift):
    body = jnp.concatenate([tile, rows], axis=0)
    beside = columns if shift == 0 else pltpu.roll(columns, TY - shift, 1)
    return jnp.concatenate([body, beside], axis=1)


def next_x(v):
    return pltpu.roll(v, EX - 1, 0) - v


def next_y(v):
    return pltpu.roll(v, EY - 1, 1) - v


def next_z(v):
    return [v[1] - v[0], -v[1]]


def last_x(v):
    return v - pltpu.roll(v, 1, 0)


def last_y(v):
    return v - pltpu.roll(v, 1, 1)


def last_z(v):
    return [v[0], v[1] - v[0]]


def curl(v, along_x, along_y, along_z):
    z_of_y, z_of_x = along_z(v[1]), along_z(v[0])
    return (
        [along_y(v[2][z]) - z_of_y[z] for z in range(NZ)],
        [z_of_x[z] - along_x(v[2][z]) for z in range(NZ)],
        [along_x(v[1][z]) - along_y(v[0][z]) for z in range(NZ)],
    )


def curl_up(v):
    return curl(v, next_x, next_y, next_z)


def curl_down(v):
    return curl(v, last_x, last_y, last_z)


def kernel(
    n_gx,
    n_gy,
    fields_in,
    stored_in,
    material_in,
    design_in,
    mat_eps_in,
    mat_chi_in,
    source_wave_in,
    source_cells_in,
    monitor_cells_in,
    owners_in,
    fields_next,
    stored_next,
    gathered,
    fields,
    stored,
    material,
    design,
    mat_eps,
    mat_chi,
    source_wave,
    source_cells,
    monitor_cells,
    owners,
    col_out,
    colh_out,
    row_out,
    rowh_out,
    col_in,
    corner_in,
    row_in,
    colh_in,
    rowh_in,
    half_in,
    rowc_out,
    rowc_in,
    colc_out,
    colc_in,
    rowc_here,
    colc_here,
    records,
    counts_ref,
    chosen,
    tiles,
    shares,
    own_sem,
    ownh_sem,
    half_send,
    in_sem,
    inh_sem,
    half_sem,
    thin_send,
    thin_sem,
    hand_send,
    hand_sem,
    second_round,
    third_round,
    fourth_round,
    go,
    record_send,
    record_sem,
    tile_send,
    tile_sem,
    share_send,
    share_sem,
    load_sem,
):
    grp, gx, gy = lax.axis_index("grp"), lax.axis_index("gx"), lax.axis_index("gy")
    forward = grp < 2
    twin = jnp.where(forward, grp + 2, grp - 2)

    def device(lane, dx, dy):
        return {
            "grp": lane,
            "gx": lax.rem(gx + dx + n_gx, n_gx),
            "gy": lax.rem(gy + dy + n_gy, n_gy),
        }

    barrier = pltpu.get_barrier_semaphore()
    adjoint = jnp.logical_not(forward)
    side = math.isqrt(n_gx)

    def on_grid(dx, dy):
        x, y = gx + dx, gy + dy
        return (x >= 0) & (x < n_gx) & (y >= 0) & (y < n_gy)

    def signal(semaphore, target):
        pl.semaphore_signal(semaphore, inc=1, device_id=target, device_id_type=MESH)

    def in_row(d):
        return {"grp": grp, "gx": gx - gx % side + (gx + d) % side, "gy": gy}

    def in_pair(d, other):
        return {"grp": grp, "gx": gx, "gy": lax.rem(gy - gy % 2 + (gy + other) % 2 + 2 * d + n_gy, n_gy)}

    beside = [(dx, dy) for dx, dy in AROUND[::-1] if dx]
    neighbours = sum(jnp.where(on_grid(dx, dy), 1, 0) for dx, dy in beside)
    pairs = [in_pair(d, other) for d in (-1, 1) for other in (0, 1)] + [in_pair(0, 1)]
    rows = [in_row(d) for d in range(1, side)]
    lines = [device(grp, side * d, 0) for d in range(1, n_gx // side)]
    other_lane = device(5 - grp, 0, 0)

    def signal_all(semaphore, targets):
        for dx, dy in beside:
            pl.when(on_grid(dx, dy))(functools.partial(signal, semaphore, device(grp, dx, dy)))
        for target in targets:
            signal(semaphore, target)

    signal(barrier, device(twin, 0, 0))

    @pl.when(adjoint)
    def _():
        signal_all(barrier, pairs + rows + lines + [other_lane])

    def all_in():
        first_round = neighbours + len(pairs) + len(rows) + len(lines) + 2
        pl.semaphore_wait(barrier, jnp.where(forward, 1, first_round))

    def begin_second():
        signal_all(second_round, pairs + rows)

    def end_second():
        pl.semaphore_wait(second_round, neighbours + len(pairs) + len(rows))
        signal(go, device(twin, 0, 0))
        for d in (-1, 1):
            signal(third_round, in_pair(d, 0))

    def end_third():
        pl.semaphore_wait(third_round, 2)
        signal(fourth_round, other_lane)

    held = (fields, stored, material, design, mat_eps, mat_chi, source_wave, source_cells, monitor_cells, owners)
    given = (
        fields_in,
        stored_in,
        material_in,
        design_in,
        mat_eps_in,
        mat_chi_in,
        source_wave_in,
        source_cells_in,
        monitor_cells_in,
        owners_in,
    )
    loads = [pltpu.make_async_copy(a, b, load_sem.at[i]) for i, (a, b) in enumerate(zip(given, held))]
    for load in loads:
        load.start()

    for i, (dx, dy) in enumerate(AROUND):
        x, y = gx - dx, gy - dy

        @pl.when((x < 0) | (x >= n_gx) | (y < 0) | (y >= n_gy))
        def _():
            if i < 2:
                row_in[i] = jnp.zeros(row_in.shape[1:], F32)
                rowh_in[i] = jnp.zeros(rowh_in.shape[1:], BF16)
                rowc_in[i] = jnp.zeros(rowc_in.shape[1:], BF16)
                return
            if i < 4:
                col_in[i - 2] = jnp.zeros(col_in.shape[1:], F32)
            else:
                corner_in[i - 4] = jnp.zeros(corner_in.shape[1:], F32)
            colh_in[i - 2] = jnp.zeros(colh_in.shape[1:], BF16)
            colc_in[i - 2] = jnp.zeros(colc_in.shape[1:], BF16)

    def lookup(index, entries):
        value = jnp.zeros(index.shape, F32)
        for k in range(4):
            value = jnp.where(index == k, entries[k], value)
        return value

    def own_planes():
        kinds = [material[z] for z in range(NZ)]
        eps = [lookup(kinds[z], mat_eps) + design[...] for z in range(NZ)]
        chi = [lookup(kinds[z], mat_chi) for z in range(NZ)]
        return [fields[c, z] for c in range(6) for z in range(NZ)] + eps + chi

    def half_planes(k, components):
        return [stored[k, c, z].astype(F32) for c in range(components) for z in range(NZ)]

    def row_copy(i):
        return pltpu.make_async_remote_copy(
            src_ref=row_out.at[i],
            dst_ref=row_in.at[i],
            send_sem=own_sem.at[i],
            recv_sem=in_sem.at[i],
            device_id=device(grp, *AROUND[i]),
            device_id_type=MESH,
        )

    def col_copy(i):
        return pltpu.make_async_remote_copy(
            src_ref=col_out,
            dst_ref=col_in.at[i - 2],
            send_sem=own_sem.at[i],
            recv_sem=in_sem.at[i],
            device_id=device(grp, *AROUND[i]),
            device_id_type=MESH,
        )

    def corner_copy(i):
        start = 0 if AROUND[i][0] < 0 else 8
        return pltpu.make_async_remote_copy(
            src_ref=col_out.at[pl.ds(start, 8)],
            dst_ref=corner_in.at[i - 4],
            send_sem=own_sem.at[i],
            recv_sem=in_sem.at[i],
            device_id=device(grp, *AROUND[i]),
            device_id_type=MESH,
        )

    def rim_copies():
        return [row_copy(0), row_copy(1), col_copy(2), col_copy(3)] + [corner_copy(i) for i in range(4, 8)]

    def half_copy(k, i):
        if i < 2:
            src, dst = rowh_out.at[i, k], rowh_in.at[i, k]
        else:
            src, dst = colh_out.at[k], colh_in.at[i - 2, k]
        return pltpu.make_async_remote_copy(
            src_ref=src,
            dst_ref=dst,
            send_sem=ownh_sem.at[k, i],
            recv_sem=inh_sem.at[k, i],
            device_id=device(grp, *AROUND[i]),
            device_id_type=MESH,
        )

    def thin_copies():
        pairs = ((rowc_out, rowc_here), (colc_out, colc_here))
        return [
            pltpu.make_async_remote_copy(
                src_ref=src,
                dst_ref=dst,
                send_sem=hand_send.at[i],
                recv_sem=hand_sem.at[i],
                device_id=device(twin, 0, 0),
                device_id_type=MESH,
            )
            for i, (src, dst) in enumerate(pairs)
        ]

    def thin_copy(i):
        if i < 2:
            src, dst = rowc_here.at[i], rowc_in.at[i]
        else:
            src, dst = colc_here, colc_in.at[i - 2]
        return pltpu.make_async_remote_copy(
            src_ref=src,
            dst_ref=dst,
            send_sem=thin_send.at[i],
            recv_sem=thin_sem.at[i],
            device_id=device(grp, *AROUND[i]),
            device_id_type=MESH,
        )

    def whole_half(k):
        return pltpu.make_async_remote_copy(
            src_ref=stored.at[k],
            dst_ref=half_in.at[k],
            send_sem=half_send.at[k],
            recv_sem=half_sem.at[k],
            device_id=device(twin, 0, 0),
            device_id_type=MESH,
        )

    def sent(i, act):
        pl.when(on_grid(*AROUND[i]))(act)

    def received(i, act):
        dx, dy = AROUND[i]
        pl.when(on_grid(-dx, -dy))(act)

    def send_rims():
        for i, copy in list(enumerate(rim_copies()))[::-1]:
            sent(i, copy.start)

    def pack_rims():
        planes = own_planes()
        col_out[...] = pack_columns(planes)
        for i in range(8):
            row_out[0, i], row_out[1, i] = pack_rows(planes[2 * i], planes[2 * i + 1])

    def tally(a, b):
        return lax.dot_general(a, b, (((1,), (1,)), ((), ())), preferred_element_type=F32)

    def count_cells():
        row = iota((NZ * EX, TY), 0)
        depth = jnp.where(row >= EX, 1, 0)
        row = row - depth * EX
        x = gx * TX + jnp.where(row < TX + RIM, row, row - EX)
        sought_x = jnp.where((x >= 0) & (x < n_gx * TX), depth * (n_gx * TX) + x, -1)
        column = iota((TY, TY), 0)
        sought_y = gy * TY + column
        sought_high = sought_y[:8] + TY
        sought_low = sought_y[TY - 8 :] - TY
        listed = jnp.where(forward, source_cells[...], monitor_cells[...])
        listed_x = listed // (n_gy * TY)
        listed_y = listed % (n_gy * TY)

        def hits(found):
            return jnp.where(found, 1.0, 0.0)

        def wide(m, i, rows):
            return jnp.broadcast_to(m[i : i + 1], (rows, TY))

        entries = listed.shape[0]
        rows_hit = jnp.concatenate(
            [hits(wide(listed_x, i, NZ * EX) == sought_x) for i in range(entries)], axis=1
        ).astype(BF16)
        columns_hit = jnp.concatenate(
            [hits(wide(listed_y, i, TY) == sought_y) for i in range(entries)], axis=1
        ).astype(BF16)
        high_hit = jnp.concatenate([hits(wide(listed_y, i, 8) == sought_high) for i in range(entries)], axis=1)
        low_hit = jnp.concatenate([hits(wide(listed_y, i, 8) == sought_low) for i in range(entries)], axis=1)
        rim_hit = jnp.concatenate(
            [high_hit, jnp.zeros((TY - 16, entries * TY), F32), low_hit], axis=0
        ).astype(BF16)

        counts_ref[...] = jnp.concatenate([tally(rows_hit, columns_hit), tally(rows_hit, rim_hit)], axis=1)

    def choose_tiles():
        lanes = owners.shape[1]
        pick = iota((TX, lanes), 1) == iota((TX, lanes), 0) * n_gy + gy
        coarse, fine = [], []
        for j in range(n_gx):
            line = jnp.broadcast_to(owners[pl.ds(lax.rem(gx - j + n_gx, n_gx), 1)], (TX, lanes))
            line = jnp.where(pick, line, 0)
            part = line // 64 * 64
            coarse.append(part.astype(F32))
            fine.append((line - part).astype(F32))
        rows = 4 * n_gy * SHARE
        ones = jnp.ones((rows, lanes), BF16)
        owner = tally(ones, jnp.concatenate(coarse, axis=0).astype(BF16))
        owner = owner + tally(ones, jnp.concatenate(fine, axis=0).astype(BF16))
        place = iota((rows, n_gx * TX), 0)
        share = place // SHARE
        lane = (grp + share // n_gy) % 4
        spot = (gy + share % n_gy) % n_gy
        wanted = ((lane * n_gx + gx) * n_gy + spot) * SHARE + place % SHARE
        chosen[...] = jnp.where(owner == wanted.astype(F32), 1.0, 0.0).astype(BF16)

    stored_load = loads.pop(1)

    @pl.when(forward)
    def _():
        stored_load.wait()
        planes = half_planes(1, 6) + half_planes(0, 3)
        colc_out[...] = pack_columns(planes, RIM).astype(BF16)
        parts = [pack_thin_rows(planes[i : i + 4]) for i in range(0, len(planes), 4)]
        parts.append(parts[-1])
        for i in range(3):
            for side in range(2):
                rowc_out[side, i] = jnp.concatenate(
                    [parts[2 * i][side], parts[2 * i + 1][side]], axis=0
                ).astype(BF16)
        all_in()
        for copy in thin_copies():
            copy.start()
        whole_half(1).start()
        for load in loads:
            load.wait()
        pack_rims()
        whole_half(1).wait_send()
        whole_half(0).start()
        count_cells()

    @pl.when(adjoint)
    def _():
        for load in loads:
            load.wait()
        pack_rims()
        stored_load.wait()
        for k in range(HALF - 1, -1, -1):
            planes = half_planes(k, 6)
            colh_out[k] = pack_columns(planes).astype(BF16)
            for i in range(3):
                one = pack_rows(planes[4 * i], planes[4 * i + 1])
                two = pack_rows(planes[4 * i + 2], planes[4 * i + 3])
                for side in range(2):
                    rowh_out[side, k, i] = jnp.concatenate([one[side], two[side]], axis=0).astype(BF16)
        all_in()
        send_rims()
        begin_second()
        for k in range(HALF - 1, -1, -1):
            for i in range(7, -1, -1):
                sent(i, half_copy(k, i).start)
        for copy in thin_copies():
            copy.wait_recv()
        for i in range(7, -1, -1):
            sent(i, thin_copy(i).start)
        count_cells()
        choose_tiles()

    row = iota((EX, EY), 0)
    column = iota((EX, EY), 1)
    x = gx * TX + jnp.where(row < TX + RIM, row, row - EX)
    y = gy * TY + jnp.where(column < TY + TY // 2, column, column - EY)
    inside = (x >= 0) & (x < n_gx * TX) & (y >= 0) & (y < n_gy * TY)
    unit = jnp.where(inside, 1.0, 0.0)
    step = jnp.where(inside, DT, 0.0)
    counts = [counts_ref[z * EX : (z + 1) * EX] for z in range(NZ)]

    @pl.when(adjoint)
    def _():
        end_second()

    @pl.when(forward)
    def _():
        pl.semaphore_wait(go, 1)
        send_rims()

    for i, copy in enumerate(rim_copies()):
        received(i, copy.wait_recv)
    own = own_planes()
    columns = merge_columns(col_in[0], col_in[1], [corner_in[i] for i in range(4)])
    whole = []
    for i in range(8):
        for k, rows in enumerate(unpack_rows(row_in[0, i], row_in[1, i])):
            whole.append(extended(own[2 * i + k], rows, columns, 8 * (2 * i + k)))
    eps = [jnp.where(inside, v, 1.0) for v in whole[12:14]]
    chi = whole[14:16]
    whole = [jnp.where(inside, v, 0.0) for v in whole[:12]]
    first = [whole[2 * c : 2 * c + 2] for c in range(3)]
    second = [whole[2 * c : 2 * c + 2] for c in range(3, 6)]

    def finish(electric, magnetic):
        for c in range(3):
            for z in range(NZ):
                fields_next[c, z] = electric[c][z][:TX, :TY]
                fields_next[3 + c, z] = magnetic[c][z][:TX, :TY]

    def record_copy(n):
        return pltpu.make_async_remote_copy(
            src_ref=records.at[n - HALF],
            dst_ref=stored_next.at[n - HALF],
            send_sem=record_send.at[n - HALF],
            recv_sem=record_sem.at[n - HALF],
            device_id=device(twin, 0, 0),
            device_id_type=MESH,
        )

    def square(v, z):
        return v[0][z] * v[0][z] + v[1][z] * v[1][z] + v[2][z] * v[2][z]

    @pl.when(forward)
    def _():
        electric, magnetic = first, second
        for n in range(STEPS):
            factor = [step / (eps[z] + chi[z] * square(electric, z)) for z in range(NZ)]
            turn = curl_up(electric)
            magnetic = [[magnetic[c][z] - step * turn[c][z] for z in range(NZ)] for c in range(3)]
            turn = curl_down(magnetic)
            for c in range(3):
                for z in range(NZ):
                    record = stored_next if n < HALF else records
                    record[n % HALF, c, z] = electric[c][z][:TX, :TY].astype(BF16)
                    record[n % HALF, 3 + c, z] = turn[c][z][:TX, :TY].astype(BF16)
            if n >= HALF:
                record_copy(n).start()
            wave = source_wave[lax.rem(grp, 2), n]
            electric = [[electric[c][z] + factor[z] * turn[c][z] for z in range(NZ)] for c in range(3)]
            electric[0] = [electric[0][z] + wave * counts[z] for z in range(NZ)]
        finish(electric, magnetic)

    def corners_of(packed):
        return [packed[2][:8], packed[3][:8], packed[4][8:], packed[5][8:]]

    def vectors(planes):
        return [planes[2 * c : 2 * c + 2] for c in range(len(planes) // 2)]

    def late_snapshot(k):
        rows = []
        for i in range(3):
            after, before = rowh_in[0, k, i].astype(F32), rowh_in[1, k, i].astype(F32)
            rows.extend(unpack_rows(after[:8], before[:8]))
            rows.extend(unpack_rows(after[8:], before[8:]))
        packed = [colh_in[i, k].astype(F32) for i in range(6)]
        columns = merge_columns(packed[0], packed[1], corners_of(packed))
        return vectors([extended(v, rows[p], columns, 8 * p) for p, v in enumerate(half_planes(k, 6))])

    def early_snapshot(k, columns):
        planes = []
        for p in range(12):
            tile = half_in[k, p // NZ, p % NZ].astype(F32)
            place = p if k else 12 + p
            if place >= 18:
                planes.append(extended(tile, jnp.zeros((8, TY), F32), jnp.zeros((EX, TY), F32), 0))
                continue
            slot = slice(8 * (place // 4 % 2), 8 * (place // 4 % 2) + 8)
            after, before = [rowc_in[side, place // 8].astype(F32)[slot] for side in range(2)]
            planes.append(extended(tile, unpack_thin_rows(after, before, place % 4), columns, RIM * place))
        return vectors(planes)

    def tile_copy(j):
        return pltpu.make_async_remote_copy(
            src_ref=tiles.at[0],
            dst_ref=tiles.at[j],
            send_sem=tile_send.at[j],
            recv_sem=tile_sem.at[j],
            device_id=device(grp, j, 0),
            device_id_type=MESH,
        )

    def share_copy(i):
        return pltpu.make_async_remote_copy(
            src_ref=shares.at[i],
            dst_ref=gathered.at[i],
            send_sem=share_send.at[i],
            recv_sem=share_sem.at[i],
            device_id=device(lax.rem(grp + i // n_gy, 4), 0, lax.rem(i, n_gy)),
            device_id_type=MESH,
        )

    @pl.when(adjoint)
    def _():
        electric, magnetic = first, second
        gradient = jnp.zeros((TX, TY), F32)
        for n in range(STEPS - 1, -1, -1):
            if n >= HALF:
                for i in range(8):
                    received(i, half_copy(n - HALF, i).wait_recv)
                snapshot = late_snapshot(n - HALF)
            else:
                whole_half(n).wait_recv()
                if n == HALF - 1:
                    for i in range(8):
                        received(i, thin_copy(i).wait_recv)
                    packed = [colc_in[i].astype(F32) for i in range(6)]
                    columns = merge_columns(packed[0], packed[1], corners_of(packed), RIM)
                snapshot = early_snapshot(n, columns)
            past, curled = snapshot[:3], snapshot[3:]
            factor = [DT / (eps[z] + chi[z] * square(past, z)) for z in range(NZ)]
            inner = [
                curled[0][z] * electric[0][z] + curled[1][z] * electric[1][z] + curled[2][z] * electric[2][z]
                for z in range(NZ)
            ]
            slope = [factor[z] * factor[z] * inner[z] for z in range(NZ)]
            gradient = gradient - (1.0 / DT) * (slope[0] + slope[1])[:TX, :TY]
            if n == 0:
                tiles[0] = gradient
                for place in range(n_gx):

                    @pl.when(gx != place)
                    def _():
                        tile_copy(lax.rem(place - gx + n_gx, n_gx)).start()

            turn = curl_up([[factor[z] * electric[c][z] for z in range(NZ)] for c in range(3)])
            magnetic = [[magnetic[c][z] + unit * turn[c][z] for z in range(NZ)] for c in range(3)]
            turn = curl_down(magnetic)
            weight = [counts[z] - (2.0 / DT) * chi[z] * slope[z] for z in range(NZ)]
            electric = [
                [electric[c][z] + weight[z] * past[c][z] - step * turn[c][z] for z in range(NZ)] for c in range(3)
            ]
        finish(electric, magnetic)

    def each(low, high, act):
        def body(i, carry):
            act(i)
            return carry

        lax.fori_loop(low, high, body, 0)

    @pl.when(adjoint)
    def _():
        end_third()
        for j in range(1, n_gx):
            tile_copy(j).wait_recv()
        rest = jnp.concatenate([tiles[j] for j in range(n_gx)], axis=0)
        total = jnp.zeros((4 * n_gy * SHARE, TY), F32)
        for _ in range(3):
            part = rest.astype(BF16)
            total = total + jnp.dot(chosen[...], part, preferred_element_type=F32)
            rest = rest - part.astype(F32)
        for i in range(4 * n_gy):
            shares[i] = total[SHARE * i : SHARE * (i + 1)]
        gathered[0] = total[:SHARE]
        pl.semaphore_wait(fourth_round, 1)
        pair, count = gy // 2, n_gy // 2
        first = jnp.where(pair == 0, count // 2, count - pair)
        for step_on in range(count - 1):
            away = lax.rem(first - 1 + step_on, count - 1) + 1
            for lane in range(4):
                ahead = lax.rem(lane + 4 - grp, 4) * n_gy
                for core in (1, 0):
                    place = 2 * lax.rem(pair + away, count) + core
                    share_copy(ahead + lax.rem(place - gy + n_gy, n_gy)).start()
        for lane in range(4):
            for other in (0, 1):
                if lane or other:
                    place = gy - gy % 2 + (gy + other) % 2
                    share_copy(lane * n_gy + lax.rem(place - gy + n_gy, n_gy)).start()

    for i, copy in enumerate(rim_copies()):
        sent(i, copy.wait_send)

    @pl.when(forward)
    def _():
        for copy in thin_copies():
            copy.wait_send()
        for k in range(HALF - 1):
            whole_half(k).wait_send()
        for n in range(HALF, STEPS):
            record_copy(n).wait_send()

    @pl.when(adjoint)
    def _():
        for k in range(HALF):
            for i in range(8):
                sent(i, half_copy(k, i).wait_send)
        for i in range(8):
            sent(i, thin_copy(i).wait_send)
        for n in range(HALF, STEPS):
            record_copy(n).wait_recv()
        for j in range(1, n_gx):
            tile_copy(j).wait_send()
        for i in range(1, 4 * n_gy):
            share_copy(i).wait_send()

    for lane in (2, 3):
        start = lax.rem(grp + 4 - lane, 4) * n_gy
        each(start + jnp.where(start == 0, 1, 0), start + n_gy, lambda i: share_copy(i).wait_recv())


def store(n_gy, fields, stored, gathered, fields_next, stored_next, design_grad, total, sem):
    copies = [
        pltpu.make_async_copy(fields, fields_next, sem.at[0]),
        pltpu.make_async_copy(stored, stored_next, sem.at[1]),
        pltpu.make_async_copy(total, design_grad, sem.at[2]),
    ]
    copies[0].start()
    copies[1].start()
    value = jnp.zeros((SHARE, TY), F32)
    for lane in (2, 3):
        start = lax.rem(lax.axis_index("grp") + 4 - lane, 4) * n_gy
        for j in range(n_gy):
            value = value + gathered[start + j]
    total[...] = value
    copies[2].start()
    for copy in copies:
        copy.wait()


def local(fields, stored, material, design, mat_eps, mat_chi, source_wave, source_cells, monitor_cells, owners):
    n_gx, n_gy = lax.axis_size("gx"), lax.axis_size("gy")
    vmem = pl.BlockSpec(memory_space=pltpu.VMEM)
    hbm = pl.BlockSpec(memory_space=pltpu.HBM)
    dma = pltpu.SemaphoreType.DMA
    cells = source_cells.shape[0]
    outs = pl.pallas_call(
        functools.partial(kernel, n_gx, n_gy),
        out_shape=(
            pltpu.VMEM((6, NZ, TX, TY), F32),
            pltpu.VMEM((HALF, 6, NZ, TX, TY), BF16),
            pltpu.VMEM((4 * n_gy, SHARE, TY), F32),
        ),
        in_specs=[hbm] * 10,
        out_specs=(vmem, vmem, vmem),
        scratch_shapes=[
            pltpu.VMEM((6, NZ, TX, TY), F32),
            pltpu.VMEM((HALF, 6, NZ, TX, TY), BF16),
            pltpu.VMEM((NZ, TX, TY), jnp.int32),
            pltpu.VMEM((TX, TY), F32),
            pltpu.SMEM((4,), F32),
            pltpu.SMEM((4,), F32),
            pltpu.SMEM((2, STEPS), F32),
            pltpu.VMEM((cells // TY, TY), jnp.int32),
            pltpu.VMEM((cells // TY, TY), jnp.int32),
            pltpu.VMEM((n_gx, TX * n_gy), jnp.int32),
            pltpu.VMEM((TX, TY), F32),
            pltpu.VMEM((HALF, TX, TY), BF16),
            pltpu.VMEM((2, 8, 8, TY), F32),
            pltpu.VMEM((2, HALF, 3, TX, TY), BF16),
            pltpu.VMEM((2, TX, TY), F32),
            pltpu.VMEM((4, 8, TY), F32),
            pltpu.VMEM((2, 8, 8, TY), F32),
            pltpu.VMEM((6, HALF, TX, TY), BF16),
            pltpu.VMEM((2, HALF, 3, TX, TY), BF16),
            pltpu.VMEM((HALF, 6, NZ, TX, TY), BF16),
            pltpu.VMEM((2, 3, TX, TY), BF16),
            pltpu.VMEM((2, 3, TX, TY), BF16),
            pltpu.VMEM((TX, TY), BF16),
            pltpu.VMEM((6, TX, TY), BF16),
            pltpu.VMEM((2, 3, TX, TY), BF16),
            pltpu.VMEM((TX, TY), BF16),
            pltpu.VMEM((HALF, 6, NZ, TX, TY), BF16),
            pltpu.VMEM((NZ * EX, EY), F32),
            pltpu.VMEM((4 * n_gy * SHARE, n_gx * TX), BF16),
            pltpu.VMEM((n_gx, TX, TY), F32),
            pltpu.VMEM((4 * n_gy, SHARE, TY), F32),
            dma((8,)),
            dma((HALF, 8)),
            dma((HALF,)),
            dma((8,)),
            dma((HALF, 8)),
            dma((HALF,)),
            dma((8,)),
            dma((8,)),
            dma((2,)),
            dma((2,)),
            pltpu.SemaphoreType.REGULAR,
            pltpu.SemaphoreType.REGULAR,
            pltpu.SemaphoreType.REGULAR,
            pltpu.SemaphoreType.REGULAR,
            dma((HALF,)),
            dma((HALF,)),
            dma((n_gx,)),
            dma((n_gx,)),
            dma((4 * n_gy,)),
            dma((4 * n_gy,)),
            dma((10,)),
        ],
        compiler_params=pltpu.CompilerParams(
            collective_id=0, has_side_effects=True, vmem_limit_bytes=56 * 1024 * 1024
        ),
        name="interval",
    )(
        fields[0],
        stored[0],
        material,
        design,
        mat_eps,
        mat_chi,
        source_wave,
        source_cells.reshape(cells // TY, TY),
        monitor_cells.reshape(cells // TY, TY),
        owners.reshape(n_gx, TX * n_gy),
    )
    fields_next, stored_next, design_grad = pl.pallas_call(
        functools.partial(store, n_gy),
        out_shape=(
            jax.ShapeDtypeStruct(outs[0].shape, F32),
            jax.ShapeDtypeStruct(outs[1].shape, BF16),
            jax.ShapeDtypeStruct((SHARE, TY), F32),
        ),
        in_specs=[vmem] * 3,
        out_specs=(hbm,) * 3,
        scratch_shapes=[pltpu.VMEM((SHARE, TY), F32), dma((3,))],
        compiler_params=pltpu.CompilerParams(vmem_limit_bytes=8 * 1024 * 1024),
        name="store",
    )(*outs)
    return fields_next[None], stored_next[None], design_grad


def solution(mesh):
    in_specs = (
        P("grp", None, None, "gx", "gy"),
        P("grp", None, None, None, "gx", "gy"),
        P(None, "gx", "gy"),
        P("gx", "gy"),
        P(),
        P(),
        P(),
        P(),
        P(),
        P(),
    )
    out_specs = (
        P("grp", None, None, "gx", "gy"),
        P("grp", None, None, None, "gx", "gy"),
        P(("grp", "gx", "gy"), None),
    )
    return jax.shard_map(local, mesh=mesh, in_specs=in_specs, out_specs=out_specs, check_vma=False)
```

```python
import functools
import math

import jax
import jax.numpy as jnp
from jax import lax
from jax.experimental import pallas as pl
from jax.experimental.pallas import tpu as pltpu
from jax.sharding import PartitionSpec as P

MESH = pl.DeviceIdType.MESH
F32 = jnp.float32
BF16 = jnp.bfloat16

NZ = 2
TX = 16
TY = 128
RIM = 4
EX = TX + 2 * RIM
EY = 2 * TY
STEPS = 4
HALF = 2
DT = 0.5
SHARE = 4

AROUND = ((-1, 0), (1, 0), (0, -1), (0, 1), (-1, -1), (-1, 1), (1, -1), (1, 1))


def iota(shape, axis):
    return lax.broadcasted_iota(jnp.int32, shape, axis)


def pack_columns(planes, slot=8):
    column = iota((TX, TY), 1)
    window = ((column + slot // 2) // slot) % (TY // slot)
    packed = planes[0]
    for p in range(1, len(planes)):
        packed = jnp.where(window == p, pltpu.roll(planes[p], slot * p, 1), packed)
    return packed


def pack_rows(one, two):
    low = iota((8, TY), 0) < RIM
    first = jnp.where(low, one[:8], one[8:])
    second = pltpu.roll(jnp.where(low, two[:8], two[8:]), RIM, 0)
    return jnp.where(low, first, second), jnp.where(low, second, first)


def unpack_rows(after, before):
    low = iota((8, TY), 0) < RIM
    return jnp.where(low, after, before), pltpu.roll(jnp.where(low, before, after), RIM, 0)


def pack_thin_rows(planes):
    row = iota((8, TY), 0)
    both = [jnp.where(row < RIM, p[:8], p[8:]) for p in planes]
    before = after = both[0]
    for q in range(1, len(planes)):
        turned = pltpu.roll(both[q], 2 * q, 0)
        before = jnp.where(row // 2 == q, turned, before)
        after = jnp.where((row // 2 + 1) % 4 == q, turned, after)
    return before, after


def unpack_thin_rows(after, before, q):
    rows = jnp.where(iota((8, TY), 0) // 2 == q, after, before)
    return rows if q == 0 else pltpu.roll(rows, 8 - 2 * q, 0)


def merge_columns(right, left, corners, slot=8):
    side = iota((TX, TY), 1) % slot < slot // 2
    beside = jnp.where(side, right, left)
    side = side[:8]
    from_after_right, from_after_left, from_before_right, from_before_left = corners
    low = iota((8, TY), 0) < RIM
    after = jnp.where(side, from_after_right, from_after_left)
    before = jnp.where(side, from_before_right, from_before_left)
    return jnp.concatenate([beside, jnp.where(low, after, before)], axis=0)


def extended(tile, rows, columns, shift):
    body = jnp.concatenate([tile, rows], axis=0)
    beside = columns if shift == 0 else pltpu.roll(columns, TY - shift, 1)
    return jnp.concatenate([body, beside], axis=1)


def next_x(v):
    return pltpu.roll(v, EX - 1, 0) - v


def next_y(v):
    return pltpu.roll(v, EY - 1, 1) - v


def next_z(v):
    return [v[1] - v[0], -v[1]]


def last_x(v):
    return v - pltpu.roll(v, 1, 0)


def last_y(v):
    return v - pltpu.roll(v, 1, 1)


def last_z(v):
    return [v[0], v[1] - v[0]]


def curl(v, along_x, along_y, along_z):
    z_of_y, z_of_x = along_z(v[1]), along_z(v[0])
    return (
        [along_y(v[2][z]) - z_of_y[z] for z in range(NZ)],
        [z_of_x[z] - along_x(v[2][z]) for z in range(NZ)],
        [along_x(v[1][z]) - along_y(v[0][z]) for z in range(NZ)],
    )


def curl_up(v):
    return curl(v, next_x, next_y, next_z)


def curl_down(v):
    return curl(v, last_x, last_y, last_z)


def kernel(
    n_gx,
    n_gy,
    fields_in,
    stored_in,
    material_in,
    design_in,
    mat_eps_in,
    mat_chi_in,
    source_wave_in,
    source_cells_in,
    monitor_cells_in,
    owners_in,
    fields_next,
    stored_next,
    gathered,
    fields,
    stored,
    material,
    design,
    mat_eps,
    mat_chi,
    source_wave,
    source_cells,
    monitor_cells,
    owners,
    col_out,
    colh_out,
    row_out,
    rowh_out,
    col_in,
    corner_in,
    row_in,
    colh_in,
    rowh_in,
    half_in,
    rowc_out,
    rowc_in,
    colc_out,
    colc_in,
    rowc_here,
    colc_here,
    records,
    counts_ref,
    chosen,
    tiles,
    shares,
    own_sem,
    ownh_sem,
    half_send,
    in_sem,
    inh_sem,
    half_sem,
    thin_send,
    thin_sem,
    hand_send,
    hand_sem,
    second_round,
    third_round,
    fourth_round,
    go,
    record_send,
    record_sem,
    tile_send,
    tile_sem,
    share_send,
    share_sem,
    load_sem,
):
    grp, gx, gy = lax.axis_index("grp"), lax.axis_index("gx"), lax.axis_index("gy")
    forward = grp < 2
    twin = jnp.where(forward, grp + 2, grp - 2)

    def device(lane, dx, dy):
        return {
            "grp": lane,
            "gx": lax.rem(gx + dx + n_gx, n_gx),
            "gy": lax.rem(gy + dy + n_gy, n_gy),
        }

    barrier = pltpu.get_barrier_semaphore()
    adjoint = jnp.logical_not(forward)
    side = math.isqrt(n_gx)

    def on_grid(dx, dy):
        x, y = gx + dx, gy + dy
        return (x >= 0) & (x < n_gx) & (y >= 0) & (y < n_gy)

    def signal(semaphore, target):
        pl.semaphore_signal(semaphore, inc=1, device_id=target, device_id_type=MESH)

    def in_row(d):
        return {"grp": grp, "gx": gx - gx % side + (gx + d) % side, "gy": gy}

    def in_pair(d, other):
        return {"grp": grp, "gx": gx, "gy": lax.rem(gy - gy % 2 + (gy + other) % 2 + 2 * d + n_gy, n_gy)}

    beside = [(dx, dy) for dx, dy in AROUND[::-1] if dx]
    neighbours = sum(jnp.where(on_grid(dx, dy), 1, 0) for dx, dy in beside)
    pairs = [in_pair(d, other) for d in (-1, 1) for other in (0, 1)] + [in_pair(0, 1)]
    rows = [in_row(d) for d in range(1, side)]
    lines = [device(grp, side * d, 0) for d in range(1, n_gx // side)]
    other_lane = device(5 - grp, 0, 0)

    def signal_all(semaphore, targets):
        for dx, dy in beside:
            pl.when(on_grid(dx, dy))(functools.partial(signal, semaphore, device(grp, dx, dy)))
        for target in targets:
            signal(semaphore, target)

    signal(barrier, device(twin, 0, 0))

    @pl.when(adjoint)
    def _():
        signal_all(barrier, pairs + rows + lines + [other_lane])

    def all_in():
        first_round = neighbours + len(pairs) + len(rows) + len(lines) + 2
        pl.semaphore_wait(barrier, jnp.where(forward, 1, first_round))

    def begin_second():
        signal_all(second_round, pairs + rows)

    def end_second():
        pl.semaphore_wait(second_round, neighbours + len(pairs) + len(rows))
        signal(go, device(twin, 0, 0))
        for d in (-1, 1):
            signal(third_round, in_pair(d, 0))

    def end_third():
        pl.semaphore_wait(third_round, 2)
        signal(fourth_round, other_lane)

    held = (fields, stored, material, design, mat_eps, mat_chi, source_wave, source_cells, monitor_cells, owners)
    given = (
        fields_in,
        stored_in,
        material_in,
        design_in,
        mat_eps_in,
        mat_chi_in,
        source_wave_in,
        source_cells_in,
        monitor_cells_in,
        owners_in,
    )
    loads = [pltpu.make_async_copy(a, b, load_sem.at[i]) for i, (a, b) in enumerate(zip(given, held))]
    for load in loads:
        load.start()

    for i, (dx, dy) in enumerate(AROUND):
        x, y = gx - dx, gy - dy

        @pl.when((x < 0) | (x >= n_gx) | (y < 0) | (y >= n_gy))
        def _():
            if i < 2:
                row_in[i] = jnp.zeros(row_in.shape[1:], F32)
                rowh_in[i] = jnp.zeros(rowh_in.shape[1:], BF16)
                rowc_in[i] = jnp.zeros(rowc_in.shape[1:], BF16)
                return
            if i < 4:
                col_in[i - 2] = jnp.zeros(col_in.shape[1:], F32)
            else:
                corner_in[i - 4] = jnp.zeros(corner_in.shape[1:], F32)
            colh_in[i - 2] = jnp.zeros(colh_in.shape[1:], BF16)
            colc_in[i - 2] = jnp.zeros(colc_in.shape[1:], BF16)

    def lookup(index, entries):
        value = jnp.zeros(index.shape, F32)
        for k in range(4):
            value = jnp.where(index == k, entries[k], value)
        return value

    def own_planes():
        kinds = [material[z] for z in range(NZ)]
        eps = [lookup(kinds[z], mat_eps) + design[...] for z in range(NZ)]
        chi = [lookup(kinds[z], mat_chi) for z in range(NZ)]
        return [fields[c, z] for c in range(6) for z in range(NZ)] + eps + chi

    def half_planes_of(half, k, components):
        return [half[k, c, z].astype(F32) for c in range(components) for z in range(NZ)]

    def half_planes(k, components):
        return half_planes_of(stored, k, components)

    def row_copy(i):
        return pltpu.make_async_remote_copy(
            src_ref=row_out.at[i],
            dst_ref=row_in.at[i],
            send_sem=own_sem.at[i],
            recv_sem=in_sem.at[i],
            device_id=device(grp, *AROUND[i]),
            device_id_type=MESH,
        )

    def col_copy(i):
        return pltpu.make_async_remote_copy(
            src_ref=col_out,
            dst_ref=col_in.at[i - 2],
            send_sem=own_sem.at[i],
            recv_sem=in_sem.at[i],
            device_id=device(grp, *AROUND[i]),
            device_id_type=MESH,
        )

    def corner_copy(i):
        start = 0 if AROUND[i][0] < 0 else 8
        return pltpu.make_async_remote_copy(
            src_ref=col_out.at[pl.ds(start, 8)],
            dst_ref=corner_in.at[i - 4],
            send_sem=own_sem.at[i],
            recv_sem=in_sem.at[i],
            device_id=device(grp, *AROUND[i]),
            device_id_type=MESH,
        )

    def rim_copies():
        return [row_copy(0), row_copy(1), col_copy(2), col_copy(3)] + [corner_copy(i) for i in range(4, 8)]

    def half_copy(i):
        if i < 2:
            src, dst = rowh_out.at[i], rowh_in.at[i]
        else:
            src, dst = colh_out, colh_in.at[i - 2]
        return pltpu.make_async_remote_copy(
            src_ref=src,
            dst_ref=dst,
            send_sem=ownh_sem.at[i],
            recv_sem=inh_sem.at[i],
            device_id=device(grp, *AROUND[i]),
            device_id_type=MESH,
        )

    def thin_copies():
        pairs = ((rowc_out, rowc_here), (colc_out, colc_here))
        return [
            pltpu.make_async_remote_copy(
                src_ref=src,
                dst_ref=dst,
                send_sem=hand_send.at[i],
                recv_sem=hand_sem.at[i],
                device_id=device(twin, 0, 0),
                device_id_type=MESH,
            )
            for i, (src, dst) in enumerate(pairs)
        ]

    def thin_copy(i):
        if i < 2:
            src, dst = rowc_here.at[i], rowc_in.at[i]
        else:
            src, dst = colc_here, colc_in.at[i - 2]
        return pltpu.make_async_remote_copy(
            src_ref=src,
            dst_ref=dst,
            send_sem=thin_send.at[i],
            recv_sem=thin_sem.at[i],
            device_id=device(grp, *AROUND[i]),
            device_id_type=MESH,
        )

    def whole_half(k):
        return pltpu.make_async_remote_copy(
            src_ref=stored.at[k],
            dst_ref=half_in.at[k],
            send_sem=half_send.at[k],
            recv_sem=half_sem.at[k],
            device_id=device(twin, 0, 0),
            device_id_type=MESH,
        )

    def sent(i, act):
        pl.when(on_grid(*AROUND[i]))(act)

    def received(i, act):
        dx, dy = AROUND[i]
        pl.when(on_grid(-dx, -dy))(act)

    def send_rims():
        for i, copy in list(enumerate(rim_copies()))[::-1]:
            sent(i, copy.start)

    def pack_rims():
        planes = own_planes()
        col_out[...] = pack_columns(planes)
        for i in range(8):
            row_out[0, i], row_out[1, i] = pack_rows(planes[2 * i], planes[2 * i + 1])

    def tally(a, b):
        return lax.dot_general(a, b, (((1,), (1,)), ((), ())), preferred_element_type=F32)

    def count_cells():
        row = iota((NZ * EX, TY), 0)
        depth = jnp.where(row >= EX, 1, 0)
        row = row - depth * EX
        x = gx * TX + jnp.where(row < TX + RIM, row, row - EX)
        sought_x = jnp.where((x >= 0) & (x < n_gx * TX), depth * (n_gx * TX) + x, -1)
        column = iota((TY, TY), 0)
        sought_y = gy * TY + column
        sought_high = sought_y[:8] + TY
        sought_low = sought_y[TY - 8 :] - TY
        listed = jnp.where(forward, source_cells[...], monitor_cells[...])
        listed_x = listed // (n_gy * TY)
        listed_y = listed % (n_gy * TY)

        def hits(found):
            return jnp.where(found, 1.0, 0.0)

        def wide(m, i, rows):
            return jnp.broadcast_to(m[i : i + 1], (rows, TY))

        entries = listed.shape[0]
        rows_hit = jnp.concatenate(
            [hits(wide(listed_x, i, NZ * EX) == sought_x) for i in range(entries)], axis=1
        ).astype(BF16)
        columns_hit = jnp.concatenate(
            [hits(wide(listed_y, i, TY) == sought_y) for i in range(entries)], axis=1
        ).astype(BF16)
        high_hit = jnp.concatenate([hits(wide(listed_y, i, 8) == sought_high) for i in range(entries)], axis=1)
        low_hit = jnp.concatenate([hits(wide(listed_y, i, 8) == sought_low) for i in range(entries)], axis=1)
        rim_hit = jnp.concatenate(
            [high_hit, jnp.zeros((TY - 16, entries * TY), F32), low_hit], axis=0
        ).astype(BF16)

        counts_ref[...] = jnp.concatenate([tally(rows_hit, columns_hit), tally(rows_hit, rim_hit)], axis=1)

    def choose_tiles():
        lanes = owners.shape[1]
        pick = iota((TX, lanes), 1) == iota((TX, lanes), 0) * n_gy + gy
        coarse, fine = [], []
        for j in range(n_gx):
            line = jnp.broadcast_to(owners[pl.ds(lax.rem(gx - j + n_gx, n_gx), 1)], (TX, lanes))
            line = jnp.where(pick, line, 0)
            part = line // 64 * 64
            coarse.append(part.astype(F32))
            fine.append((line - part).astype(F32))
        rows = 4 * n_gy * SHARE
        ones = jnp.ones((rows, lanes), BF16)
        owner = tally(ones, jnp.concatenate(coarse, axis=0).astype(BF16))
        owner = owner + tally(ones, jnp.concatenate(fine, axis=0).astype(BF16))
        place = iota((rows, n_gx * TX), 0)
        share = place // SHARE
        lane = (grp + share // n_gy) % 4
        spot = (gy + share % n_gy) % n_gy
        wanted = ((lane * n_gx + gx) * n_gy + spot) * SHARE + place % SHARE
        chosen[...] = jnp.where(owner == wanted.astype(F32), 1.0, 0.0).astype(BF16)

    stored_load = loads.pop(1)

    @pl.when(forward)
    def _():
        stored_load.wait()
        planes = half_planes(1, 6) + half_planes(0, 3)
        colc_out[...] = pack_columns(planes, RIM).astype(BF16)
        parts = [pack_thin_rows(planes[i : i + 4]) for i in range(0, len(planes), 4)]
        parts.append(parts[-1])
        for i in range(3):
            for side in range(2):
                rowc_out[side, i] = jnp.concatenate(
                    [parts[2 * i][side], parts[2 * i + 1][side]], axis=0
                ).astype(BF16)
        all_in()
        for copy in thin_copies():
            copy.start()
        whole_half(1).start()
        for load in loads:
            load.wait()
        pack_rims()
        whole_half(1).wait_send()
        whole_half(0).start()
        count_cells()

    @pl.when(adjoint)
    def _():
        for load in loads:
            load.wait()
        pack_rims()
        stored_load.wait()
        for k in range(HALF - 1, -1, -1):
            planes = half_planes(k, 6)
            colh_out[k] = pack_columns(planes).astype(BF16)
            for i in range(3):
                one = pack_rows(planes[4 * i], planes[4 * i + 1])
                two = pack_rows(planes[4 * i + 2], planes[4 * i + 3])
                for side in range(2):
                    rowh_out[side, k, i] = jnp.concatenate([one[side], two[side]], axis=0).astype(BF16)
        all_in()
        send_rims()
        for i in range(7, -1, -1):
            sent(i, half_copy(i).start)
        begin_second()
        for copy in thin_copies():
            copy.wait_recv()
        for i in range(7, -1, -1):
            sent(i, thin_copy(i).start)
        count_cells()
        choose_tiles()

    row = iota((EX, EY), 0)
    column = iota((EX, EY), 1)
    x = gx * TX + jnp.where(row < TX + RIM, row, row - EX)
    y = gy * TY + jnp.where(column < TY + TY // 2, column, column - EY)
    inside = (x >= 0) & (x < n_gx * TX) & (y >= 0) & (y < n_gy * TY)
    unit = jnp.where(inside, 1.0, 0.0)
    step = jnp.where(inside, DT, 0.0)
    counts = [counts_ref[z * EX : (z + 1) * EX] for z in range(NZ)]

    @pl.when(adjoint)
    def _():
        end_second()

    @pl.when(forward)
    def _():
        pl.semaphore_wait(go, 1)
        send_rims()

    for i, copy in enumerate(rim_copies()):
        received(i, copy.wait_recv)
    own = own_planes()
    columns = merge_columns(col_in[0], col_in[1], [corner_in[i] for i in range(4)])
    whole = []
    for i in range(8):
        for k, rows in enumerate(unpack_rows(row_in[0, i], row_in[1, i])):
            whole.append(extended(own[2 * i + k], rows, columns, 8 * (2 * i + k)))
    eps = [jnp.where(inside, v, 1.0) for v in whole[12:14]]
    chi = whole[14:16]
    whole = [jnp.where(inside, v, 0.0) for v in whole[:12]]
    first = [whole[2 * c : 2 * c + 2] for c in range(3)]
    second = [whole[2 * c : 2 * c + 2] for c in range(3, 6)]

    def finish(electric, magnetic):
        for c in range(3):
            for z in range(NZ):
                fields_next[c, z] = electric[c][z][:TX, :TY]
                fields_next[3 + c, z] = magnetic[c][z][:TX, :TY]

    def record_copy(n):
        return pltpu.make_async_remote_copy(
            src_ref=records.at[n - HALF],
            dst_ref=stored_next.at[n - HALF],
            send_sem=record_send.at[n - HALF],
            recv_sem=record_sem.at[n - HALF],
            device_id=device(twin, 0, 0),
            device_id_type=MESH,
        )

    def square(v, z):
        return v[0][z] * v[0][z] + v[1][z] * v[1][z] + v[2][z] * v[2][z]

    @pl.when(forward)
    def _():
        electric, magnetic = first, second
        for n in range(STEPS):
            factor = [step / (eps[z] + chi[z] * square(electric, z)) for z in range(NZ)]
            turn = curl_up(electric)
            magnetic = [[magnetic[c][z] - step * turn[c][z] for z in range(NZ)] for c in range(3)]
            turn = curl_down(magnetic)
            for c in range(3):
                for z in range(NZ):
                    record = stored_next if n < HALF else records
                    record[n % HALF, c, z] = electric[c][z][:TX, :TY].astype(BF16)
                    record[n % HALF, 3 + c, z] = turn[c][z][:TX, :TY].astype(BF16)
            if n >= HALF:
                record_copy(n).start()
            wave = source_wave[lax.rem(grp, 2), n]
            electric = [[electric[c][z] + factor[z] * turn[c][z] for z in range(NZ)] for c in range(3)]
            electric[0] = [electric[0][z] + wave * counts[z] for z in range(NZ)]
        finish(electric, magnetic)

    def corners_of(packed):
        return [packed[2][:8], packed[3][:8], packed[4][8:], packed[5][8:]]

    def vectors(planes):
        return [planes[2 * c : 2 * c + 2] for c in range(len(planes) // 2)]

    def late_snapshot(k):
        rows = []
        for i in range(3):
            after, before = rowh_in[0, k, i].astype(F32), rowh_in[1, k, i].astype(F32)
            rows.extend(unpack_rows(after[:8], before[:8]))
            rows.extend(unpack_rows(after[8:], before[8:]))
        packed = [colh_in[i, k].astype(F32) for i in range(6)]
        columns = merge_columns(packed[0], packed[1], corners_of(packed))
        return vectors([extended(v, rows[p], columns, 8 * p) for p, v in enumerate(half_planes(k, 6))])

    def early_snapshot(k, columns):
        planes = []
        for p in range(12):
            tile = half_in[k, p // NZ, p % NZ].astype(F32)
            place = p if k else 12 + p
            if place >= 18:
                planes.append(extended(tile, jnp.zeros((8, TY), F32), jnp.zeros((EX, TY), F32), 0))
                continue
            slot = slice(8 * (place // 4 % 2), 8 * (place // 4 % 2) + 8)
            after, before = [rowc_in[side, place // 8].astype(F32)[slot] for side in range(2)]
            planes.append(extended(tile, unpack_thin_rows(after, before, place % 4), columns, RIM * place))
        return vectors(planes)

    def tile_copy(j):
        return pltpu.make_async_remote_copy(
            src_ref=tiles.at[0],
            dst_ref=tiles.at[j],
            send_sem=tile_send.at[j],
            recv_sem=tile_sem.at[j],
            device_id=device(grp, j, 0),
            device_id_type=MESH,
        )

    def share_copy(i):
        return pltpu.make_async_remote_copy(
            src_ref=shares.at[i],
            dst_ref=gathered.at[i],
            send_sem=share_send.at[i],
            recv_sem=share_sem.at[i],
            device_id=device(lax.rem(grp + i // n_gy, 4), 0, lax.rem(i, n_gy)),
            device_id_type=MESH,
        )

    @pl.when(adjoint)
    def _():
        electric, magnetic = first, second
        gradient = jnp.zeros((TX, TY), F32)
        for n in range(STEPS - 1, -1, -1):
            if n == 0:
                whole_half(0).wait_recv()
                tile = vectors(half_planes_of(half_in, 0, 6))
                field = [[electric[c][z][:TX, :TY] for z in range(NZ)] for c in range(3)]
                for z in range(NZ):
                    divisor = eps[z][:TX, :TY] + chi[z][:TX, :TY] * square(tile[:3], z)
                    product = sum(tile[3 + c][z] * field[c][z] for c in range(3))
                    part = DT / divisor
                    gradient = gradient - (1.0 / DT) * part * part * product
                tiles[0] = gradient
                for place in range(n_gx):

                    @pl.when(gx != place)
                    def _():
                        tile_copy(lax.rem(place - gx + n_gx, n_gx)).start()

            if n >= HALF:
                if n == STEPS - 1:
                    for i in range(8):
                        received(i, half_copy(i).wait_recv)
                snapshot = late_snapshot(n - HALF)
            else:
                if n == HALF - 1:
                    whole_half(n).wait_recv()
                    for i in range(8):
                        received(i, thin_copy(i).wait_recv)
                    packed = [colc_in[i].astype(F32) for i in range(6)]
                    columns = merge_columns(packed[0], packed[1], corners_of(packed), RIM)
                snapshot = early_snapshot(n, columns)
            past, curled = snapshot[:3], snapshot[3:]
            factor = [DT / (eps[z] + chi[z] * square(past, z)) for z in range(NZ)]
            inner = [
                curled[0][z] * electric[0][z] + curled[1][z] * electric[1][z] + curled[2][z] * electric[2][z]
                for z in range(NZ)
            ]
            slope = [factor[z] * factor[z] * inner[z] for z in range(NZ)]
            if n:
                gradient = gradient - (1.0 / DT) * (slope[0] + slope[1])[:TX, :TY]
            turn = curl_up([[factor[z] * electric[c][z] for z in range(NZ)] for c in range(3)])
            magnetic = [[magnetic[c][z] + unit * turn[c][z] for z in range(NZ)] for c in range(3)]
            turn = curl_down(magnetic)
            weight = [counts[z] - (2.0 / DT) * chi[z] * slope[z] for z in range(NZ)]
            electric = [
                [electric[c][z] + weight[z] * past[c][z] - step * turn[c][z] for z in range(NZ)] for c in range(3)
            ]
        finish(electric, magnetic)

    @pl.when(adjoint)
    def _():
        end_third()
        for j in range(1, n_gx):
            tile_copy(j).wait_recv()
        rest = jnp.concatenate([tiles[j] for j in range(n_gx)], axis=0)
        total = jnp.zeros((4 * n_gy * SHARE, TY), F32)
        for _ in range(3):
            part = rest.astype(BF16)
            total = total + jnp.dot(chosen[...], part, preferred_element_type=F32)
            rest = rest - part.astype(F32)
        for i in range(4 * n_gy):
            shares[i] = total[SHARE * i : SHARE * (i + 1)]
        gathered[0] = total[:SHARE]
        pl.semaphore_wait(fourth_round, 1)
        pair, count = gy // 2, n_gy // 2
        first = jnp.where(pair == 0, count // 2, count - pair)
        for step_on in range(count - 1):
            away = lax.rem(first - 1 + step_on, count - 1) + 1
            for lane in range(4):
                ahead = lax.rem(lane + 4 - grp, 4) * n_gy
                for core in (1, 0):
                    place = 2 * lax.rem(pair + away, count) + core
                    share_copy(ahead + lax.rem(place - gy + n_gy, n_gy)).start()
        for lane in range(4):
            for other in (0, 1):
                if lane or other:
                    place = gy - gy % 2 + (gy + other) % 2
                    share_copy(lane * n_gy + lax.rem(place - gy + n_gy, n_gy)).start()

    for i, copy in enumerate(rim_copies()):
        sent(i, copy.wait_send)

    @pl.when(forward)
    def _():
        for copy in thin_copies():
            copy.wait_send()
        for k in range(HALF - 1):
            whole_half(k).wait_send()
        for n in range(HALF, STEPS):
            record_copy(n).wait_send()

    @pl.when(adjoint)
    def _():
        for i in range(8):
            sent(i, half_copy(i).wait_send)
        for i in range(8):
            sent(i, thin_copy(i).wait_send)
        for n in range(HALF, STEPS):
            record_copy(n).wait_recv()
        for j in range(1, n_gx):
            tile_copy(j).wait_send()
        for i in range(1, 4 * n_gy):
            share_copy(i).wait_send()

    for lane in (2, 3):
        start = lax.rem(grp + 4 - lane, 4) * n_gy
        pl.when(start > 0)(share_copy(start).wait_recv)
        for j in range(1, n_gy):
            share_copy(start + j).wait_recv()


def store(n_gy, fields, stored, gathered, fields_next, stored_next, design_grad, total, sem):
    copies = [
        pltpu.make_async_copy(fields, fields_next, sem.at[0]),
        pltpu.make_async_copy(stored, stored_next, sem.at[1]),
        pltpu.make_async_copy(total, design_grad, sem.at[2]),
    ]
    copies[0].start()
    copies[1].start()
    value = jnp.zeros((SHARE, TY), F32)
    for lane in (2, 3):
        start = lax.rem(lax.axis_index("grp") + 4 - lane, 4) * n_gy
        for j in range(n_gy):
            value = value + gathered[start + j]
    total[...] = value
    copies[2].start()
    for copy in copies:
        copy.wait()


def local(fields, stored, material, design, mat_eps, mat_chi, source_wave, source_cells, monitor_cells, owners):
    n_gx, n_gy = lax.axis_size("gx"), lax.axis_size("gy")
    vmem = pl.BlockSpec(memory_space=pltpu.VMEM)
    hbm = pl.BlockSpec(memory_space=pltpu.HBM)
    dma = pltpu.SemaphoreType.DMA
    cells = source_cells.shape[0]
    outs = pl.pallas_call(
        functools.partial(kernel, n_gx, n_gy),
        out_shape=(
            pltpu.VMEM((6, NZ, TX, TY), F32),
            pltpu.VMEM((HALF, 6, NZ, TX, TY), BF16),
            pltpu.VMEM((4 * n_gy, SHARE, TY), F32),
        ),
        in_specs=[hbm] * 10,
        out_specs=(vmem, vmem, vmem),
        scratch_shapes=[
            pltpu.VMEM((6, NZ, TX, TY), F32),
            pltpu.VMEM((HALF, 6, NZ, TX, TY), BF16),
            pltpu.VMEM((NZ, TX, TY), jnp.int32),
            pltpu.VMEM((TX, TY), F32),
            pltpu.SMEM((4,), F32),
            pltpu.SMEM((4,), F32),
            pltpu.SMEM((2, STEPS), F32),
            pltpu.VMEM((cells // TY, TY), jnp.int32),
            pltpu.VMEM((cells // TY, TY), jnp.int32),
            pltpu.VMEM((n_gx, TX * n_gy), jnp.int32),
            pltpu.VMEM((TX, TY), F32),
            pltpu.VMEM((HALF, TX, TY), BF16),
            pltpu.VMEM((2, 8, 8, TY), F32),
            pltpu.VMEM((2, HALF, 3, TX, TY), BF16),
            pltpu.VMEM((2, TX, TY), F32),
            pltpu.VMEM((4, 8, TY), F32),
            pltpu.VMEM((2, 8, 8, TY), F32),
            pltpu.VMEM((6, HALF, TX, TY), BF16),
            pltpu.VMEM((2, HALF, 3, TX, TY), BF16),
            pltpu.VMEM((HALF, 6, NZ, TX, TY), BF16),
            pltpu.VMEM((2, 3, TX, TY), BF16),
            pltpu.VMEM((2, 3, TX, TY), BF16),
            pltpu.VMEM((TX, TY), BF16),
            pltpu.VMEM((6, TX, TY), BF16),
            pltpu.VMEM((2, 3, TX, TY), BF16),
            pltpu.VMEM((TX, TY), BF16),
            pltpu.VMEM((HALF, 6, NZ, TX, TY), BF16),
            pltpu.VMEM((NZ * EX, EY), F32),
            pltpu.VMEM((4 * n_gy * SHARE, n_gx * TX), BF16),
            pltpu.VMEM((n_gx, TX, TY), F32),
            pltpu.VMEM((4 * n_gy, SHARE, TY), F32),
            dma((8,)),
            dma((8,)),
            dma((HALF,)),
            dma((8,)),
            dma((8,)),
            dma((HALF,)),
            dma((8,)),
            dma((8,)),
            dma((2,)),
            dma((2,)),
            pltpu.SemaphoreType.REGULAR,
            pltpu.SemaphoreType.REGULAR,
            pltpu.SemaphoreType.REGULAR,
            pltpu.SemaphoreType.REGULAR,
            dma((HALF,)),
            dma((HALF,)),
            dma((n_gx,)),
            dma((n_gx,)),
            dma((4 * n_gy,)),
            dma((4 * n_gy,)),
            dma((10,)),
        ],
        compiler_params=pltpu.CompilerParams(
            collective_id=0, has_side_effects=True, vmem_limit_bytes=56 * 1024 * 1024
        ),
        name="interval",
    )(
        fields[0],
        stored[0],
        material,
        design,
        mat_eps,
        mat_chi,
        source_wave,
        source_cells.reshape(cells // TY, TY),
        monitor_cells.reshape(cells // TY, TY),
        owners.reshape(n_gx, TX * n_gy),
    )
    fields_next, stored_next, design_grad = pl.pallas_call(
        functools.partial(store, n_gy),
        out_shape=(
            jax.ShapeDtypeStruct(outs[0].shape, F32),
            jax.ShapeDtypeStruct(outs[1].shape, BF16),
            jax.ShapeDtypeStruct((SHARE, TY), F32),
        ),
        in_specs=[vmem] * 3,
        out_specs=(hbm,) * 3,
        scratch_shapes=[pltpu.VMEM((SHARE, TY), F32), dma((3,))],
        compiler_params=pltpu.CompilerParams(vmem_limit_bytes=8 * 1024 * 1024),
        name="store",
    )(*outs)
    return fields_next[None], stored_next[None], design_grad


def solution(mesh):
    in_specs = (
        P("grp", None, None, "gx", "gy"),
        P("grp", None, None, None, "gx", "gy"),
        P(None, "gx", "gy"),
        P("gx", "gy"),
        P(),
        P(),
        P(),
        P(),
        P(),
        P(),
    )
    out_specs = (
        P("grp", None, None, "gx", "gy"),
        P("grp", None, None, None, "gx", "gy"),
        P(("grp", "gx", "gy"), None),
    )
    return jax.shard_map(local, mesh=mesh, in_specs=in_specs, out_specs=out_specs, check_vma=False)
```
